256 devices in a mesh: dp: 16 (over y_hi, z), mp: 16 (over x, y_lo, core).
Axes of the slice: x: 4, y: 4 (y_hi: 2, y_lo: 2; y = y_hi * 2 + y_lo), z: 8, core: 2. Of those that a mesh axis runs over, the one named last changes fastest.
Arguments:
- normed: bfloat16 [6144, 9216], P(('dp', 'mp')), may hold values from -6 to 6
- w_query: bfloat16 [9216, 8192], P(None, 'mp'), may hold values from -0.0625 to 0.0625
- w_key: bfloat16 [9216, 256], P(None, 'mp'), may hold values from -0.0625 to 0.0625
- w_value: bfloat16 [9216, 256], P(None, 'mp'), may hold values from -0.0625 to 0.0625
- query: bfloat16 [6144, 8192], P('dp', 'mp'), may hold values from -42 to 42
- key: bfloat16 [6144, 256], P('dp'), may hold values from -6 to 6
- value: bfloat16 [6144, 256], P('dp'), may hold values from -6 to 6
- grad_context: bfloat16 [6144, 8192], P('dp', 'mp'), may hold values from -12 to 12
Outputs:
- grad_input: bfloat16 [6144, 9216], P(('dp', 'mp'))
- grad_wq: bfloat16 [9216, 8192], P('dp', 'mp')
- grad_wk: bfloat16 [9216, 256], P('dp', 'mp')
- grad_wv: bfloat16 [9216, 256], P('dp', 'mp')
The draws below stay inside these ranges and needn't reach their ends.
All inputs are finite; a program needn't handle non-finite values.
Results may differ from the reference program's by a relative error of at most 0.04.
Values may be sent and summed in bfloat16 or wider, within the bound.
A program may use at most 128 MiB of HBM per device.

```python
import jax
import jax.numpy as jnp
from jax import lax

D_WIN = 9216
HEADS = 32
HEAD_DIM = 256
TOK_DEV = 384
TOKENS = 6144
N_DP = 16
N_MP = 16


def draw_key(key, part):
    key = jax.random.fold_in(key, 3)
    base = jax.random.truncated_normal(key, -5.0, 5.0, (TOKENS, HEAD_DIM), jnp.float32)
    return base.astype(jnp.bfloat16)


def draw_query(key, part):
    key = jax.random.fold_in(key, 5)
    drawn = jax.random.truncated_normal(key, -5.0, 5.0, (TOKENS, HEADS * HEAD_DIM), jnp.float32)
    return drawn.astype(jnp.bfloat16)


def raised(result, own_key, source, target, blocks, factor):
    owner, partner = [(jnp.arange(result.shape[axis_at]) // (result.shape[axis_at] // blocks)).reshape([-1 if axis == axis_at else 1 for axis in range(result.ndim)]) for axis_at in (source, target)]
    chosen = jax.random.permutation(own_key, blocks)[partner]
    strong = (owner == chosen) | (owner == (partner + blocks // 2) % blocks)
    return jnp.where(strong, factor * result, result)


def block_levels(key, dims, pieces, smallest, high):
    def one(position, blocks):
        draws = jax.random.uniform(jax.random.fold_in(jax.random.fold_in(key, 6), position), (blocks,), jnp.float32, smallest / len(pieces), high / len(pieces))
        return jnp.repeat(jnp.exp(draws), dims[position] // blocks).reshape((-1,) + (1,) * (len(dims) - position - 1))

    factor_of = one(*pieces[0])
    for cut in pieces[1:]:
        factor_of = factor_of * one(*cut)
    return factor_of


def normal_values(stream_key, shape, deviation, most, cuts=(), dtype=jnp.bfloat16):
    loudness = block_levels(stream_key, shape, cuts, -0.22, 0.18) if cuts else 1.0
    array = jax.random.normal(stream_key, shape, jnp.float32) * deviation * loudness
    return jnp.minimum(jnp.maximum(array, -most), most).astype(dtype)


def bell_draw_with(own_key, dims, scale, most, cuts, heavy, kind=jnp.bfloat16):
    result = scale * jax.random.normal(own_key, dims, jnp.float32)
    if cuts:
        result = result * block_levels(own_key, dims, cuts, -0.22, 0.18)
    return jnp.clip(raised(result, jax.random.fold_in(own_key, 3), *heavy), -most, most).astype(kind)


def setup_inputs(seed: int = 0) -> dict:
    seeds = jax.random.split(jax.random.key(seed), 9)
    normed = bell_draw_with(seeds[0], (TOKENS, D_WIN), 0.25, 6.0, ((0, 256),), (0, 1, 256, 6.0))
    w_query = normal_values(seeds[1], (D_WIN, HEADS * HEAD_DIM), D_WIN ** -0.5, 0.0625, ((1, 16),))
    w_key = normal_values(seeds[2], (D_WIN, HEAD_DIM), D_WIN ** -0.5, 0.0625, ((1, 16),))
    w_value = normal_values(seeds[3], (D_WIN, HEAD_DIM), D_WIN ** -0.5, 0.0625, ((1, 16),))
    query = draw_query(jax.random.fold_in(seeds[8], 71), 0)
    key = draw_key(jax.random.fold_in(seeds[8], 71), 0)
    value = normal_values(seeds[6], (TOKENS, HEAD_DIM), 1.0, 6.0, ((0, 16),))
    grad_context = normal_values(seeds[7], (TOKENS, HEADS * HEAD_DIM), 2.0, 12.0, ((0, 16), (1, 16)))
    return {"normed": normed, "w_query": w_query, "w_key": w_key, "w_value": w_value, "query": query, "key": key, "value": value, "grad_context": grad_context}


def shard_step(carry, items):
    normed_b, query_b, key_b, value_b, grad_b, w_query, w_key, w_value = items[0], items[1], items[2], items[3], items[4], items[5], items[6], items[7]
    count = query_b.shape[0]
    scale = HEAD_DIM ** -0.5
    q_heads = query_b.reshape(count, HEADS, HEAD_DIM).astype(jnp.float32)
    g_heads = grad_b.reshape(count, HEADS, HEAD_DIM).astype(jnp.float32)
    key_f = key_b.astype(jnp.float32)
    value_f = value_b.astype(jnp.float32)
    scores = jnp.einsum("thd,sd->hts", q_heads, key_f) * scale
    causal = jnp.arange(count)[:, None] >= jnp.arange(count)[None, :]
    scores = jnp.where(causal[None], scores, -jnp.inf)
    top = jnp.max(scores, axis=-1, keepdims=True)
    expo = jnp.exp(scores - top)
    probs = expo / jnp.sum(expo, axis=-1, keepdims=True)
    probs_low = probs.astype(jnp.bfloat16).astype(jnp.float32)
    context = jnp.einsum("hts,sd->thd", probs_low, value_f)
    delta = jnp.sum(g_heads * context, axis=-1)
    dprob = jnp.einsum("thd,sd->hts", g_heads, value_f)
    dscore = (probs * (dprob - jnp.transpose(delta)[:, :, None])).astype(jnp.bfloat16).astype(jnp.float32)
    grad_q = (jnp.einsum("hts,sd->thd", dscore, key_f) * scale).reshape(count, HEADS * HEAD_DIM).astype(jnp.bfloat16)
    grad_k = (jnp.einsum("hts,thd->sd", dscore, q_heads) * scale).astype(jnp.bfloat16)
    grad_v = jnp.einsum("hts,thd->sd", probs_low, g_heads).astype(jnp.bfloat16)
    grads_all = jnp.concatenate([grad_q, grad_k, grad_v], axis=1)
    wpart = jnp.dot(normed_b.T, grads_all, preferred_element_type=jnp.float32).astype(jnp.bfloat16)
    wpart = lax.optimization_barrier(wpart)
    carry = carry + wpart.astype(jnp.float32)
    width = w_query.shape[0]
    q_groups = grad_q.reshape(count, N_MP, -1).astype(jnp.float32)
    k_groups = grad_k.reshape(count, N_MP, -1).astype(jnp.float32)
    v_groups = grad_v.reshape(count, N_MP, -1).astype(jnp.float32)
    wq_groups = w_query.reshape(width, N_MP, -1).astype(jnp.float32)
    wk_groups = w_key.reshape(width, N_MP, -1).astype(jnp.float32)
    wv_groups = w_value.reshape(width, N_MP, -1).astype(jnp.float32)
    ipart = jnp.einsum("tgc,dgc->gtd", q_groups, wq_groups)
    ipart = ipart + jnp.einsum("tgc,dgc->gtd", k_groups, wk_groups)
    ipart = ipart + jnp.einsum("tgc,dgc->gtd", v_groups, wv_groups)
    ipart = lax.optimization_barrier(ipart.astype(jnp.bfloat16))
    grad_input_b = jnp.sum(ipart.astype(jnp.float32), axis=0).astype(jnp.bfloat16)
    return carry, grad_input_b


def reference(normed, w_query, w_key, w_value, query, key, value, grad_context):
    width = w_query.shape[0]
    shards = (
        normed.reshape(N_DP, TOK_DEV, width),
        query.reshape(N_DP, TOK_DEV, HEADS * HEAD_DIM),
        key.reshape(N_DP, TOK_DEV, HEAD_DIM),
        value.reshape(N_DP, TOK_DEV, HEAD_DIM),
        grad_context.reshape(N_DP, TOK_DEV, HEADS * HEAD_DIM),
    )

    def step(carry, items):
        return shard_step(carry, (items[0], items[1], items[2], items[3], items[4], w_query, w_key, w_value))

    start = jnp.zeros((width, HEADS * HEAD_DIM + 2 * HEAD_DIM), jnp.float32)
    total, grad_rows = lax.scan(step, start, shards)
    grads_w = total.astype(jnp.bfloat16)
    grad_input = grad_rows.reshape(N_DP * TOK_DEV, width)
    grad_wq = grads_w[:, :HEADS * HEAD_DIM]
    grad_wk = grads_w[:, HEADS * HEAD_DIM:HEADS * HEAD_DIM + HEAD_DIM]
    grad_wv = grads_w[:, HEADS * HEAD_DIM + HEAD_DIM:]
    return (grad_input, grad_wq, grad_wk, grad_wv)
```

```python
import jax
import jax.numpy as jnp
from jax import lax
from jax.sharding import PartitionSpec as P

HEAD_DIM = 256
Z_GROUPS = [list(range(0, 8)), list(range(8, 16))]
Y_GROUPS = [[z, z + 8] for z in range(8)]


def shards(normed, w_query, w_key, w_value, query, key, value, grad_context):
    rows = query.shape[0]
    heads_local = query.shape[1] // HEAD_DIM
    scale = HEAD_DIM ** (-0.5)
    exchanged = lax.all_to_all(
        jnp.transpose(normed.reshape(normed.shape[0], 2, 8, -1), (2, 0, 1, 3)).reshape(
            8, normed.shape[0], -1
        ),
        "dp", split_axis=0, concat_axis=0, axis_index_groups=Z_GROUPS, tiled=True,
    )
    gathered = lax.all_gather(exchanged, "mp", axis=0, tiled=False)
    gathered = jnp.transpose(gathered, (1, 0, 2, 3)).reshape(8 * rows, -1)
    q_heads = query.reshape(rows, heads_local, HEAD_DIM)
    g_heads = grad_context.reshape(rows, heads_local, HEAD_DIM)
    scores = jnp.einsum("thd,sd->hts", q_heads, key, preferred_element_type=jnp.float32) * scale
    causal = lax.broadcasted_iota(jnp.int32, (rows, rows), 0) >= lax.broadcasted_iota(
        jnp.int32, (rows, rows), 1
    )
    scores = jnp.where(causal[None], scores, -jnp.inf)
    top = jnp.max(scores, axis=-1, keepdims=True)
    expo = jnp.exp(scores - top)
    probs = expo / jnp.sum(expo, axis=-1, keepdims=True)
    probs_low = probs.astype(jnp.bfloat16)
    context = jnp.einsum("hts,sd->thd", probs_low, value, preferred_element_type=jnp.float32)
    delta = jnp.sum(g_heads.astype(jnp.float32) * context, axis=-1)
    dprob = jnp.einsum("thd,sd->hts", g_heads, value, preferred_element_type=jnp.float32)
    dscore = (probs * (dprob - jnp.transpose(delta)[:, :, None])).astype(jnp.bfloat16)
    grad_q = (
        (jnp.einsum("hts,sd->thd", dscore, key, preferred_element_type=jnp.float32) * scale)
        .reshape(rows, -1)
        .astype(jnp.bfloat16)
    )
    key_part = (
        jnp.einsum("hts,thd->ds", dscore, q_heads, preferred_element_type=jnp.float32) * scale
    )
    value_part = jnp.einsum("hts,thd->ds", probs_low, g_heads, preferred_element_type=jnp.float32)
    columns = w_key.shape[1]
    kv = jnp.concatenate(
        [key_part.reshape(-1, columns, rows), value_part.reshape(-1, columns, rows)], axis=1
    ).astype(jnp.bfloat16)
    kv = lax.psum_scatter(kv, "mp", scatter_dimension=0, tiled=False)
    local_grads = jnp.concatenate([grad_q, jnp.transpose(kv)], axis=1)
    grads = lax.all_gather(local_grads, "dp", axis=0, tiled=True, axis_index_groups=Z_GROUPS)
    part = lax.dot_general(
        gathered, grads, (((0,), (0,)), ((), ())), preferred_element_type=jnp.float32
    ).astype(jnp.bfloat16)
    return part, local_grads


def whole(normed, w_query, w_key, w_value, query, key, value, grad_context):
    part, local_grads = shards(
        normed, w_query, w_key, w_value, query, key, value, grad_context
    )
    weights = jnp.concatenate([w_query, w_key, w_value], axis=1)
    total = lax.dot_general(
        local_grads, weights, (((1,), (1,)), ((), ())), preferred_element_type=jnp.float32
    ).astype(jnp.bfloat16)
    grad_input = lax.psum_scatter(total, "mp", scatter_dimension=0, tiled=True)
    weight_sum = lax.psum_scatter(
        part, "dp", scatter_dimension=0, tiled=True, axis_index_groups=Y_GROUPS
    )
    query_cols = w_query.shape[1]
    columns = w_key.shape[1]
    return (
        grad_input,
        weight_sum[:, :query_cols],
        weight_sum[:, query_cols : query_cols + columns],
        weight_sum[:, query_cols + columns :],
    )


def solution(mesh):
    placed = (
        P(("dp", "mp"), None),
        P(None, "mp"),
        P(None, "mp"),
        P(None, "mp"),
        P("dp", "mp"),
        P("dp", None),
        P("dp", None),
        P("dp", "mp"),
    )
    return jax.shard_map(
        whole,
        mesh=mesh,
        in_specs=placed,
        out_specs=(P(("dp", "mp"), None), P("dp", "mp"), P("dp", "mp"), P("dp", "mp")),
        check_vma=False,
    )
```

```python
import jax
import jax.numpy as jnp
from jax import lax
from jax.experimental import pallas as pl
from jax.experimental.pallas import tpu as pltpu
from jax.sharding import PartitionSpec as P

HEAD_DIM = 256
TOK = 384
NZ = 8
CHIPS = 8
CHIP_TOK = 48
FEAT = 9216
HALF = FEAT // 2
BLOCK = 576
ZF = 2 * BLOCK
QC = 512
GC = 544
FC = 768
NCH = HALF // FC
YW = 640
MESH = pl.DeviceIdType.MESH
F32 = jnp.float32
BF16 = jnp.bfloat16
NT = (((1,), (1,)), ((), ()))


def dot(a, b):
    return jnp.dot(a, b, preferred_element_type=F32)


def dot_nt(a, b):
    return lax.dot_general(a, b, NT, preferred_element_type=F32)


def kernel(
    normed, wq_hbm, wkv, query, key, value, grad,
    out_in, out_wq, out_wkv,
    w_buf, s_buf, s_recv, t_buf, n_buf, gt_buf, g_buf, kv_buf, kv_recv, kv_all, kvg_buf,
    p_send, p_recv, r_buf, r_recv, f_send, f_buf, acc, own_buf, y_send, y_recv,
    w_sem, s_sems, a2a_ss, a2a_rs, ag_ss, ag_rs, sib_ss, sib_rs, kv_ss, kv_rs, kz_ss, kz_rs,
    cw_ss, cw_rs, cc_ss, cc_rs, p_ss, p_rs, r_ss, r_rs, f_ss, f_rs, y_sems,
):
    dp = lax.axis_index("dp")
    mp = lax.axis_index("mp")
    z = lax.rem(dp, NZ)
    y_hi = lax.div(dp, NZ)
    base = y_hi * NZ
    core = lax.rem(mp, 2)
    chip = lax.div(mp, 2)
    other = 1 - core
    sibling = (dp, chip * 2 + other)
    zhalf = lax.div(z, 4)
    y_mate = (lax.rem(dp + NZ, 2 * NZ), mp)

    def remote(src, dst, ss, rs, device):
        return pltpu.make_async_remote_copy(
            src_ref=src, dst_ref=dst, send_sem=ss, recv_sem=rs,
            device_id=device, device_id_type=MESH,
        )

    w_copy = pltpu.make_async_copy(wq_hbm, w_buf, w_sem)
    w_copy.start()

    barrier = pltpu.get_barrier_semaphore()
    for i in range(1, NZ):
        there = base + lax.rem(z + i, NZ)
        pl.semaphore_signal(barrier, inc=1, device_id=(there, mp), device_id_type=MESH)
        pl.semaphore_signal(
            barrier, inc=1, device_id=(there, chip * 2 + other), device_id_type=MESH
        )
    pl.semaphore_signal(barrier, inc=1, device_id=y_mate, device_id_type=MESH)
    for i in range(1, 2 * CHIPS):
        pl.semaphore_signal(
            barrier, inc=1, device_id=(dp, lax.rem(mp + i, 2 * CHIPS)), device_id_type=MESH
        )

    for h in range(2):
        for part in range(2):
            cols = normed[:, HALF * part + 2304 * h : HALF * part + 2304 * h + 2304].astype(F32)
            padded = jnp.concatenate([cols, jnp.zeros((8, 2304), F32)], axis=0)
            s_buf[h, :, 2304 * part : 2304 * part + 2304] = padded.astype(BF16)
    pl.semaphore_wait(barrier, 2 * (NZ - 1) + 1 + 2 * CHIPS - 1)
    s_copy = remote(s_buf.at[other], s_recv, s_sems.at[0], s_sems.at[1], sibling)
    s_copy.start()

    key_v = key[...]
    value_v = value[...]
    key_t = jnp.transpose(key_v.astype(F32)).astype(BF16)
    scale = HEAD_DIM ** (-0.5)
    causal = lax.broadcasted_iota(jnp.int32, (TOK, TOK), 0) <= lax.broadcasted_iota(
        jnp.int32, (TOK, TOK), 1
    )
    kp = None
    vp = None
    for h in range(2):
        q_h = query[:, HEAD_DIM * h : HEAD_DIM * h + HEAD_DIM]
        g_h = grad[:, HEAD_DIM * h : HEAD_DIM * h + HEAD_DIM]
        scores = jnp.where(causal, dot_nt(key_v, q_h) * scale, -jnp.inf)
        expo = jnp.exp(scores - jnp.max(scores, axis=0, keepdims=True))
        probs = expo * (1.0 / jnp.sum(expo, axis=0, keepdims=True))
        low = probs.astype(BF16)
        dprob = dot_nt(value_v, g_h)
        delta = jnp.sum(low.astype(F32) * dprob, axis=0, keepdims=True)
        dscore = (probs * (dprob - delta)).astype(BF16)
        kp_h = dot(dscore, q_h)
        vp_h = dot(low, g_h)
        kp = kp_h if kp is None else kp + kp_h
        vp = vp_h if vp is None else vp + vp_h
        gq = dot(key_t, dscore) * scale
        gt_buf[z, HEAD_DIM * h : HEAD_DIM * h + HEAD_DIM, :] = gq.astype(BF16)
        g_buf[:, HEAD_DIM * h : HEAD_DIM * h + HEAD_DIM] = jnp.transpose(gq).astype(BF16)
        if h == 0:
            s_copy.wait_recv()
            mine = s_buf[core].astype(F32)[:24]
            theirs = s_recv[...].astype(F32)[:24]
            first = jnp.where(core == 0, mine, theirs)
            second = jnp.where(core == 0, theirs, mine)
            both = jnp.concatenate([first, second], axis=0)
            for j in range(4):
                block = jnp.concatenate(
                    [
                        both[:, BLOCK * j : BLOCK * j + BLOCK],
                        both[:, 2304 + BLOCK * j : 2304 + BLOCK * j + BLOCK],
                    ],
                    axis=1,
                )
                t_buf[j] = block.astype(BF16)
            chip_rows = pl.ds(pl.multiple_of(chip * CHIP_TOK, 16), CHIP_TOK)

            def a2a(j):
                peer = 4 * core + j
                return remote(
                    t_buf.at[j], n_buf.at[z, chip_rows, :], a2a_ss.at[j], a2a_rs.at[lax.rem(z, 4)],
                    (base + peer, chip * 2 + zhalf),
                )

            def a2a_in(j):
                peer = 4 * core + j
                return remote(
                    t_buf.at[j], n_buf.at[peer, chip_rows, :], a2a_ss.at[j], a2a_rs.at[j],
                    (base + peer, chip * 2 + zhalf),
                )

            for j in range(4):
                @pl.when(4 * core + j != z)
                def _(j=j):
                    a2a(j).start()

                @pl.when(4 * core + j == z)
                def _(j=j):
                    n_buf[z, chip_rows, :] = t_buf[j]

    right = (base + lax.rem(z + 1, NZ), mp)
    left = (base + lax.rem(z + NZ - 1, NZ), mp)

    def ring(s):
        slot_r = lax.rem(z - (s - 1) + NZ, NZ)
        slot_l = lax.rem(z + (s - 1), NZ)
        if s < 4:
            src_r, src_l = gt_buf.at[slot_r], gt_buf.at[slot_l]
        else:
            src_r, src_l = gt_buf.at[slot_r, 0:256, :], gt_buf.at[slot_l, 256:512, :]
        return (
            remote(src_r, src_r, cw_ss.at[s - 1], cw_rs.at[s - 1], right),
            remote(src_l, src_l, cc_ss.at[s - 1], cc_rs.at[s - 1], left),
        )

    def ring_in(s):
        slot_r = lax.rem(z - s + NZ, NZ)
        slot_l = lax.rem(z + s, NZ)
        if s < 4:
            dst_r, dst_l = gt_buf.at[slot_r], gt_buf.at[slot_l]
        else:
            dst_r, dst_l = gt_buf.at[slot_r, 0:256, :], gt_buf.at[slot_l, 256:512, :]
        return (
            remote(dst_r, dst_r, cw_ss.at[s - 1], cw_rs.at[s - 1], right),
            remote(dst_l, dst_l, cc_ss.at[s - 1], cc_rs.at[s - 1], left),
        )

    def ring_start(s):
        for copy in ring(s):
            copy.start()

    def ring_wait(s):
        for copy in ring_in(s):
            copy.wait_recv()

    kp_t = jnp.transpose(kp * scale)
    vp_t = jnp.transpose(vp)
    kv_buf[:, 0:16, :] = kp_t.reshape(16, 16, TOK).astype(BF16)
    kv_buf[:, 16:32, :] = vp_t.reshape(16, 16, TOK).astype(BF16)

    def kv_copy(i):
        there = lax.rem(mp + i, 2 * CHIPS)
        return remote(
            kv_buf.at[there], kv_recv.at[i - 1], kv_ss.at[i - 1], kv_rs.at[i - 1], (dp, there)
        )

    for i in range(1, 2 * CHIPS):
        kv_copy(i).start()
    ring_start(1)

    def n_block(k):
        return n_buf.at[
            pl.ds(4 * core, 4), pl.ds(pl.multiple_of(k * CHIP_TOK, 16), CHIP_TOK), :
        ]

    def n_block_in(k):
        return n_buf.at[
            pl.ds(4 * other, 4), pl.ds(pl.multiple_of(k * CHIP_TOK, 16), CHIP_TOK), :
        ]

    def ag(i):
        there = lax.rem(chip + i, CHIPS)
        return remote(
            n_block(chip), n_block(chip), ag_ss.at[i - 1], ag_rs.at[i - 1],
            (dp, there * 2 + core),
        )

    def ag_in(i):
        k = lax.rem(chip - i + CHIPS, CHIPS)
        return remote(n_block(k), n_block(k), ag_ss.at[i - 1], ag_rs.at[i - 1], sibling)

    def sib(i):
        k = lax.rem(chip - i + CHIPS, CHIPS)
        return remote(n_block(k), n_block(k), sib_ss.at[i], sib_rs.at[i], sibling)

    def sib_in(i):
        k = lax.rem(chip - i + CHIPS, CHIPS)
        return remote(n_block_in(k), n_block_in(k), sib_ss.at[i], sib_rs.at[i], sibling)

    for j in range(4):
        @pl.when(4 * core + j != z)
        def _(j=j):
            a2a_in(j).wait_recv()
    for i in range(1, CHIPS):
        ag(i).start()
    sib(0).start()

    for i in range(1, 2 * CHIPS):
        kv_copy(i).wait_recv()
    kv_sum = kv_buf[mp].astype(F32)
    for i in range(15):
        kv_sum = kv_sum + kv_recv[i].astype(F32)
    kv_all[z] = kv_sum.astype(BF16)
    kvg_buf[...] = jnp.transpose(kv_sum).astype(BF16)

    def kz(i):
        return remote(
            kv_all.at[z], kv_all.at[z], kz_ss.at[i - 1], kz_rs.at[i - 1],
            (base + lax.rem(z + i, NZ), mp),
        )

    def kz_in(i):
        slot = lax.rem(z - i + NZ, NZ)
        return remote(
            kv_all.at[slot], kv_all.at[slot], kz_ss.at[i - 1], kz_rs.at[i - 1],
            (base + lax.rem(z + i, NZ), mp),
        )

    for i in range(1, NZ):
        kz(i).start()

    w_copy.wait()

    def partial(first):
        first = pl.multiple_of(first, FC)
        total = dot_nt(g_buf[...], w_buf[pl.ds(first, FC), :])
        return total + dot(kvg_buf[...], wkv[:, pl.ds(first, FC)])

    def p_copy(j):
        return remote(p_send.at[j], p_recv.at[j], p_ss.at[j], p_rs.at[j], sibling)

    def sib_half(j, carry):
        p_send[j] = partial(other * HALF + j * FC).astype(BF16)
        p_copy(j).start()
        return carry

    lax.fori_loop(0, NCH, sib_half, 0)
    ring_wait(1)
    ring_start(2)

    def r_copy(i, j):
        there = lax.rem(chip + i, CHIPS)
        return remote(
            r_buf.at[j, pl.ds(pl.multiple_of(there * CHIP_TOK, 16), CHIP_TOK), :],
            r_recv.at[i - 1, j], r_ss.at[i - 1, j], r_rs.at[i - 1, j],
            (dp, there * 2 + core),
        )

    def own_half(j, carry):
        total = partial(core * HALF + j * FC)
        p_copy(j).wait_recv()
        r_buf[j] = (total + p_recv[j].astype(F32)).astype(BF16)
        for i in range(1, CHIPS):
            r_copy(i, j).start()
        return carry

    lax.fori_loop(0, NCH, own_half, 0)
    ring_wait(2)
    ring_start(3)
    for i in range(1, 4):
        ag_in(i).wait_recv()
        sib(i).start()
    ring_wait(3)
    ring_start(4)
    for i in range(4, CHIPS):
        ag_in(i).wait_recv()
        sib(i).start()
    for i in range(1, NZ):
        kz_in(i).wait_recv()
    ring_wait(4)
    for i in range(CHIPS):
        sib_in(i).wait_recv()

    acc[...] = jnp.zeros_like(acc)

    def wgrad(p, carry):
        top = jnp.concatenate([gt_buf[2 * p], gt_buf[2 * p + 1]], axis=1)
        low = jnp.concatenate([kv_all[2 * p], kv_all[2 * p + 1]], axis=1)
        for c in range(3):
            cols = slice(TOK * c, TOK * c + TOK)
            rhs = jnp.concatenate([n_buf[2 * p, :, cols], n_buf[2 * p + 1, :, cols]], axis=0)
            acc[0:QC, cols] += dot(top, rhs)
            acc[QC:GC, cols] += dot(low, rhs)
        return carry

    lax.fori_loop(0, NZ // 2, wgrad, 0)

    def split(r, carry):
        rows = pl.ds(pl.multiple_of(r * 32, 32), 32)
        here = acc[rows, :]
        lower = here[:, 0:YW]
        upper = pltpu.roll(here, BLOCK, 1)[:, 0:YW]
        y_send[rows, :] = jnp.where(y_hi == 0, upper, lower).astype(BF16)
        own_buf[rows, :] = jnp.where(y_hi == 0, lower, upper)
        return carry

    lax.fori_loop(0, GC // 32, split, 0)
    y_copy = remote(y_send, y_recv, y_sems.at[0], y_sems.at[1], y_mate)
    y_copy.start()

    def f_copy(j):
        return remote(f_send.at[j], f_buf.at[core, j], f_ss.at[j], f_rs.at[j], sibling)

    def f_in(j):
        return remote(f_send.at[j], f_buf.at[other, j], f_ss.at[j], f_rs.at[j], sibling)

    def finish(j, carry):
        rows = pl.ds(pl.multiple_of(chip * CHIP_TOK, 16), CHIP_TOK)
        total = r_buf[j, rows, :].astype(F32)
        for i in range(1, CHIPS):
            r_copy(i, j).wait_recv()
            total = total + r_recv[i - 1, j].astype(F32)
        low, high = total[0:24], total[24:48]
        pad = jnp.zeros((8, FC), F32)
        mine = jnp.where(core == 0, low, high)
        theirs = jnp.where(core == 0, high, low)
        f_buf[core, j] = jnp.concatenate([mine, pad], axis=0).astype(BF16)
        f_send[j] = jnp.concatenate([theirs, pad], axis=0).astype(BF16)
        f_copy(j).start()
        return carry

    lax.fori_loop(0, NCH, finish, 0)
    for j in range(NCH):
        f_in(j).wait_recv()
    for h in range(2):
        for j in range(NCH):
            out_in[:, HALF * h + FC * j : HALF * h + FC * j + FC] = f_buf[h, j].astype(F32)[
                0:24
            ].astype(BF16)

    y_copy.wait_recv()
    for c in range(4):
        rows = slice(128 * c, 128 * c + 128)
        total = own_buf[rows, :] + y_recv[rows, :].astype(F32)
        out_wq[:, rows] = jnp.transpose(total)[0:BLOCK].astype(BF16)
    total = own_buf[QC:GC, :] + y_recv[QC:GC, :].astype(F32)
    out_wkv[...] = total[:, 0:BLOCK].astype(BF16)

    s_copy.wait_send()
    for j in range(4):
        @pl.when(4 * core + j != z)
        def _(j=j):
            a2a(j).wait_send()
    for i in range(1, 2 * CHIPS):
        kv_copy(i).wait_send()
    for i in range(1, NZ):
        kz(i).wait_send()
    for i in range(1, CHIPS):
        ag(i).wait_send()
    for i in range(CHIPS):
        sib(i).wait_send()
    for s in range(1, 5):
        for copy in ring(s):
            copy.wait_send()

    def drain(j, carry):
        p_copy(j).wait_send()
        f_copy(j).wait_send()
        for i in range(1, CHIPS):
            r_copy(i, j).wait_send()
        return carry

    lax.fori_loop(0, NCH, drain, 0)
    y_copy.wait_send()


def shards(normed, w_query, w_key, w_value, query, key, value, grad_context):
    wkv = jnp.concatenate([jnp.transpose(w_key), jnp.transpose(w_value)], axis=0)
    vmem = pl.BlockSpec(memory_space=pltpu.VMEM)
    dma = pltpu.SemaphoreType.DMA
    grad_input, grad_wq, grad_wkv = pl.pallas_call(
        kernel,
        out_shape=(
            jax.ShapeDtypeStruct((24, FEAT), BF16),
            jax.ShapeDtypeStruct((BLOCK, QC), BF16),
            jax.ShapeDtypeStruct((32, BLOCK), BF16),
        ),
        in_specs=[vmem, pl.BlockSpec(memory_space=pl.ANY), vmem, vmem, vmem, vmem, vmem],
        out_specs=(vmem, vmem, vmem),
        scratch_shapes=[
            pltpu.VMEM((FEAT, QC), BF16),
            pltpu.VMEM((2, 32, HALF), BF16),
            pltpu.VMEM((32, HALF), BF16),
            pltpu.VMEM((4, CHIP_TOK, ZF), BF16),
            pltpu.VMEM((NZ, TOK, ZF), BF16),
            pltpu.VMEM((NZ, QC, TOK), BF16),
            pltpu.VMEM((TOK, QC), BF16),
            pltpu.VMEM((16, 32, TOK), BF16),
            pltpu.VMEM((15, 32, TOK), BF16),
            pltpu.VMEM((NZ, 32, TOK), BF16),
            pltpu.VMEM((TOK, 32), BF16),
            pltpu.VMEM((NCH, TOK, FC), BF16),
            pltpu.VMEM((NCH, TOK, FC), BF16),
            pltpu.VMEM((NCH, TOK, FC), BF16),
            pltpu.VMEM((CHIPS - 1, NCH, CHIP_TOK, FC), BF16),
            pltpu.VMEM((NCH, 32, FC), BF16),
            pltpu.VMEM((2, NCH, 32, FC), BF16),
            pltpu.VMEM((GC, ZF), F32),
            pltpu.VMEM((GC, YW), F32),
            pltpu.VMEM((GC, YW), BF16),
            pltpu.VMEM((GC, YW), BF16),
            dma,
            dma((2,)),
            dma((4,)), dma((4,)),
            dma((7,)), dma((7,)),
            dma((8,)), dma((8,)),
            dma((15,)), dma((15,)),
            dma((7,)), dma((7,)),
            dma((4,)), dma((4,)), dma((4,)), dma((4,)),
            dma((NCH,)), dma((NCH,)),
            dma((7, NCH)), dma((7, NCH)),
            dma((NCH,)), dma((NCH,)),
            dma((2,)),
        ],
        compiler_params=pltpu.CompilerParams(
            collective_id=0, has_side_effects=True, vmem_limit_bytes=60 * 1024 * 1024
        ),
    )(normed, w_query, wkv, query, key, value, grad_context)
    return grad_input, grad_wq, jnp.transpose(grad_wkv[0:16]), jnp.transpose(grad_wkv[16:32])


def solution(mesh):
    placed = (
        P(("dp", "mp"), None),
        P(None, "mp"),
        P(None, "mp"),
        P(None, "mp"),
        P("dp", "mp"),
        P("dp", None),
        P("dp", None),
        P("dp", "mp"),
    )
    return jax.shard_map(
        shards,
        mesh=mesh,
        in_specs=placed,
        out_specs=(P(("dp", "mp"), None), P("dp", "mp"), P("dp", "mp"), P("dp", "mp")),
        check_vma=False,
    )
```

```python
import jax
import jax.numpy as jnp
from jax import lax
from jax.experimental import pallas as pl
from jax.experimental.pallas import tpu as pltpu
from jax.sharding import PartitionSpec as P

HEAD_DIM = 256
TOK = 384
NZ = 8
CHIPS = 8
CHIP_TOK = 48
FEAT = 9216
HALF = FEAT // 2
BLOCK = 576
ZF = 2 * BLOCK
QC = 512
GC = 544
FC = 768
NCH = HALF // FC
YW = 640
MESH = pl.DeviceIdType.MESH
F32 = jnp.float32
BF16 = jnp.bfloat16
NT = (((1,), (1,)), ((), ()))


def dot(a, b):
    return jnp.dot(a, b, preferred_element_type=F32)


def dot_nt(a, b):
    return lax.dot_general(a, b, NT, preferred_element_type=F32)


def kernel(
    normed, wq_hbm, wk_t, wv_t, query, key, value, grad,
    out_in, out_wq, out_wk, out_wv,
    w_buf, wkv, s_buf, s_recv, t_buf, n_buf, gt_buf, g_buf, kv_buf, kv_recv, kv_all, kvg_buf,
    p_send, p_recv, r_buf, rx_recv, rx_send, rx_last, ry_recv, ry_last, f_send, f_buf,
    acc, own_buf, own_kv, y_send, y_recv, ykv_send, ykv_recv,
    w_sems, s_sems, a2a_ss, a2a_rs, agy_ss, agy_rs, agx_ss, agx_rs, agd_ss, agd_rs,
    sib_ss, sib_rs, kv_ss, kv_rs, kz_ss, kz_rs,
    cw_ss, cw_rs, cc_ss, cc_rs, p_ss, p_rs,
    rx_ss, rx_rs, rxy_ss, rxy_rs, ry_ss, ry_rs, ryx_ss, ryx_rs, f_ss, f_rs, y_ss, y_rs,
):
    dp = lax.axis_index("dp")
    mp = lax.axis_index("mp")
    z = lax.rem(dp, NZ)
    y_hi = lax.div(dp, NZ)
    base = y_hi * NZ
    core = lax.rem(mp, 2)
    chip = lax.div(mp, 2)
    other = 1 - core
    sibling = (dp, chip * 2 + other)
    zhalf = lax.div(z, 4)
    x = lax.div(chip, 2)
    y_lo = lax.rem(chip, 2)
    y_chip = chip + 1 - 2 * y_lo
    y_mate = (lax.rem(dp + NZ, 2 * NZ), mp)

    def remote(src, dst, ss, rs, device):
        return pltpu.make_async_remote_copy(
            src_ref=src, dst_ref=dst, send_sem=ss, recv_sem=rs,
            device_id=device, device_id_type=MESH,
        )

    def w_copy(half, j):
        rows = pl.ds(pl.multiple_of((half * NCH + j) * FC, FC), FC)
        return pltpu.make_async_copy(
            wq_hbm.at[rows, :], w_buf.at[rows, :], w_sems.at[half * NCH + j]
        )

    for j in range(NCH):
        w_copy(other, j).start()
    for j in range(NCH):
        w_copy(core, j).start()

    barrier = pltpu.get_barrier_semaphore()
    for i in range(1, NZ):
        there = base + lax.rem(z + i, NZ)
        pl.semaphore_signal(barrier, inc=1, device_id=(there, mp), device_id_type=MESH)
        pl.semaphore_signal(
            barrier, inc=1, device_id=(there, chip * 2 + other), device_id_type=MESH
        )
    pl.semaphore_signal(barrier, inc=1, device_id=y_mate, device_id_type=MESH)
    for i in range(1, 2 * CHIPS):
        pl.semaphore_signal(
            barrier, inc=1, device_id=(dp, lax.rem(mp + i, 2 * CHIPS)), device_id_type=MESH
        )

    wkv[0:16, :] = wk_t[...]
    wkv[16:32, :] = wv_t[...]
    for h in range(2):
        for part in range(2):
            cols = normed[:, HALF * part + 2304 * h : HALF * part + 2304 * h + 2304].astype(F32)
            padded = jnp.concatenate([cols, jnp.zeros((8, 2304), F32)], axis=0)
            s_buf[h, :, 2304 * part : 2304 * part + 2304] = padded.astype(BF16)
    pl.semaphore_wait(barrier, 2 * (NZ - 1) + 1 + 2 * CHIPS - 1)
    s_copy = remote(s_buf.at[other], s_recv, s_sems.at[0], s_sems.at[1], sibling)
    s_copy.start()

    key_v = key[...]
    value_v = value[...]
    key_t = jnp.transpose(key_v.astype(F32)).astype(BF16)
    scale = HEAD_DIM ** (-0.5)
    causal = lax.broadcasted_iota(jnp.int32, (TOK, TOK), 0) <= lax.broadcasted_iota(
        jnp.int32, (TOK, TOK), 1
    )
    kp = None
    vp = None
    for h in range(2):
        q_h = query[:, HEAD_DIM * h : HEAD_DIM * h + HEAD_DIM]
        g_h = grad[:, HEAD_DIM * h : HEAD_DIM * h + HEAD_DIM]
        scores = jnp.where(causal, dot_nt(key_v, q_h) * scale, -jnp.inf)
        expo = jnp.exp(scores - jnp.max(scores, axis=0, keepdims=True))
        probs = expo * (1.0 / jnp.sum(expo, axis=0, keepdims=True))
        low = probs.astype(BF16)
        dprob = dot_nt(value_v, g_h)
        delta = jnp.sum(low.astype(F32) * dprob, axis=0, keepdims=True)
        dscore = (probs * (dprob - delta)).astype(BF16)
        kp_h = dot(dscore, q_h)
        vp_h = dot(low, g_h)
        kp = kp_h if kp is None else kp + kp_h
        vp = vp_h if vp is None else vp + vp_h
        gq = dot(key_t, dscore) * scale
        gt_buf[z, HEAD_DIM * h : HEAD_DIM * h + HEAD_DIM, :] = gq.astype(BF16)
        g_buf[:, HEAD_DIM * h : HEAD_DIM * h + HEAD_DIM] = jnp.transpose(gq).astype(BF16)
        if h == 0:
            s_copy.wait_recv()
            mine = s_buf[core].astype(F32)[:24]
            theirs = s_recv[...].astype(F32)[:24]
            first = jnp.where(core == 0, mine, theirs)
            second = jnp.where(core == 0, theirs, mine)
            both = jnp.concatenate([first, second], axis=0)
            for j in range(4):
                block = jnp.concatenate(
                    [
                        both[:, BLOCK * j : BLOCK * j + BLOCK],
                        both[:, 2304 + BLOCK * j : 2304 + BLOCK * j + BLOCK],
                    ],
                    axis=1,
                )
                t_buf[j] = block.astype(BF16)
            chip_rows = pl.ds(pl.multiple_of(chip * CHIP_TOK, 16), CHIP_TOK)

            def a2a(j):
                peer = 4 * core + j
                return remote(
                    t_buf.at[j], n_buf.at[z, chip_rows, :], a2a_ss.at[j], a2a_rs.at[lax.rem(z, 4)],
                    (base + peer, chip * 2 + zhalf),
                )

            def a2a_in(j):
                peer = 4 * core + j
                return remote(
                    t_buf.at[j], n_buf.at[peer, chip_rows, :], a2a_ss.at[j], a2a_rs.at[j],
                    (base + peer, chip * 2 + zhalf),
                )

            for j in range(4):
                @pl.when(4 * core + j != z)
                def _(j=j):
                    a2a(j).start()

                @pl.when(4 * core + j == z)
                def _(j=j):
                    n_buf[z, chip_rows, :] = t_buf[j]

    right = (base + lax.rem(z + 1, NZ), mp)
    left = (base + lax.rem(z + NZ - 1, NZ), mp)

    def ring(s):
        slot_r = lax.rem(z - (s - 1) + NZ, NZ)
        slot_l = lax.rem(z + (s - 1), NZ)
        if s < 4:
            src_r, src_l = gt_buf.at[slot_r], gt_buf.at[slot_l]
        else:
            src_r, src_l = gt_buf.at[slot_r, 0:256, :], gt_buf.at[slot_l, 256:512, :]
        return (
            remote(src_r, src_r, cw_ss.at[s - 1], cw_rs.at[s - 1], right),
            remote(src_l, src_l, cc_ss.at[s - 1], cc_rs.at[s - 1], left),
        )

    def ring_in(s):
        slot_r = lax.rem(z - s + NZ, NZ)
        slot_l = lax.rem(z + s, NZ)
        if s < 4:
            dst_r, dst_l = gt_buf.at[slot_r], gt_buf.at[slot_l]
        else:
            dst_r, dst_l = gt_buf.at[slot_r, 0:256, :], gt_buf.at[slot_l, 256:512, :]
        return (
            remote(dst_r, dst_r, cw_ss.at[s - 1], cw_rs.at[s - 1], right),
            remote(dst_l, dst_l, cc_ss.at[s - 1], cc_rs.at[s - 1], left),
        )

    def ring_start(s):
        for copy in ring(s):
            copy.start()

    def ring_wait(s):
        for copy in ring_in(s):
            copy.wait_recv()

    kp_t = jnp.transpose(kp * scale)
    vp_t = jnp.transpose(vp)
    kv_buf[:, 0:16, :] = kp_t.reshape(16, 16, TOK).astype(BF16)
    kv_buf[:, 16:32, :] = vp_t.reshape(16, 16, TOK).astype(BF16)

    def kv_copy(i):
        there = lax.rem(mp + i, 2 * CHIPS)
        return remote(
            kv_buf.at[there], kv_recv.at[i - 1], kv_ss.at[i - 1], kv_rs.at[i - 1], (dp, there)
        )

    for i in range(1, 2 * CHIPS):
        kv_copy(i).start()
    ring_start(1)

    def n_rows(k):
        return pl.ds(pl.multiple_of(k * CHIP_TOK, 16), CHIP_TOK)

    def piece(n, k):
        return n_buf.at[4 * core + lax.rem(z + n, 4), n_rows(k), :]

    def x_chip(d):
        return lax.rem(x + d, 4) * 2 + y_lo

    def x_from(d):
        return lax.rem(x + 4 - d, 4) * 2 + y_lo

    def ag_y(n):
        return remote(
            piece(n, chip), piece(n, chip), agy_ss.at[n], agy_rs.at[n], (dp, y_chip * 2 + core)
        )

    def ag_x(n, d):
        return remote(
            piece(n, chip), piece(n, chip), agx_ss.at[n, d - 1], agx_rs.at[n, d - 1],
            (dp, x_chip(d) * 2 + core),
        )

    def ag_d(n, d):
        if n % 2 == 0:
            k, device = y_chip, (dp, x_chip(d) * 2 + core)
        else:
            k, device = x_from(d), (dp, y_chip * 2 + core)
        return remote(piece(n, k), piece(n, k), agd_ss.at[n, d - 1], agd_rs.at[n, d - 1], device)

    def n_block(half, k):
        return n_buf.at[pl.ds(4 * half, 4), n_rows(k), :]

    def sib_chip(i):
        if i == 0:
            return chip
        if i == 1:
            return y_chip
        k = x_from((i - 2) % 3 + 1)
        return k if i < 5 else k + 1 - 2 * y_lo

    def sib(i):
        block = n_block(core, sib_chip(i))
        return remote(block, block, sib_ss.at[i], sib_rs.at[i], sibling)

    def sib_in(i):
        block = n_block(other, sib_chip(i))
        return remote(block, block, sib_ss.at[i], sib_rs.at[i], sibling)

    def ag_first(n):
        j = lax.rem(z + n, 4)

        @pl.when(4 * core + j != z)
        def _():
            a2a_in(j).wait_recv()

        ag_y(n).start()
        for d in (1, 3, 2):
            ag_x(n, d).start()

    def ag_second(n):
        if n % 2 == 0:
            ag_y(n).wait_recv()
            for d in (1, 3, 2):
                ag_d(n, d).start()
        else:
            for d in (1, 3, 2):
                ag_x(n, d).wait_recv()
                ag_d(n, d).start()

    def ag_last():
        for n in (1, 3):
            ag_y(n).wait_recv()
        sib(1).start()
        for d in (1, 3, 2):
            for n in (0, 2):
                ag_x(n, d).wait_recv()
            sib(1 + d).start()
        for d in (1, 3, 2):
            for n in range(4):
                ag_d(n, d).wait_recv()
            sib(4 + d).start()

    for i in range(1, 2 * CHIPS):
        kv_copy(i).wait_recv()
    kv_sum = kv_buf[mp].astype(F32)
    for i in range(15):
        kv_sum = kv_sum + kv_recv[i].astype(F32)
    kv_all[z] = kv_sum.astype(BF16)
    kvg_buf[...] = jnp.transpose(kv_sum).astype(BF16)

    def kz(i):
        return remote(
            kv_all.at[z], kv_all.at[z], kz_ss.at[i - 1], kz_rs.at[i - 1],
            (base + lax.rem(z + i, NZ), mp),
        )

    def kz_in(i):
        slot = lax.rem(z - i + NZ, NZ)
        return remote(
            kv_all.at[slot], kv_all.at[slot], kz_ss.at[i - 1], kz_rs.at[i - 1],
            (base + lax.rem(z + i, NZ), mp),
        )

    for i in range(1, NZ):
        kz(i).start()

    def partial(half, j):
        first = pl.multiple_of((half * NCH + j) * FC, FC)
        w_copy(half, j).wait()
        total = dot_nt(g_buf[...], w_buf[pl.ds(first, FC), :])
        return total + dot(kvg_buf[...], wkv[:, pl.ds(first, FC)])

    def p_copy(j):
        return remote(p_send.at[j], p_recv.at[j], p_ss.at[j], p_rs.at[j], sibling)

    def sib_half(j):
        p_send[j] = partial(other, j).astype(BF16)
        p_copy(j).start()

    def rx_copy(j, d):
        n = 2 * (j // 3) + j % 3 - 1
        return remote(
            r_buf.at[j, lax.rem(x + d, 4)], rx_recv.at[n, d - 1],
            rx_ss.at[n, d - 1], rx_rs.at[n, d - 1], (dp, x_chip(d) * 2 + core),
        )

    def rxy_copy(j):
        n = 2 * (j // 3) + j % 3 - 1
        return remote(
            rx_send.at[n], rx_last.at[n], rxy_ss.at[n], rxy_rs.at[n], (dp, y_chip * 2 + core)
        )

    def ry_copy(j):
        return remote(
            r_buf.at[j, :, 1 - y_lo], ry_recv.at[j // 3], ry_ss.at[j // 3], ry_rs.at[j // 3],
            (dp, y_chip * 2 + core),
        )

    def ryx_copy(j, d):
        return remote(
            r_buf.at[j, lax.rem(x + d, 4), y_lo], ry_last.at[j // 3, d - 1],
            ryx_ss.at[j // 3, d - 1], ryx_rs.at[j // 3, d - 1], (dp, x_chip(d) * 2 + core),
        )

    def own_half(j):
        total = partial(core, j)
        p_copy(j).wait_recv()
        total = (total + p_recv[j].astype(F32)).astype(BF16)
        r_buf[j] = total.reshape(4, 2, CHIP_TOK, FC)
        if j % 3 == 0:
            ry_copy(j).start()
        else:
            for d in (1, 3, 2):
                rx_copy(j, d).start()

    def rs_second(j):
        if j % 3 == 0:
            ry_copy(j).wait_recv()
            for k in range(4):
                r_buf[j, k, y_lo] = (
                    r_buf[j, k, y_lo].astype(F32) + ry_recv[j // 3, k].astype(F32)
                ).astype(BF16)
            for d in (1, 3, 2):
                ryx_copy(j, d).start()
        else:
            n = 2 * (j // 3) + j % 3 - 1
            for d in range(1, 4):
                rx_copy(j, d).wait_recv()
            out = r_buf[j, x, 1 - y_lo].astype(F32)
            for d in range(3):
                out = out + rx_recv[n, d, 1 - y_lo].astype(F32)
            rx_send[n] = out.astype(BF16)
            rxy_copy(j).start()

    def rs_last(j):
        total = r_buf[j, x, y_lo].astype(F32)
        if j % 3 == 0:
            for d in range(1, 4):
                ryx_copy(j, d).wait_recv()
                total = total + ry_last[j // 3, d - 1].astype(F32)
        else:
            n = 2 * (j // 3) + j % 3 - 1
            for d in range(3):
                total = total + rx_recv[n, d, y_lo].astype(F32)
            rxy_copy(j).wait_recv()
            total = total + rx_last[n].astype(F32)
        low, high = total[0:24], total[24:48]
        pad = jnp.zeros((8, FC), F32)
        mine = jnp.where(core == 0, low, high)
        theirs = jnp.where(core == 0, high, low)
        f_buf[core, j] = jnp.concatenate([mine, pad], axis=0).astype(BF16)
        f_send[j] = jnp.concatenate([theirs, pad], axis=0).astype(BF16)
        f_copy(j).start()

    def f_copy(j):
        return remote(f_send.at[j], f_buf.at[core, j], f_ss.at[j], f_rs.at[j], sibling)

    def f_in(j):
        return remote(f_send.at[j], f_buf.at[other, j], f_ss.at[j], f_rs.at[j], sibling)

    def wgrad(za, zb, top_rows, with_kv):
        top = jnp.concatenate([gt_buf[za, top_rows, :], gt_buf[zb, top_rows, :]], axis=1)
        low = jnp.concatenate([kv_all[za], kv_all[zb]], axis=1)
        for c in range(3):
            cols = slice(TOK * c, TOK * c + TOK)
            rhs = jnp.concatenate([n_buf[za, :, cols], n_buf[zb, :, cols]], axis=0)
            acc[top_rows, cols] += dot(top, rhs)
            if with_kv:
                acc[QC:GC, cols] += dot(low, rhs)

    def wgrad_pair(s):
        wgrad(lax.rem(z + NZ - s, NZ), lax.rem(z + s, NZ), slice(0, QC), True)

    def y_copy(r):
        cols = slice(256 * r, 256 * r + 256)
        return remote(y_send.at[:, cols], y_recv.at[:, cols], y_ss.at[r], y_rs.at[r], y_mate)

    def ykv_copy():
        return remote(ykv_send, ykv_recv, y_ss.at[2], y_rs.at[2], y_mate)

    def halves(rows):
        here = acc[rows, :]
        lower = here[:, 0:YW]
        upper = pltpu.roll(here, BLOCK, 1)[:, 0:YW]
        return jnp.where(y_hi == 0, lower, upper), jnp.where(y_hi == 0, upper, lower)

    acc[...] = jnp.zeros_like(acc)
    sib_half(0)
    ag_first(0)
    sib_half(1)
    sib_half(2)
    ag_first(1)
    sib_half(3)
    ag_first(2)
    sib_half(4)
    sib_half(5)
    ag_first(3)
    sib(0).start()
    ag_second(0)
    ring_wait(1)
    ring_start(2)
    ag_second(1)
    own_half(0)
    own_half(1)
    ag_second(2)
    ag_second(3)
    own_half(2)
    ring_wait(2)
    ring_start(3)
    own_half(3)
    own_half(4)
    own_half(5)
    rs_second(0)
    ag_last()
    ring_wait(3)
    ring_start(4)
    for i in range(1, NZ):
        kz_in(i).wait_recv()
    for i in range(CHIPS):
        sib_in(i).wait_recv()
    wgrad_pair(1)
    rs_second(1)
    wgrad_pair(2)
    rs_second(2)
    rs_second(3)
    wgrad_pair(3)
    ring_wait(4)
    for r in range(2):
        rows = slice(256 * r, 256 * r + 256)
        wgrad(z, lax.rem(z + 4, NZ), rows, r == 1)
        for q in range(2):
            quarter = slice(256 * r + 128 * q, 256 * r + 128 * q + 128)
            mine, theirs = halves(quarter)
            y_send[:, quarter] = jnp.transpose(theirs)[0:BLOCK].astype(BF16)
            own_buf[:, quarter] = jnp.transpose(mine)[0:BLOCK]
        y_copy(r).start()
    mine, theirs = halves(slice(QC, GC))
    own_kv[...] = mine
    ykv_send[...] = theirs.astype(BF16)
    ykv_copy().start()
    rs_second(4)
    rs_second(5)
    for j in range(NCH):
        rs_last(j)
    for j in range(NCH):
        f_in(j).wait_recv()
    for h in range(2):
        for j in range(NCH):
            out_in[:, HALF * h + FC * j : HALF * h + FC * j + FC] = f_buf[h, j].astype(F32)[
                0:24
            ].astype(BF16)
    for r in range(2):
        y_copy(r).wait_recv()
        cols = slice(256 * r, 256 * r + 256)
        out_wq[:, cols] = (own_buf[:, cols] + y_recv[:, cols].astype(F32)).astype(BF16)
    ykv_copy().wait_recv()
    total = (own_kv[...] + ykv_recv[...].astype(F32))[:, 0:BLOCK].astype(BF16)
    out_wk[...] = total[0:16]
    out_wv[...] = total[16:32]

    s_copy.wait_send()
    for j in range(4):
        @pl.when(4 * core + j != z)
        def _(j=j):
            a2a(j).wait_send()
    for i in range(1, 2 * CHIPS):
        kv_copy(i).wait_send()
    for i in range(1, NZ):
        kz(i).wait_send()
    for n in range(4):
        ag_y(n).wait_send()
        for d in range(1, 4):
            ag_x(n, d).wait_send()
            ag_d(n, d).wait_send()
    for i in range(CHIPS):
        sib(i).wait_send()
    for s in range(1, 5):
        for copy in ring(s):
            copy.wait_send()
    for j in range(NCH):
        p_copy(j).wait_send()
        f_copy(j).wait_send()
        if j % 3 == 0:
            ry_copy(j).wait_send()
            for d in range(1, 4):
                ryx_copy(j, d).wait_send()
        else:
            for d in range(1, 4):
                rx_copy(j, d).wait_send()
            rxy_copy(j).wait_send()
    for r in range(2):
        y_copy(r).wait_send()
    ykv_copy().wait_send()


def shards(normed, w_query, w_key, w_value, query, key, value, grad_context):
    vmem = pl.BlockSpec(memory_space=pltpu.VMEM)
    dma = pltpu.SemaphoreType.DMA
    grad_input, grad_wq, grad_wk, grad_wv = pl.pallas_call(
        kernel,
        out_shape=(
            jax.ShapeDtypeStruct((24, FEAT), BF16),
            jax.ShapeDtypeStruct((BLOCK, QC), BF16),
            jax.ShapeDtypeStruct((16, BLOCK), BF16),
            jax.ShapeDtypeStruct((16, BLOCK), BF16),
        ),
        in_specs=[vmem, pl.BlockSpec(memory_space=pl.ANY), vmem, vmem, vmem, vmem, vmem, vmem],
        out_specs=(vmem, vmem, vmem, vmem),
        scratch_shapes=[
            pltpu.VMEM((FEAT, QC), BF16),
            pltpu.VMEM((32, FEAT), BF16),
            pltpu.VMEM((2, 32, HALF), BF16),
            pltpu.VMEM((32, HALF), BF16),
            pltpu.VMEM((4, CHIP_TOK, ZF), BF16),
            pltpu.VMEM((NZ, TOK, ZF), BF16),
            pltpu.VMEM((NZ, QC, TOK), BF16),
            pltpu.VMEM((TOK, QC), BF16),
            pltpu.VMEM((16, 32, TOK), BF16),
            pltpu.VMEM((15, 32, TOK), BF16),
            pltpu.VMEM((NZ, 32, TOK), BF16),
            pltpu.VMEM((TOK, 32), BF16),
            pltpu.VMEM((NCH, TOK, FC), BF16),
            pltpu.VMEM((NCH, TOK, FC), BF16),
            pltpu.VMEM((NCH, 4, 2, CHIP_TOK, FC), BF16),
            pltpu.VMEM((4, 3, 2, CHIP_TOK, FC), BF16),
            pltpu.VMEM((4, CHIP_TOK, FC), BF16),
            pltpu.VMEM((4, CHIP_TOK, FC), BF16),
            pltpu.VMEM((2, 4, CHIP_TOK, FC), BF16),
            pltpu.VMEM((2, 3, CHIP_TOK, FC), BF16),
            pltpu.VMEM((NCH, 32, FC), BF16),
            pltpu.VMEM((2, NCH, 32, FC), BF16),
            pltpu.VMEM((GC, ZF), F32),
            pltpu.VMEM((BLOCK, QC), F32),
            pltpu.VMEM((32, YW), F32),
            pltpu.VMEM((BLOCK, QC), BF16),
            pltpu.VMEM((BLOCK, QC), BF16),
            pltpu.VMEM((32, YW), BF16),
            pltpu.VMEM((32, YW), BF16),
            dma((2 * NCH,)),
            dma((2,)),
            dma((4,)), dma((4,)),
            dma((4,)), dma((4,)),
            dma((4, 3)), dma((4, 3)),
            dma((4, 3)), dma((4, 3)),
            dma((8,)), dma((8,)),
            dma((15,)), dma((15,)),
            dma((7,)), dma((7,)),
            dma((4,)), dma((4,)), dma((4,)), dma((4,)),
            dma((NCH,)), dma((NCH,)),
            dma((4, 3)), dma((4, 3)), dma((4,)), dma((4,)),
            dma((2,)), dma((2,)), dma((2, 3)), dma((2, 3)),
            dma((NCH,)), dma((NCH,)),
            dma((3,)), dma((3,)),
        ],
        compiler_params=pltpu.CompilerParams(
            collective_id=0, has_side_effects=True, vmem_limit_bytes=60 * 1024 * 1024
        ),
    )(
        normed, w_query, jnp.transpose(w_key), jnp.transpose(w_value),
        query, key, value, grad_context,
    )
    return grad_input, grad_wq, jnp.transpose(grad_wk), jnp.transpose(grad_wv)


def solution(mesh):
    placed = (
        P(("dp", "mp"), None),
        P(None, "mp"),
        P(None, "mp"),
        P(None, "mp"),
        P("dp", "mp"),
        P("dp", None),
        P("dp", None),
        P("dp", "mp"),
    )
    return jax.shard_map(
        shards,
        mesh=mesh,
        in_specs=placed,
        out_specs=(P(("dp", "mp"), None), P("dp", "mp"), P("dp", "mp"), P("dp", "mp")),
        check_vma=False,
    )
```

```python
import jax
import jax.numpy as jnp
from jax import lax
from jax.experimental import pallas as pl
from jax.experimental.pallas import tpu as pltpu
from jax.sharding import PartitionSpec as P

HEAD_DIM = 256
TOK = 384
NZ = 8
CHIPS = 8
CHIP_TOK = 48
FEAT = 9216
HALF = FEAT // 2
BLOCK = 576
ZF = 2 * BLOCK
QC = 512
GC = 544
FC = 768
NCH = HALF // FC
YW = 640
MESH = pl.DeviceIdType.MESH
F32 = jnp.float32
BF16 = jnp.bfloat16
NT = (((1,), (1,)), ((), ()))


def dot(a, b):
    return jnp.dot(a, b, preferred_element_type=F32)


def dot_nt(a, b):
    return lax.dot_general(a, b, NT, preferred_element_type=F32)


def kernel(
    normed, wq_hbm, wk_t, wv_t, query, key, value, grad,
    out_in, out_wq, out_wk, out_wv,
    w_buf, wkv, s_buf, s_recv, t_buf, n_buf, gt_buf, g_buf, kv_buf, kv_recv, kv_all, kvg_buf,
    p_send, p_recv, r_buf, rx_recv, rx_send, rx_last, ry_recv, ry_last, f_send, f_buf,
    acc, own_buf, own_kv, y_send, y_recv, ykv_send, ykv_recv,
    w_sems, s_sems, a2a_ss, a2a_rs, agy_ss, agy_rs, agx_ss, agx_rs, agd_ss, agd_rs,
    sib_ss, sib_rs, kv_ss, kv_rs, kz_ss, kz_rs,
    cw_ss, cw_rs, cc_ss, cc_rs, p_ss, p_rs,
    rx_ss, rx_rs, rxy_ss, rxy_rs, ry_ss, ry_rs, ryx_ss, ryx_rs, f_ss, f_rs, y_ss, y_rs,
):
    dp = lax.axis_index("dp")
    mp = lax.axis_index("mp")
    z = lax.rem(dp, NZ)
    y_hi = lax.div(dp, NZ)
    base = y_hi * NZ
    core = lax.rem(mp, 2)
    chip = lax.div(mp, 2)
    other = 1 - core
    sibling = (dp, chip * 2 + other)
    zhalf = lax.div(z, 4)
    x = lax.div(chip, 2)
    y_lo = lax.rem(chip, 2)
    y_chip = chip + 1 - 2 * y_lo
    y_mate = (lax.rem(dp + NZ, 2 * NZ), mp)

    def remote(src, dst, ss, rs, device):
        return pltpu.make_async_remote_copy(
            src_ref=src, dst_ref=dst, send_sem=ss, recv_sem=rs,
            device_id=device, device_id_type=MESH,
        )

    def w_copy(half, j):
        rows = pl.ds(pl.multiple_of((half * NCH + j) * FC, FC), FC)
        return pltpu.make_async_copy(
            wq_hbm.at[rows, :], w_buf.at[rows, :], w_sems.at[half * NCH + j]
        )

    for j in range(NCH):
        w_copy(other, j).start()
    for j in range(NCH):
        w_copy(core, j).start()

    barrier = pltpu.get_barrier_semaphore()
    for i in range(1, NZ):
        there = base + lax.rem(z + i, NZ)
        pl.semaphore_signal(barrier, inc=1, device_id=(there, mp), device_id_type=MESH)
        pl.semaphore_signal(
            barrier, inc=1, device_id=(there, chip * 2 + other), device_id_type=MESH
        )
    pl.semaphore_signal(barrier, inc=1, device_id=y_mate, device_id_type=MESH)
    for i in range(1, 2 * CHIPS):
        pl.semaphore_signal(
            barrier, inc=1, device_id=(dp, lax.rem(mp + i, 2 * CHIPS)), device_id_type=MESH
        )

    wkv[0:16, :] = wk_t[...]
    wkv[16:32, :] = wv_t[...]
    for h in range(2):
        for part in range(2):
            cols = normed[:, HALF * part + 2304 * h : HALF * part + 2304 * h + 2304].astype(F32)
            padded = jnp.concatenate([cols, jnp.zeros((8, 2304), F32)], axis=0)
            s_buf[h, :, 2304 * part : 2304 * part + 2304] = padded.astype(BF16)
    pl.semaphore_wait(barrier, 2 * (NZ - 1) + 1 + 2 * CHIPS - 1)
    s_copy = remote(s_buf.at[other], s_recv, s_sems.at[0], s_sems.at[1], sibling)
    s_copy.start()

    right = (base + lax.rem(z + 1, NZ), mp)
    left = (base + lax.rem(z + NZ - 1, NZ), mp)

    def ring_pair(h, s, slot_r, slot_l):
        first = HEAD_DIM * h
        if s < 4:
            src_r = gt_buf.at[slot_r, first : first + 256, :]
            src_l = gt_buf.at[slot_l, first : first + 256, :]
        else:
            src_r = gt_buf.at[slot_r, first : first + 128, :]
            src_l = gt_buf.at[slot_l, first + 128 : first + 256, :]
        return (
            remote(src_r, src_r, cw_ss.at[h, s - 1], cw_rs.at[h, s - 1], right),
            remote(src_l, src_l, cc_ss.at[h, s - 1], cc_rs.at[h, s - 1], left),
        )

    def ring(h, s):
        return ring_pair(h, s, lax.rem(z - (s - 1) + NZ, NZ), lax.rem(z + (s - 1), NZ))

    def ring_start(h, s):
        for copy in ring(h, s):
            copy.start()

    def ring_wait(h, s):
        for copy in ring_pair(h, s, lax.rem(z - s + NZ, NZ), lax.rem(z + s, NZ)):
            copy.wait_recv()

    def kz_pair(s, slot_r, slot_l):
        src_r, src_l = kv_all.at[slot_r], kv_all.at[slot_l]
        copies = [remote(src_r, src_r, kz_ss.at[0, s - 1], kz_rs.at[0, s - 1], right)]
        if s < 4:
            copies.append(remote(src_l, src_l, kz_ss.at[1, s - 1], kz_rs.at[1, s - 1], left))
        return copies

    def kz(s):
        return kz_pair(s, lax.rem(z - (s - 1) + NZ, NZ), lax.rem(z + (s - 1), NZ))

    def kz_start(s):
        for copy in kz(s):
            copy.start()

    def kz_wait(s):
        for copy in kz_pair(s, lax.rem(z - s + NZ, NZ), lax.rem(z + s, NZ)):
            copy.wait_recv()

    key_v = key[...]
    value_v = value[...]
    key_t = jnp.transpose(key_v.astype(F32)).astype(BF16)
    scale = HEAD_DIM ** (-0.5)
    causal = lax.broadcasted_iota(jnp.int32, (TOK, TOK), 0) <= lax.broadcasted_iota(
        jnp.int32, (TOK, TOK), 1
    )
    kp = None
    vp = None
    for h in range(2):
        q_h = query[:, HEAD_DIM * h : HEAD_DIM * h + HEAD_DIM]
        g_h = grad[:, HEAD_DIM * h : HEAD_DIM * h + HEAD_DIM]
        scores = jnp.where(causal, dot_nt(key_v, q_h) * scale, -jnp.inf)
        expo = jnp.exp(scores - jnp.max(scores, axis=0, keepdims=True))
        probs = expo * (1.0 / jnp.sum(expo, axis=0, keepdims=True))
        low = probs.astype(BF16)
        dprob = dot_nt(value_v, g_h)
        delta = jnp.sum(low.astype(F32) * dprob, axis=0, keepdims=True)
        dscore = (probs * (dprob - delta)).astype(BF16)
        kp_h = dot(dscore, q_h)
        vp_h = dot(low, g_h)
        kp = kp_h if kp is None else kp + kp_h
        vp = vp_h if vp is None else vp + vp_h
        gq = dot(key_t, dscore) * scale
        gt_buf[z, HEAD_DIM * h : HEAD_DIM * h + HEAD_DIM, :] = gq.astype(BF16)
        g_buf[:, HEAD_DIM * h : HEAD_DIM * h + HEAD_DIM] = jnp.transpose(gq).astype(BF16)
        ring_start(h, 1)
        if h == 0:
            s_copy.wait_recv()
            mine = s_buf[core].astype(F32)[:24]
            theirs = s_recv[...].astype(F32)[:24]
            first = jnp.where(core == 0, mine, theirs)
            second = jnp.where(core == 0, theirs, mine)
            both = jnp.concatenate([first, second], axis=0)
            for j in range(4):
                block = jnp.concatenate(
                    [
                        both[:, BLOCK * j : BLOCK * j + BLOCK],
                        both[:, 2304 + BLOCK * j : 2304 + BLOCK * j + BLOCK],
                    ],
                    axis=1,
                )
                t_buf[j] = block.astype(BF16)
            chip_rows = pl.ds(pl.multiple_of(chip * CHIP_TOK, 16), CHIP_TOK)

            def a2a(j):
                peer = 4 * core + j
                return remote(
                    t_buf.at[j], n_buf.at[z, chip_rows, :], a2a_ss.at[j], a2a_rs.at[lax.rem(z, 4)],
                    (base + peer, chip * 2 + zhalf),
                )

            def a2a_in(j):
                peer = 4 * core + j
                return remote(
                    t_buf.at[j], n_buf.at[peer, chip_rows, :], a2a_ss.at[j], a2a_rs.at[j],
                    (base + peer, chip * 2 + zhalf),
                )

            for j in range(4):
                @pl.when(4 * core + j != z)
                def _(j=j):
                    a2a(j).start()

                @pl.when(4 * core + j == z)
                def _(j=j):
                    n_buf[z, chip_rows, :] = t_buf[j]

    kp_t = jnp.transpose(kp * scale)
    vp_t = jnp.transpose(vp)
    kv_buf[:, 0:16, :] = kp_t.reshape(16, 16, TOK).astype(BF16)
    kv_buf[:, 16:32, :] = vp_t.reshape(16, 16, TOK).astype(BF16)

    def kv_copy(i):
        there = lax.rem(mp + i, 2 * CHIPS)
        return remote(
            kv_buf.at[there], kv_recv.at[i - 1], kv_ss.at[i - 1], kv_rs.at[i - 1], (dp, there)
        )

    for i in range(1, 2 * CHIPS):
        kv_copy(i).start()

    def n_rows(k):
        return pl.ds(pl.multiple_of(k * CHIP_TOK, 16), CHIP_TOK)

    def piece(n, k):
        return n_buf.at[4 * core + lax.rem(z + n, 4), n_rows(k), :]

    def x_chip(d):
        return lax.rem(x + d, 4) * 2 + y_lo

    def x_from(d):
        return lax.rem(x + 4 - d, 4) * 2 + y_lo

    def ag_y(n):
        return remote(
            piece(n, chip), piece(n, chip), agy_ss.at[n], agy_rs.at[n], (dp, y_chip * 2 + core)
        )

    def ag_x(n, d):
        return remote(
            piece(n, chip), piece(n, chip), agx_ss.at[n, d - 1], agx_rs.at[n, d - 1],
            (dp, x_chip(d) * 2 + core),
        )

    def ag_d(n, d):
        if n % 2 == 0:
            k, device = y_chip, (dp, x_chip(d) * 2 + core)
        else:
            k, device = x_from(d), (dp, y_chip * 2 + core)
        return remote(piece(n, k), piece(n, k), agd_ss.at[n, d - 1], agd_rs.at[n, d - 1], device)

    def sib(n):
        block = n_buf.at[4 * core + lax.rem(z + n, 4)]
        return remote(block, block, sib_ss.at[n], sib_rs.at[n], sibling)

    def sib_in(n):
        block = n_buf.at[4 * other + lax.rem(z + n, 4)]
        return remote(block, block, sib_ss.at[n], sib_rs.at[n], sibling)

    def ag_first(n):
        j = lax.rem(z + n, 4)

        @pl.when(4 * core + j != z)
        def _():
            a2a_in(j).wait_recv()

        ag_y(n).start()
        for d in (1, 3, 2):
            ag_x(n, d).start()

    def ag_second(n):
        if n % 2 == 0:
            ag_y(n).wait_recv()
            for d in (1, 3, 2):
                ag_d(n, d).start()
        else:
            for d in (1, 3, 2):
                ag_x(n, d).wait_recv()
                ag_d(n, d).start()

    def ag_last(n):
        if n % 2 == 0:
            for d in (1, 3, 2):
                ag_x(n, d).wait_recv()
        else:
            ag_y(n).wait_recv()
        for d in (1, 3, 2):
            ag_d(n, d).wait_recv()
        sib(n).start()

    ag_first(2)
    for i in range(1, 2 * CHIPS):
        kv_copy(i).wait_recv()
    kv_sum = kv_buf[mp].astype(F32)
    for i in range(15):
        kv_sum = kv_sum + kv_recv[i].astype(F32)
    kv_all[z] = kv_sum.astype(BF16)
    kvg_buf[...] = jnp.transpose(kv_sum).astype(BF16)

    kz_start(1)

    def partial(half, j):
        first = pl.multiple_of((half * NCH + j) * FC, FC)
        w_copy(half, j).wait()
        total = dot_nt(g_buf[...], w_buf[pl.ds(first, FC), :])
        return total + dot(kvg_buf[...], wkv[:, pl.ds(first, FC)])

    def p_copy(j):
        return remote(p_send.at[j], p_recv.at[j], p_ss.at[j], p_rs.at[j], sibling)

    def sib_half(j):
        p_send[j] = partial(other, j).astype(BF16)
        p_copy(j).start()

    def rx_copy(j, d):
        n = 2 * (j // 3) + j % 3 - 1
        return remote(
            r_buf.at[j, lax.rem(x + d, 4)], rx_recv.at[n, d - 1],
            rx_ss.at[n, d - 1], rx_rs.at[n, d - 1], (dp, x_chip(d) * 2 + core),
        )

    def rxy_copy(j):
        n = 2 * (j // 3) + j % 3 - 1
        return remote(
            rx_send.at[n], rx_last.at[n], rxy_ss.at[n], rxy_rs.at[n], (dp, y_chip * 2 + core)
        )

    def ry_copy(j):
        return remote(
            r_buf.at[j, :, 1 - y_lo], ry_recv.at[j // 3], ry_ss.at[j // 3], ry_rs.at[j // 3],
            (dp, y_chip * 2 + core),
        )

    def ryx_copy(j, d):
        return remote(
            r_buf.at[j, lax.rem(x + d, 4), y_lo], ry_last.at[j // 3, d - 1],
            ryx_ss.at[j // 3, d - 1], ryx_rs.at[j // 3, d - 1], (dp, x_chip(d) * 2 + core),
        )

    def own_half(j):
        total = partial(core, j)
        p_copy(j).wait_recv()
        total = (total + p_recv[j].astype(F32)).astype(BF16)
        r_buf[j] = total.reshape(4, 2, CHIP_TOK, FC)
        if j % 3 == 0:
            ry_copy(j).start()
        else:
            for d in (1, 3, 2):
                rx_copy(j, d).start()

    def rs_second(j):
        if j % 3 == 0:
            ry_copy(j).wait_recv()
            for k in range(4):
                r_buf[j, k, y_lo] = (
                    r_buf[j, k, y_lo].astype(F32) + ry_recv[j // 3, k].astype(F32)
                ).astype(BF16)
            for d in (1, 3, 2):
                ryx_copy(j, d).start()
        else:
            n = 2 * (j // 3) + j % 3 - 1
            for d in range(1, 4):
                rx_copy(j, d).wait_recv()
            out = r_buf[j, x, 1 - y_lo].astype(F32)
            for d in range(3):
                out = out + rx_recv[n, d, 1 - y_lo].astype(F32)
            rx_send[n] = out.astype(BF16)
            rxy_copy(j).start()

    def rs_last(j):
        total = r_buf[j, x, y_lo].astype(F32)
        if j % 3 == 0:
            for d in range(1, 4):
                ryx_copy(j, d).wait_recv()
                total = total + ry_last[j // 3, d - 1].astype(F32)
        else:
            n = 2 * (j // 3) + j % 3 - 1
            for d in range(3):
                total = total + rx_recv[n, d, y_lo].astype(F32)
            rxy_copy(j).wait_recv()
            total = total + rx_last[n].astype(F32)
        low, high = total[0:24], total[24:48]
        pad = jnp.zeros((8, FC), F32)
        mine = jnp.where(core == 0, low, high)
        theirs = jnp.where(core == 0, high, low)
        f_buf[core, j] = jnp.concatenate([mine, pad], axis=0).astype(BF16)
        f_send[j] = jnp.concatenate([theirs, pad], axis=0).astype(BF16)
        f_copy(j).start()

    def f_copy(j):
        return remote(f_send.at[j], f_buf.at[core, j], f_ss.at[j], f_rs.at[j], sibling)

    def f_in(j):
        return remote(f_send.at[j], f_buf.at[other, j], f_ss.at[j], f_rs.at[j], sibling)

    def wgrad(za, zb, top_rows, with_kv):
        top = jnp.concatenate([gt_buf[za, top_rows, :], gt_buf[zb, top_rows, :]], axis=1)
        low = jnp.concatenate([kv_all[za], kv_all[zb]], axis=1)
        for c in range(3):
            cols = slice(TOK * c, TOK * c + TOK)
            rhs = jnp.concatenate([n_buf[za, :, cols], n_buf[zb, :, cols]], axis=0)
            acc[top_rows, cols] += dot(top, rhs)
            if with_kv:
                acc[QC:GC, cols] += dot(low, rhs)

    def wgrad_pair(n):
        wgrad(lax.rem(z + n, NZ), lax.rem(z + n + 4, NZ), slice(0, QC), True)

    def y_copy(r):
        cols = slice(256 * r, 256 * r + 256)
        return remote(y_send.at[:, cols], y_recv.at[:, cols], y_ss.at[r], y_rs.at[r], y_mate)

    def ykv_copy():
        return remote(ykv_send, ykv_recv, y_ss.at[2], y_rs.at[2], y_mate)

    def halves(rows):
        here = acc[rows, :]
        lower = here[:, 0:YW]
        upper = pltpu.roll(here, BLOCK, 1)[:, 0:YW]
        return jnp.where(y_hi == 0, lower, upper), jnp.where(y_hi == 0, upper, lower)

    acc[...] = jnp.zeros_like(acc)
    sib_half(0)
    ag_first(1)
    sib_half(1)
    sib_half(2)
    ag_first(3)
    sib_half(3)
    ring_wait(0, 1)
    ring_start(0, 2)
    sib_half(4)
    ag_first(0)
    sib_half(5)
    ag_second(2)
    ring_wait(1, 1)
    ring_start(1, 2)
    kz_wait(1)
    kz_start(2)
    ag_second(1)
    own_half(0)
    own_half(1)
    ag_second(3)
    ring_wait(0, 2)
    ring_start(0, 3)
    own_half(2)
    ag_second(0)
    ring_wait(1, 2)
    ring_start(1, 3)
    kz_wait(2)
    kz_start(3)
    own_half(3)
    ag_last(2)
    own_half(4)
    own_half(5)
    ag_last(1)
    ring_wait(0, 3)
    ring_start(0, 4)
    sib_in(2).wait_recv()
    wgrad_pair(2)
    ring_wait(1, 3)
    ring_start(1, 4)
    kz_wait(3)
    kz_start(4)
    rs_second(0)
    sib_in(1).wait_recv()
    wgrad_pair(1)
    ag_last(3)
    rs_second(1)
    ag_last(0)
    rs_second(2)
    sib_in(3).wait_recv()
    wgrad_pair(3)
    rs_second(3)
    sib_in(0).wait_recv()
    kz_wait(4)
    for r in range(2):
        rows = slice(256 * r, 256 * r + 256)
        ring_wait(r, 4)
        wgrad(z, lax.rem(z + 4, NZ), rows, r == 1)
        for q in range(2):
            quarter = slice(256 * r + 128 * q, 256 * r + 128 * q + 128)
            mine, theirs = halves(quarter)
            y_send[:, quarter] = jnp.transpose(theirs)[0:BLOCK].astype(BF16)
            own_buf[:, quarter] = jnp.transpose(mine)[0:BLOCK]
        y_copy(r).start()
    mine, theirs = halves(slice(QC, GC))
    own_kv[...] = mine
    ykv_send[...] = theirs.astype(BF16)
    ykv_copy().start()
    rs_second(4)
    rs_second(5)
    for j in range(NCH):
        rs_last(j)
    for j in range(NCH):
        f_in(j).wait_recv()
    for h in range(2):
        for j in range(NCH):
            out_in[:, HALF * h + FC * j : HALF * h + FC * j + FC] = f_buf[h, j].astype(F32)[
                0:24
            ].astype(BF16)
    for r in range(2):
        y_copy(r).wait_recv()
        cols = slice(256 * r, 256 * r + 256)
        out_wq[:, cols] = (own_buf[:, cols] + y_recv[:, cols].astype(F32)).astype(BF16)
    ykv_copy().wait_recv()
    total = (own_kv[...] + ykv_recv[...].astype(F32))[:, 0:BLOCK].astype(BF16)
    out_wk[...] = total[0:16]
    out_wv[...] = total[16:32]

    s_copy.wait_send()
    for j in range(4):
        @pl.when(4 * core + j != z)
        def _(j=j):
            a2a(j).wait_send()
    for i in range(1, 2 * CHIPS):
        kv_copy(i).wait_send()
    for n in range(4):
        ag_y(n).wait_send()
        for d in range(1, 4):
            ag_x(n, d).wait_send()
            ag_d(n, d).wait_send()
    for n in range(4):
        sib(n).wait_send()
    for s in range(1, 5):
        for copy in (*ring(0, s), *ring(1, s), *kz(s)):
            copy.wait_send()
    for j in range(NCH):
        p_copy(j).wait_send()
        f_copy(j).wait_send()
        if j % 3 == 0:
            ry_copy(j).wait_send()
            for d in range(1, 4):
                ryx_copy(j, d).wait_send()
        else:
            for d in range(1, 4):
                rx_copy(j, d).wait_send()
            rxy_copy(j).wait_send()
    for r in range(2):
        y_copy(r).wait_send()
    ykv_copy().wait_send()


def place(*refs):
    sems = refs[-1]
    copies = [pltpu.make_async_copy(refs[i], refs[4 + i], sems.at[i]) for i in range(4)]
    for copy in copies:
        copy.start()
    for copy in copies:
        copy.wait()


def shards(normed, w_query, w_key, w_value, query, key, value, grad_context):
    vmem = pl.BlockSpec(memory_space=pltpu.VMEM)
    dma = pltpu.SemaphoreType.DMA
    anywhere = pl.BlockSpec(memory_space=pl.ANY)
    results = (
        jax.ShapeDtypeStruct((24, FEAT), BF16),
        jax.ShapeDtypeStruct((BLOCK, QC), BF16),
        jax.ShapeDtypeStruct((16, BLOCK), BF16),
        jax.ShapeDtypeStruct((16, BLOCK), BF16),
    )
    grads = pl.pallas_call(
        kernel,
        out_shape=results,
        in_specs=[vmem, anywhere, vmem, vmem, vmem, vmem, vmem, vmem],
        out_specs=(vmem, vmem, vmem, vmem),
        scratch_shapes=[
            pltpu.VMEM((FEAT, QC), BF16),
            pltpu.VMEM((32, FEAT), BF16),
            pltpu.VMEM((2, 32, HALF), BF16),
            pltpu.VMEM((32, HALF), BF16),
            pltpu.VMEM((4, CHIP_TOK, ZF), BF16),
            pltpu.VMEM((NZ, TOK, ZF), BF16),
            pltpu.VMEM((NZ, QC, TOK), BF16),
            pltpu.VMEM((TOK, QC), BF16),
            pltpu.VMEM((16, 32, TOK), BF16),
            pltpu.VMEM((15, 32, TOK), BF16),
            pltpu.VMEM((NZ, 32, TOK), BF16),
            pltpu.VMEM((TOK, 32), BF16),
            pltpu.VMEM((NCH, TOK, FC), BF16),
            pltpu.VMEM((NCH, TOK, FC), BF16),
            pltpu.VMEM((NCH, 4, 2, CHIP_TOK, FC), BF16),
            pltpu.VMEM((4, 3, 2, CHIP_TOK, FC), BF16),
            pltpu.VMEM((4, CHIP_TOK, FC), BF16),
            pltpu.VMEM((4, CHIP_TOK, FC), BF16),
            pltpu.VMEM((2, 4, CHIP_TOK, FC), BF16),
            pltpu.VMEM((2, 3, CHIP_TOK, FC), BF16),
            pltpu.VMEM((NCH, 32, FC), BF16),
            pltpu.VMEM((2, NCH, 32, FC), BF16),
            pltpu.VMEM((GC, ZF), F32),
            pltpu.VMEM((BLOCK, QC), F32),
            pltpu.VMEM((32, YW), F32),
            pltpu.VMEM((BLOCK, QC), BF16),
            pltpu.VMEM((BLOCK, QC), BF16),
            pltpu.VMEM((32, YW), BF16),
            pltpu.VMEM((32, YW), BF16),
            dma((2 * NCH,)),
            dma((2,)),
            dma((4,)), dma((4,)),
            dma((4,)), dma((4,)),
            dma((4, 3)), dma((4, 3)),
            dma((4, 3)), dma((4, 3)),
            dma((4,)), dma((4,)),
            dma((15,)), dma((15,)),
            dma((2, 4)), dma((2, 4)),
            dma((2, 4)), dma((2, 4)), dma((2, 4)), dma((2, 4)),
            dma((NCH,)), dma((NCH,)),
            dma((4, 3)), dma((4, 3)), dma((4,)), dma((4,)),
            dma((2,)), dma((2,)), dma((2, 3)), dma((2, 3)),
            dma((NCH,)), dma((NCH,)),
            dma((3,)), dma((3,)),
        ],
        compiler_params=pltpu.CompilerParams(
            collective_id=0, has_side_effects=True, vmem_limit_bytes=60 * 1024 * 1024
        ),
    )(
        normed, w_query, jnp.transpose(w_key), jnp.transpose(w_value),
        query, key, value, grad_context,
    )
    grad_input, grad_wq, grad_wk, grad_wv = pl.pallas_call(
        place,
        out_shape=results,
        in_specs=[anywhere] * 4,
        out_specs=(anywhere,) * 4,
        scratch_shapes=[dma((4,))],
        compiler_params=pltpu.CompilerParams(vmem_limit_bytes=60 * 1024 * 1024),
    )(*grads)
    return grad_input, grad_wq, jnp.transpose(grad_wk), jnp.transpose(grad_wv)


def solution(mesh):
    placed = (
        P(("dp", "mp"), None),
        P(None, "mp"),
        P(None, "mp"),
        P(None, "mp"),
        P("dp", "mp"),
        P("dp", None),
        P("dp", None),
        P("dp", "mp"),
    )
    return jax.shard_map(
        shards,
        mesh=mesh,
        in_specs=placed,
        out_specs=(P(("dp", "mp"), None), P("dp", "mp"), P("dp", "mp"), P("dp", "mp")),
        check_vma=False,
    )
```

```python
import jax
import jax.numpy as jnp
from jax import lax
from jax.experimental import pallas as pl
from jax.experimental.pallas import tpu as pltpu
from jax.sharding import PartitionSpec as P

HEAD_DIM = 256
TOK = 384
NZ = 8
CHIPS = 8
CHIP_TOK = 48
FEAT = 9216
HALF = FEAT // 2
BLOCK = 576
ZF = 2 * BLOCK
QC = 512
GC = 544
FC = 768
NCH = HALF // FC
YW = 640
MESH = pl.DeviceIdType.MESH
F32 = jnp.float32
BF16 = jnp.bfloat16
NT = (((1,), (1,)), ((), ()))


def dot(a, b):
    return jnp.dot(a, b, preferred_element_type=F32)


def dot_nt(a, b):
    return lax.dot_general(a, b, NT, preferred_element_type=F32)


def kernel(
    normed, wq_hbm, wk_t, wv_t, query, key, value, grad,
    out_in, out_wq, out_wk, out_wv,
    w_buf, wkv, s_buf, s_recv, t_buf, n_buf, gt_buf, g_buf, kv_buf, kv_recv, kv_all, kvg_buf,
    p_send, p_recv, r_buf, rx_recv, rx_send, rx_last, ry_recv, ry_last, f_send, f_buf,
    acc, own_buf, own_kv, y_send, y_recv, ykv_send, ykv_recv,
    w_sems, s_sems, a2a_ss, a2a_rs, agy_ss, agy_rs, agx_ss, agx_rs, agd_ss, agd_rs,
    sib_ss, sib_rs, kv_ss, kv_rs, kz_ss, kz_rs,
    cw_ss, cw_rs, cc_ss, cc_rs, p_ss, p_rs,
    rx_ss, rx_rs, rxy_ss, rxy_rs, ry_ss, ry_rs, ryx_ss, ryx_rs, f_ss, f_rs, y_ss, y_rs,
):
    dp = lax.axis_index("dp")
    mp = lax.axis_index("mp")
    z = lax.rem(dp, NZ)
    y_hi = lax.div(dp, NZ)
    base = y_hi * NZ
    core = lax.rem(mp, 2)
    chip = lax.div(mp, 2)
    other = 1 - core
    sibling = (dp, chip * 2 + other)
    zhalf = lax.div(z, 4)
    x = lax.div(chip, 2)
    y_lo = lax.rem(chip, 2)
    y_chip = chip + 1 - 2 * y_lo
    y_mate = (lax.rem(dp + NZ, 2 * NZ), mp)

    def remote(src, dst, ss, rs, device):
        return pltpu.make_async_remote_copy(
            src_ref=src, dst_ref=dst, send_sem=ss, recv_sem=rs,
            device_id=device, device_id_type=MESH,
        )

    def w_copy(half, j):
        rows = pl.ds(pl.multiple_of((half * NCH + j) * FC, FC), FC)
        return pltpu.make_async_copy(
            wq_hbm.at[rows, :], w_buf.at[rows, :], w_sems.at[half * NCH + j]
        )

    for j in range(NCH):
        w_copy(other, j).start()
    for j in range(NCH):
        w_copy(core, j).start()

    barrier = pltpu.get_barrier_semaphore()
    for i in range(1, NZ):
        there = base + lax.rem(z + i, NZ)
        pl.semaphore_signal(barrier, inc=1, device_id=(there, mp), device_id_type=MESH)
        pl.semaphore_signal(
            barrier, inc=1, device_id=(there, chip * 2 + other), device_id_type=MESH
        )
    pl.semaphore_signal(barrier, inc=1, device_id=y_mate, device_id_type=MESH)
    for i in range(1, 2 * CHIPS):
        pl.semaphore_signal(
            barrier, inc=1, device_id=(dp, lax.rem(mp + i, 2 * CHIPS)), device_id_type=MESH
        )

    wkv[0:16, :] = wk_t[...]
    wkv[16:32, :] = wv_t[...]
    for h in range(2):
        for part in range(2):
            cols = normed[:, HALF * part + 2304 * h : HALF * part + 2304 * h + 2304].astype(F32)
            padded = jnp.concatenate([cols, jnp.zeros((8, 2304), F32)], axis=0)
            s_buf[h, :, 2304 * part : 2304 * part + 2304] = padded.astype(BF16)
    pl.semaphore_wait(barrier, 2 * (NZ - 1) + 1 + 2 * CHIPS - 1)
    s_copy = remote(s_buf.at[other], s_recv, s_sems.at[0], s_sems.at[1], sibling)
    s_copy.start()

    right = (base + lax.rem(z + 1, NZ), mp)
    left = (base + lax.rem(z + NZ - 1, NZ), mp)

    def ring_pair(h, s, slot_r, slot_l):
        first = HEAD_DIM * h
        if s < 4:
            src_r = gt_buf.at[slot_r, first : first + 256, :]
            src_l = gt_buf.at[slot_l, first : first + 256, :]
        else:
            src_r = gt_buf.at[slot_r, first : first + 128, :]
            src_l = gt_buf.at[slot_l, first + 128 : first + 256, :]
        return (
            remote(src_r, src_r, cw_ss.at[h, s - 1], cw_rs.at[h, s - 1], right),
            remote(src_l, src_l, cc_ss.at[h, s - 1], cc_rs.at[h, s - 1], left),
        )

    def ring(h, s):
        return ring_pair(h, s, lax.rem(z - (s - 1) + NZ, NZ), lax.rem(z + (s - 1), NZ))

    def ring_start(h, s):
        for copy in ring(h, s):
            copy.start()

    def ring_wait(h, s):
        for copy in ring_pair(h, s, lax.rem(z - s + NZ, NZ), lax.rem(z + s, NZ)):
            copy.wait_recv()

    def kz_pair(s, slot_r, slot_l):
        src_r, src_l = kv_all.at[slot_r], kv_all.at[slot_l]
        copies = [remote(src_r, src_r, kz_ss.at[0, s - 1], kz_rs.at[0, s - 1], right)]
        if s < 4:
            copies.append(remote(src_l, src_l, kz_ss.at[1, s - 1], kz_rs.at[1, s - 1], left))
        return copies

    def kz(s):
        return kz_pair(s, lax.rem(z - (s - 1) + NZ, NZ), lax.rem(z + (s - 1), NZ))

    def kz_start(s):
        for copy in kz(s):
            copy.start()

    def kz_wait(s):
        for copy in kz_pair(s, lax.rem(z - s + NZ, NZ), lax.rem(z + s, NZ)):
            copy.wait_recv()

    key_v = key[...]
    value_v = value[...]
    key_t = jnp.transpose(key_v.astype(F32)).astype(BF16)
    scale = HEAD_DIM ** (-0.5)
    causal = lax.broadcasted_iota(jnp.int32, (TOK, TOK), 0) <= lax.broadcasted_iota(
        jnp.int32, (TOK, TOK), 1
    )
    kp = None
    vp = None
    for h in range(2):
        q_h = query[:, HEAD_DIM * h : HEAD_DIM * h + HEAD_DIM]
        g_h = grad[:, HEAD_DIM * h : HEAD_DIM * h + HEAD_DIM]
        scores = jnp.where(causal, dot_nt(key_v, q_h) * scale, -jnp.inf)
        expo = jnp.exp(scores - jnp.max(scores, axis=0, keepdims=True))
        probs = expo * (1.0 / jnp.sum(expo, axis=0, keepdims=True))
        low = probs.astype(BF16)
        dprob = dot_nt(value_v, g_h)
        delta = jnp.sum(low.astype(F32) * dprob, axis=0, keepdims=True)
        dscore = (probs * (dprob - delta)).astype(BF16)
        kp_h = dot(dscore, q_h)
        vp_h = dot(low, g_h)
        kp = kp_h if kp is None else kp + kp_h
        vp = vp_h if vp is None else vp + vp_h
        gq = dot(key_t, dscore) * scale
        gt_buf[z, HEAD_DIM * h : HEAD_DIM * h + HEAD_DIM, :] = gq.astype(BF16)
        g_buf[:, HEAD_DIM * h : HEAD_DIM * h + HEAD_DIM] = jnp.transpose(gq).astype(BF16)
        if h == 0:
            s_copy.wait_recv()
            mine = s_buf[core].astype(F32)[:24]
            theirs = s_recv[...].astype(F32)[:24]
            first = jnp.where(core == 0, mine, theirs)
            second = jnp.where(core == 0, theirs, mine)
            both = jnp.concatenate([first, second], axis=0)
            for j in range(4):
                block = jnp.concatenate(
                    [
                        both[:, BLOCK * j : BLOCK * j + BLOCK],
                        both[:, 2304 + BLOCK * j : 2304 + BLOCK * j + BLOCK],
                    ],
                    axis=1,
                )
                t_buf[j] = block.astype(BF16)
            chip_rows = pl.ds(pl.multiple_of(chip * CHIP_TOK, 16), CHIP_TOK)

            def a2a(j):
                peer = 4 * core + j
                return remote(
                    t_buf.at[j], n_buf.at[z, chip_rows, :], a2a_ss.at[j], a2a_rs.at[lax.rem(z, 4)],
                    (base + peer, chip * 2 + zhalf),
                )

            def a2a_in(j):
                peer = 4 * core + j
                return remote(
                    t_buf.at[j], n_buf.at[peer, chip_rows, :], a2a_ss.at[j], a2a_rs.at[j],
                    (base + peer, chip * 2 + zhalf),
                )

            for j in range(4):
                @pl.when(4 * core + j != z)
                def _(j=j):
                    a2a(j).start()

                @pl.when(4 * core + j == z)
                def _(j=j):
                    n_buf[z, chip_rows, :] = t_buf[j]

    kp_t = jnp.transpose(kp * scale)
    vp_t = jnp.transpose(vp)
    kv_buf[:, 0:16, :] = kp_t.reshape(16, 16, TOK).astype(BF16)
    kv_buf[:, 16:32, :] = vp_t.reshape(16, 16, TOK).astype(BF16)

    def kv_copy(i):
        there = lax.rem(mp + i, 2 * CHIPS)
        return remote(
            kv_buf.at[there], kv_recv.at[i - 1], kv_ss.at[i - 1], kv_rs.at[i - 1], (dp, there)
        )

    for i in range(1, 2 * CHIPS):
        kv_copy(i).start()

    def n_rows(k):
        return pl.ds(pl.multiple_of(k * CHIP_TOK, 16), CHIP_TOK)

    def piece_z(o):
        n = jnp.where(core == zhalf, (0, 2, 1, 3)[o], (2, 1, 3, 0)[o])
        return lax.rem(z + n, 4)

    def piece(o, k):
        return n_buf.at[4 * core + piece_z(o), n_rows(k), :]

    def x_chip(d):
        return lax.rem(x + d, 4) * 2 + y_lo

    def x_from(d):
        return lax.rem(x + 4 - d, 4) * 2 + y_lo

    def ag_y(n):
        return remote(
            piece(n, chip), piece(n, chip), agy_ss.at[n], agy_rs.at[n], (dp, y_chip * 2 + core)
        )

    def ag_x(n, d):
        return remote(
            piece(n, chip), piece(n, chip), agx_ss.at[n, d - 1], agx_rs.at[n, d - 1],
            (dp, x_chip(d) * 2 + core),
        )

    def ag_d(n, d):
        if n % 2 == 0:
            k, device = y_chip, (dp, x_chip(d) * 2 + core)
        else:
            k, device = x_from(d), (dp, y_chip * 2 + core)
        return remote(piece(n, k), piece(n, k), agd_ss.at[n, d - 1], agd_rs.at[n, d - 1], device)

    def sib(n):
        block = n_buf.at[4 * core + piece_z(n)]
        return remote(block, block, sib_ss.at[n], sib_rs.at[n], sibling)

    def sib_in(n):
        o = jnp.where(core == zhalf, (3, 1, 0, 2)[n], (0, 2, 1, 3)[n])
        block = n_buf.at[4 * other + lax.rem(z + n, 4)]
        return remote(block, block, sib_ss.at[o], sib_rs.at[o], sibling)

    def ag_first(n):
        j = piece_z(n)

        @pl.when(4 * core + j != z)
        def _():
            a2a_in(j).wait_recv()

        ag_y(n).start()
        for d in (1, 3, 2):
            ag_x(n, d).start()

    def ag_second(n):
        if n % 2 == 0:
            ag_y(n).wait_recv()
            for d in (1, 3, 2):
                ag_d(n, d).start()
        else:
            for d in (1, 3, 2):
                ag_x(n, d).wait_recv()
                ag_d(n, d).start()

    def ag_last(n):
        if n % 2 == 0:
            for d in (1, 3, 2):
                ag_x(n, d).wait_recv()
        else:
            ag_y(n).wait_recv()
        for d in (1, 3, 2):
            ag_d(n, d).wait_recv()
        sib(n).start()

    ag_first(0)
    for i in range(1, 2 * CHIPS):
        kv_copy(i).wait_recv()
    kv_sum = kv_buf[mp].astype(F32)
    for i in range(15):
        kv_sum = kv_sum + kv_recv[i].astype(F32)
    kv_all[z] = kv_sum.astype(BF16)
    kvg_buf[...] = jnp.transpose(kv_sum).astype(BF16)

    def partial(half, j):
        first = pl.multiple_of((half * NCH + j) * FC, FC)
        w_copy(half, j).wait()
        total = dot_nt(g_buf[...], w_buf[pl.ds(first, FC), :])
        return total + dot(kvg_buf[...], wkv[:, pl.ds(first, FC)])

    def p_copy(j):
        return remote(p_send.at[j], p_recv.at[j], p_ss.at[j], p_rs.at[j], sibling)

    def sib_half(j):
        p_send[j] = partial(other, j).astype(BF16)
        p_copy(j).start()

    def rx_copy(j, d):
        n = 2 * (j // 3) + j % 3 - 1
        return remote(
            r_buf.at[j, lax.rem(x + d, 4)], rx_recv.at[n, d - 1],
            rx_ss.at[n, d - 1], rx_rs.at[n, d - 1], (dp, x_chip(d) * 2 + core),
        )

    def rxy_copy(j):
        n = 2 * (j // 3) + j % 3 - 1
        return remote(
            rx_send.at[n], rx_last.at[n], rxy_ss.at[n], rxy_rs.at[n], (dp, y_chip * 2 + core)
        )

    def ry_copy(j):
        return remote(
            r_buf.at[j, :, 1 - y_lo], ry_recv.at[j // 3], ry_ss.at[j // 3], ry_rs.at[j // 3],
            (dp, y_chip * 2 + core),
        )

    def ryx_copy(j, d):
        return remote(
            r_buf.at[j, lax.rem(x + d, 4), y_lo], ry_last.at[j // 3, d - 1],
            ryx_ss.at[j // 3, d - 1], ryx_rs.at[j // 3, d - 1], (dp, x_chip(d) * 2 + core),
        )

    def own_half(j):
        total = partial(core, j)
        p_copy(j).wait_recv()
        total = (total + p_recv[j].astype(F32)).astype(BF16)
        r_buf[j] = total.reshape(4, 2, CHIP_TOK, FC)
        if j % 3 == 0:
            ry_copy(j).start()
        else:
            for d in (1, 3, 2):
                rx_copy(j, d).start()

    def rs_second(j):
        if j % 3 == 0:
            ry_copy(j).wait_recv()
            for k in range(4):
                r_buf[j, k, y_lo] = (
                    r_buf[j, k, y_lo].astype(F32) + ry_recv[j // 3, k].astype(F32)
                ).astype(BF16)
            for d in (1, 3, 2):
                ryx_copy(j, d).start()
        else:
            n = 2 * (j // 3) + j % 3 - 1
            for d in range(1, 4):
                rx_copy(j, d).wait_recv()
            out = r_buf[j, x, 1 - y_lo].astype(F32)
            for d in range(3):
                out = out + rx_recv[n, d, 1 - y_lo].astype(F32)
            rx_send[n] = out.astype(BF16)
            rxy_copy(j).start()

    def rs_last(j):
        total = r_buf[j, x, y_lo].astype(F32)
        if j % 3 == 0:
            for d in range(1, 4):
                ryx_copy(j, d).wait_recv()
                total = total + ry_last[j // 3, d - 1].astype(F32)
        else:
            n = 2 * (j // 3) + j % 3 - 1
            for d in range(3):
                total = total + rx_recv[n, d, y_lo].astype(F32)
            rxy_copy(j).wait_recv()
            total = total + rx_last[n].astype(F32)
        low, high = total[0:24], total[24:48]
        pad = jnp.zeros((8, FC), F32)
        mine = jnp.where(core == 0, low, high)
        theirs = jnp.where(core == 0, high, low)
        f_buf[core, j] = jnp.concatenate([mine, pad], axis=0).astype(BF16)
        f_send[j] = jnp.concatenate([theirs, pad], axis=0).astype(BF16)
        f_copy(j).start()

    def f_copy(j):
        return remote(f_send.at[j], f_buf.at[core, j], f_ss.at[j], f_rs.at[j], sibling)

    def f_in(j):
        return remote(f_send.at[j], f_buf.at[other, j], f_ss.at[j], f_rs.at[j], sibling)

    def wgrad(za, zb, top_rows, with_kv):
        top = jnp.concatenate([gt_buf[za, top_rows, :], gt_buf[zb, top_rows, :]], axis=1)
        low = jnp.concatenate([kv_all[za], kv_all[zb]], axis=1)
        for c in range(3):
            cols = slice(TOK * c, TOK * c + TOK)
            rhs = jnp.concatenate([n_buf[za, :, cols], n_buf[zb, :, cols]], axis=0)
            acc[top_rows, cols] += dot(top, rhs)
            if with_kv:
                acc[QC:GC, cols] += dot(low, rhs)

    def wgrad_pair(n):
        wgrad(lax.rem(z + n, NZ), lax.rem(z + n + 4, NZ), slice(0, QC), True)

    def y_copy(r):
        cols = slice(256 * r, 256 * r + 256)
        return remote(y_send.at[:, cols], y_recv.at[:, cols], y_ss.at[r], y_rs.at[r], y_mate)

    def ykv_copy():
        return remote(ykv_send, ykv_recv, y_ss.at[2], y_rs.at[2], y_mate)

    def halves(rows):
        here = acc[rows, :]
        lower = here[:, 0:YW]
        upper = pltpu.roll(here, BLOCK, 1)[:, 0:YW]
        return jnp.where(y_hi == 0, lower, upper), jnp.where(y_hi == 0, upper, lower)

    acc[...] = jnp.zeros_like(acc)
    sib_half(0)
    sib_half(1)
    ag_first(1)
    ring_start(0, 1)
    ag_first(2)
    sib_half(2)
    ag_first(3)
    ring_start(1, 1)
    kz_start(1)
    sib_half(3)
    sib_half(4)
    sib_half(5)
    ag_second(0)
    ag_second(1)
    ring_wait(0, 1)
    ring_start(0, 2)
    own_half(0)
    own_half(1)
    ag_second(2)
    ring_wait(1, 1)
    ring_start(1, 2)
    kz_wait(1)
    kz_start(2)
    ag_second(3)
    own_half(2)
    ring_wait(0, 2)
    ring_start(0, 3)
    own_half(3)
    own_half(4)
    ring_wait(1, 2)
    ring_start(1, 3)
    kz_wait(2)
    kz_start(3)
    own_half(5)
    ag_last(0)
    ag_last(1)
    ring_wait(0, 3)
    ring_start(0, 4)
    rs_second(0)
    ag_last(2)
    ring_wait(1, 3)
    ring_start(1, 4)
    kz_wait(3)
    kz_start(4)
    ag_last(3)
    rs_second(1)
    sib_in(2).wait_recv()
    wgrad_pair(2)
    sib_in(1).wait_recv()
    wgrad_pair(1)
    rs_second(2)
    sib_in(3).wait_recv()
    wgrad_pair(3)
    rs_second(3)
    sib_in(0).wait_recv()
    kz_wait(4)
    for r in range(2):
        rows = slice(256 * r, 256 * r + 256)
        ring_wait(r, 4)
        wgrad(z, lax.rem(z + 4, NZ), rows, r == 1)
        for q in range(2):
            quarter = slice(256 * r + 128 * q, 256 * r + 128 * q + 128)
            mine, theirs = halves(quarter)
            y_send[:, quarter] = jnp.transpose(theirs)[0:BLOCK].astype(BF16)
            own_buf[:, quarter] = jnp.transpose(mine)[0:BLOCK]
        y_copy(r).start()
    mine, theirs = halves(slice(QC, GC))
    own_kv[...] = mine
    ykv_send[...] = theirs.astype(BF16)
    ykv_copy().start()
    rs_second(4)
    rs_second(5)
    for j in range(NCH):
        rs_last(j)
    for j in range(NCH):
        f_in(j).wait_recv()
    for h in range(2):
        for j in range(NCH):
            out_in[:, HALF * h + FC * j : HALF * h + FC * j + FC] = f_buf[h, j].astype(F32)[
                0:24
            ].astype(BF16)
    for r in range(2):
        y_copy(r).wait_recv()
        cols = slice(256 * r, 256 * r + 256)
        out_wq[:, cols] = (own_buf[:, cols] + y_recv[:, cols].astype(F32)).astype(BF16)
    ykv_copy().wait_recv()
    total = (own_kv[...] + ykv_recv[...].astype(F32))[:, 0:BLOCK].astype(BF16)
    out_wk[...] = total[0:16]
    out_wv[...] = total[16:32]

    s_copy.wait_send()
    for j in range(4):
        @pl.when(4 * core + j != z)
        def _(j=j):
            a2a(j).wait_send()
    for i in range(1, 2 * CHIPS):
        kv_copy(i).wait_send()
    for n in range(4):
        ag_y(n).wait_send()
        for d in range(1, 4):
            ag_x(n, d).wait_send()
            ag_d(n, d).wait_send()
    for n in range(4):
        sib(n).wait_send()
    for s in range(1, 5):
        for copy in (*ring(0, s), *ring(1, s), *kz(s)):
            copy.wait_send()
    for j in range(NCH):
        p_copy(j).wait_send()
        f_copy(j).wait_send()
        if j % 3 == 0:
            ry_copy(j).wait_send()
            for d in range(1, 4):
                ryx_copy(j, d).wait_send()
        else:
            for d in range(1, 4):
                rx_copy(j, d).wait_send()
            rxy_copy(j).wait_send()
    for r in range(2):
        y_copy(r).wait_send()
    ykv_copy().wait_send()


def place(*refs):
    for i in range(4):
        refs[4 + i][...] = refs[i][...]


def shards(normed, w_query, w_key, w_value, query, key, value, grad_context):
    vmem = pl.BlockSpec(memory_space=pltpu.VMEM)
    dma = pltpu.SemaphoreType.DMA
    anywhere = pl.BlockSpec(memory_space=pl.ANY)
    results = (
        jax.ShapeDtypeStruct((24, FEAT), BF16),
        jax.ShapeDtypeStruct((BLOCK, QC), BF16),
        jax.ShapeDtypeStruct((16, BLOCK), BF16),
        jax.ShapeDtypeStruct((16, BLOCK), BF16),
    )
    grads = pl.pallas_call(
        kernel,
        out_shape=results,
        in_specs=[vmem, anywhere, vmem, vmem, vmem, vmem, vmem, vmem],
        out_specs=(vmem, vmem, vmem, vmem),
        scratch_shapes=[
            pltpu.VMEM((FEAT, QC), BF16),
            pltpu.VMEM((32, FEAT), BF16),
            pltpu.VMEM((2, 32, HALF), BF16),
            pltpu.VMEM((32, HALF), BF16),
            pltpu.VMEM((4, CHIP_TOK, ZF), BF16),
            pltpu.VMEM((NZ, TOK, ZF), BF16),
            pltpu.VMEM((NZ, QC, TOK), BF16),
            pltpu.VMEM((TOK, QC), BF16),
            pltpu.VMEM((16, 32, TOK), BF16),
            pltpu.VMEM((15, 32, TOK), BF16),
            pltpu.VMEM((NZ, 32, TOK), BF16),
            pltpu.VMEM((TOK, 32), BF16),
            pltpu.VMEM((NCH, TOK, FC), BF16),
            pltpu.VMEM((NCH, TOK, FC), BF16),
            pltpu.VMEM((NCH, 4, 2, CHIP_TOK, FC), BF16),
            pltpu.VMEM((4, 3, 2, CHIP_TOK, FC), BF16),
            pltpu.VMEM((4, CHIP_TOK, FC), BF16),
            pltpu.VMEM((4, CHIP_TOK, FC), BF16),
            pltpu.VMEM((2, 4, CHIP_TOK, FC), BF16),
            pltpu.VMEM((2, 3, CHIP_TOK, FC), BF16),
            pltpu.VMEM((NCH, 32, FC), BF16),
            pltpu.VMEM((2, NCH, 32, FC), BF16),
            pltpu.VMEM((GC, ZF), F32),
            pltpu.VMEM((BLOCK, QC), F32),
            pltpu.VMEM((32, YW), F32),
            pltpu.VMEM((BLOCK, QC), BF16),
            pltpu.VMEM((BLOCK, QC), BF16),
            pltpu.VMEM((32, YW), BF16),
            pltpu.VMEM((32, YW), BF16),
            dma((2 * NCH,)),
            dma((2,)),
            dma((4,)), dma((4,)),
            dma((4,)), dma((4,)),
            dma((4, 3)), dma((4, 3)),
            dma((4, 3)), dma((4, 3)),
            dma((4,)), dma((4,)),
            dma((15,)), dma((15,)),
            dma((2, 4)), dma((2, 4)),
            dma((2, 4)), dma((2, 4)), dma((2, 4)), dma((2, 4)),
            dma((NCH,)), dma((NCH,)),
            dma((4, 3)), dma((4, 3)), dma((4,)), dma((4,)),
            dma((2,)), dma((2,)), dma((2, 3)), dma((2, 3)),
            dma((NCH,)), dma((NCH,)),
            dma((3,)), dma((3,)),
        ],
        compiler_params=pltpu.CompilerParams(
            collective_id=0, has_side_effects=True, vmem_limit_bytes=60 * 1024 * 1024
        ),
    )(
        normed, w_query, jnp.transpose(w_key), jnp.transpose(w_value),
        query, key, value, grad_context,
    )
    grad_input, grad_wq, grad_wk, grad_wv = pl.pallas_call(
        place,
        out_shape=results,
        in_specs=[vmem] * 4,
        out_specs=(vmem,) * 4,
    )(*grads)
    return grad_input, grad_wq, jnp.transpose(grad_wk), jnp.transpose(grad_wv)


def solution(mesh):
    placed = (
        P(("dp", "mp"), None),
        P(None, "mp"),
        P(None, "mp"),
        P(None, "mp"),
        P("dp", "mp"),
        P("dp", None),
        P("dp", None),
        P("dp", "mp"),
    )
    return jax.shard_map(
        shards,
        mesh=mesh,
        in_specs=placed,
        out_specs=(P(("dp", "mp"), None), P("dp", "mp"), P("dp", "mp"), P("dp", "mp")),
        check_vma=False,
    )
```

```python
import jax
import jax.numpy as jnp
from jax import lax
from jax.experimental import pallas as pl
from jax.experimental.pallas import tpu as pltpu
from jax.sharding import PartitionSpec as P

HEAD_DIM = 256
TOK = 384
NZ = 8
CHIPS = 8
CHIP_TOK = 48
FEAT = 9216
HALF = FEAT // 2
BLOCK = 576
ZF = 2 * BLOCK
QC = 512
GC = 544
FC = 768
NCH = HALF // FC
YW = 640
MESH = pl.DeviceIdType.MESH
F32 = jnp.float32
BF16 = jnp.bfloat16
NT = (((1,), (1,)), ((), ()))


def dot(a, b):
    return jnp.dot(a, b, preferred_element_type=F32)


def dot_nt(a, b):
    return lax.dot_general(a, b, NT, preferred_element_type=F32)


def kernel(
    normed_hbm, wq_hbm, wk_hbm, wv_hbm, query_hbm, key_hbm, value_hbm, grad_hbm,
    out_in, out_wq, out_wk, out_wv,
    normed, wk_t, wv_t, query, key, value, grad,
    w_buf, wkv, wkv_sib, s_buf, s_recv, t_buf, n_buf, gt_buf, g_buf, kv_buf, kv_sib, kv_recv, kv_all, kvs_recv, kvg_buf,
    p_send, p_recv, r_buf, rx_mid, rx_recv, rx_send, rx_last, ry_recv, ry_mid, ry_last, f_send, f_buf,
    acc, own_buf, own_kv, y_send, y_recv, ykv_send, ykv_recv,
    in_sems, w_sems, s_sems, a2a_ss, a2a_rs, agy_ss, agy_rs, agx_ss, agx_rs, agd_ss, agd_rs,
    sib_ss, sib_rs, kv_ss, kv_rs, kz_ss, kz_rs,
    cw_ss, cw_rs, cc_ss, cc_rs, p_ss, p_rs,
    rx_ss, rx_rs, rxy_ss, rxy_rs, ry_ss, ry_rs, ryx_ss, ryx_rs, f_ss, f_rs, y_ss, y_rs,
):
    dp = lax.axis_index("dp")
    mp = lax.axis_index("mp")
    z = lax.rem(dp, NZ)
    y_hi = lax.div(dp, NZ)
    base = y_hi * NZ
    core = lax.rem(mp, 2)
    chip = lax.div(mp, 2)
    other = 1 - core
    sibling = (dp, chip * 2 + other)
    zhalf = lax.div(z, 4)
    x = lax.div(chip, 2)
    y_lo = lax.rem(chip, 2)
    y_chip = chip + 1 - 2 * y_lo
    y_mate = (lax.rem(dp + NZ, 2 * NZ), mp)

    def remote(src, dst, ss, rs, device):
        return pltpu.make_async_remote_copy(
            src_ref=src, dst_ref=dst, send_sem=ss, recv_sem=rs,
            device_id=device, device_id_type=MESH,
        )

    def w_copy(half, j):
        rows = pl.ds(pl.multiple_of((half * NCH + j) * FC, FC), FC)
        return pltpu.make_async_copy(
            wq_hbm.at[rows, :], w_buf.at[rows, :], w_sems.at[half * NCH + j]
        )


    inputs = (
        (normed_hbm, normed), (query_hbm, query), (key_hbm, key), (grad_hbm, grad),
        (value_hbm, value), (wk_hbm, wk_t), (wv_hbm, wv_t),
    )
    loads = [
        pltpu.make_async_copy(there, here, in_sems.at[i])
        for i, (there, here) in enumerate(inputs)
    ]
    for load in loads:
        load.start()

    barrier = pltpu.get_barrier_semaphore()
    for i in range(1, NZ):
        there = base + lax.rem(z + i, NZ)
        pl.semaphore_signal(barrier, inc=1, device_id=(there, mp), device_id_type=MESH)
        pl.semaphore_signal(
            barrier, inc=1, device_id=(there, chip * 2 + other), device_id_type=MESH
        )
    pl.semaphore_signal(barrier, inc=1, device_id=y_mate, device_id_type=MESH)
    for i in range(1, 2 * CHIPS):
        pl.semaphore_signal(
            barrier, inc=1, device_id=(dp, lax.rem(mp + i, 2 * CHIPS)), device_id_type=MESH
        )

    for j in range(NCH):
        w_copy(other, j).start()
    for j in range(NCH):
        w_copy(core, j).start()
    loads[0].wait()
    for h in range(2):
        for part in range(2):
            cols = normed[:, HALF * part + 2304 * h : HALF * part + 2304 * h + 2304].astype(F32)
            padded = jnp.concatenate([cols, jnp.zeros((8, 2304), F32)], axis=0)
            s_buf[h, :, 2304 * part : 2304 * part + 2304] = padded.astype(BF16)
    pl.semaphore_wait(barrier, 2 * (NZ - 1) + 1 + 2 * CHIPS - 1)
    s_copy = remote(s_buf.at[other], s_recv, s_sems.at[0], s_sems.at[1], sibling)
    s_copy.start()
    loads[5].wait()
    loads[6].wait()
    for h in range(2):
        wkv[h, 0:16, :] = wk_t[:, HALF * h : HALF * h + HALF]
        wkv[h, 16:32, :] = wv_t[:, HALF * h : HALF * h + HALF]
    wkv_copy = remote(wkv.at[other], wkv_sib, s_sems.at[2], s_sems.at[3], sibling)
    wkv_copy.start()

    right = (base + lax.rem(z + 1, NZ), mp)
    left = (base + lax.rem(z + NZ - 1, NZ), mp)

    def ring_pair(h, s, slot_r, slot_l):
        first = HEAD_DIM * h
        if s < 4:
            src_r = gt_buf.at[slot_r, first : first + 256, :]
            src_l = gt_buf.at[slot_l, first : first + 256, :]
        else:
            src_r = gt_buf.at[slot_r, first : first + 128, :]
            src_l = gt_buf.at[slot_l, first + 128 : first + 256, :]
        return (
            remote(src_r, src_r, cw_ss.at[h, s - 1], cw_rs.at[h, s - 1], right),
            remote(src_l, src_l, cc_ss.at[h, s - 1], cc_rs.at[h, s - 1], left),
        )

    def ring(h, s):
        return ring_pair(h, s, lax.rem(z - (s - 1) + NZ, NZ), lax.rem(z + (s - 1), NZ))

    def ring_start(h, s):
        for copy in ring(h, s):
            copy.start()

    def ring_wait(h, s):
        for copy in ring_pair(h, s, lax.rem(z - s + NZ, NZ), lax.rem(z + s, NZ)):
            copy.wait_recv()

    def kz_pair(s, slot_r, slot_l):
        src_r, src_l = kv_all.at[slot_r], kv_all.at[slot_l]
        copies = [remote(src_r, src_r, kz_ss.at[0, s - 1], kz_rs.at[0, s - 1], right)]
        if s < 4:
            copies.append(remote(src_l, src_l, kz_ss.at[1, s - 1], kz_rs.at[1, s - 1], left))
        return copies

    def kz(s):
        return kz_pair(s, lax.rem(z - (s - 1) + NZ, NZ), lax.rem(z + (s - 1), NZ))

    def kz_start(s):
        for copy in kz(s):
            copy.start()

    def kz_wait(s):
        for copy in kz_pair(s, lax.rem(z - s + NZ, NZ), lax.rem(z + s, NZ)):
            copy.wait_recv()

    for i in range(1, 5):
        loads[i].wait()
    key_v = key[...]
    value_v = value[...]
    key_t = jnp.transpose(key_v.astype(F32)).astype(BF16)
    scale = HEAD_DIM ** (-0.5)
    causal = lax.broadcasted_iota(jnp.int32, (TOK, TOK), 0) <= lax.broadcasted_iota(
        jnp.int32, (TOK, TOK), 1
    )
    kp = None
    vp = None
    for h in range(2):
        q_h = query[:, HEAD_DIM * h : HEAD_DIM * h + HEAD_DIM]
        g_h = grad[:, HEAD_DIM * h : HEAD_DIM * h + HEAD_DIM]
        scores = jnp.where(causal, dot_nt(key_v, q_h) * scale, -jnp.inf)
        expo = jnp.exp(scores - jnp.max(scores, axis=0, keepdims=True))
        probs = expo * (1.0 / jnp.sum(expo, axis=0, keepdims=True))
        low = probs.astype(BF16)
        dprob = dot_nt(value_v, g_h)
        delta = jnp.sum(low.astype(F32) * dprob, axis=0, keepdims=True)
        dscore = (probs * (dprob - delta)).astype(BF16)
        kp_h = dot(dscore, q_h)
        vp_h = dot(low, g_h)
        kp = kp_h if kp is None else kp + kp_h
        vp = vp_h if vp is None else vp + vp_h
        gq = dot(key_t, dscore) * scale
        gt_buf[z, HEAD_DIM * h : HEAD_DIM * h + HEAD_DIM, :] = gq.astype(BF16)
        g_buf[:, HEAD_DIM * h : HEAD_DIM * h + HEAD_DIM] = jnp.transpose(gq).astype(BF16)
        if h == 0:
            s_copy.wait_recv()
            mine = s_buf[core].astype(F32)[:24]
            theirs = s_recv[...].astype(F32)[:24]
            first = jnp.where(core == 0, mine, theirs)
            second = jnp.where(core == 0, theirs, mine)
            both = jnp.concatenate([first, second], axis=0)
            for j in range(4):
                block = jnp.concatenate(
                    [
                        both[:, BLOCK * j : BLOCK * j + BLOCK],
                        both[:, 2304 + BLOCK * j : 2304 + BLOCK * j + BLOCK],
                    ],
                    axis=1,
                )
                t_buf[j] = block.astype(BF16)
            chip_rows = pl.ds(pl.multiple_of(chip * CHIP_TOK, 16), CHIP_TOK)

            def a2a(j):
                peer = 4 * core + j
                return remote(
                    t_buf.at[j], n_buf.at[z, chip_rows, :], a2a_ss.at[j], a2a_rs.at[lax.rem(z, 4)],
                    (base + peer, chip * 2 + zhalf),
                )

            def a2a_in(j):
                peer = 4 * core + j
                return remote(
                    t_buf.at[j], n_buf.at[peer, chip_rows, :], a2a_ss.at[j], a2a_rs.at[j],
                    (base + peer, chip * 2 + zhalf),
                )

            for j in range(4):
                @pl.when(4 * core + j != z)
                def _(j=j):
                    a2a(j).start()

                @pl.when(4 * core + j == z)
                def _(j=j):
                    n_buf[z, chip_rows, :] = t_buf[j]

    kp_t = jnp.transpose(kp * scale)
    vp_t = jnp.transpose(vp)
    for c in range(2):
        kv_buf[c, :, 0:16, :] = kp_t.reshape(CHIPS, 2, 16, TOK)[:, c].astype(BF16)
        kv_buf[c, :, 16:32, :] = vp_t.reshape(CHIPS, 2, 16, TOK)[:, c].astype(BF16)
    kv_pair = remote(kv_buf.at[other], kv_sib, kv_ss.at[7], kv_rs.at[7], sibling)
    kv_pair.start()

    def kv_copy(i):
        there = lax.rem(chip + i, CHIPS)
        return remote(
            kv_buf.at[core, there], kv_recv.at[i - 1], kv_ss.at[i - 1], kv_rs.at[i - 1],
            (dp, there * 2 + core),
        )

    def n_rows(k):
        return pl.ds(pl.multiple_of(k * CHIP_TOK, 16), CHIP_TOK)

    def piece_z(o):
        n = jnp.where(core == zhalf, (0, 2, 1, 3)[o], (2, 1, 3, 0)[o])
        return lax.rem(z + n, 4)

    def piece(o, k):
        return n_buf.at[4 * core + piece_z(o), n_rows(k), :]

    def x_chip(d):
        return lax.rem(x + d, 4) * 2 + y_lo

    def x_from(d):
        return lax.rem(x + 4 - d, 4) * 2 + y_lo

    def ag_y(n):
        return remote(
            piece(n, chip), piece(n, chip), agy_ss.at[n], agy_rs.at[n], (dp, y_chip * 2 + core)
        )

    def ag_x(n, d):
        k, to = (x_from(1), 1) if d == 2 else (chip, d)
        return remote(
            piece(n, k), piece(n, k), agx_ss.at[n, d - 1], agx_rs.at[n, d - 1],
            (dp, x_chip(to) * 2 + core),
        )

    def ag_d(n, d):
        if d == 2:
            k, there = x_from(3) + 1 - 2 * y_lo, x_chip(3)
        else:
            k, there = y_chip, x_chip(d)
        return remote(
            piece(n, k), piece(n, k), agd_ss.at[n, d - 1], agd_rs.at[n, d - 1],
            (dp, there * 2 + core),
        )

    def sib(n):
        block = n_buf.at[4 * core + piece_z(n)]
        return remote(block, block, sib_ss.at[n], sib_rs.at[n], sibling)

    def sib_in(n):
        o = jnp.where(core == zhalf, (3, 1, 0, 2)[n], (0, 2, 1, 3)[n])
        block = n_buf.at[4 * other + lax.rem(z + n, 4)]
        return remote(block, block, sib_ss.at[o], sib_rs.at[o], sibling)

    def ag_send(n):
        ag_y(n).start()
        ag_x(n, 1).start()
        ag_x(n, 3).start()

    def ag_first(n):
        j = piece_z(n)
        if n == 0:
            @pl.when(core != zhalf)
            def _():
                a2a_in(j).wait_recv()
                ag_send(0)
        else:
            @pl.when(4 * core + j != z)
            def _():
                a2a_in(j).wait_recv()

            ag_send(n)

    def ag_second(n):
        ag_x(n, 1).wait_recv()
        ag_x(n, 2).start()
        ag_y(n).wait_recv()
        ag_d(n, 1).start()
        ag_d(n, 3).start()

    def ag_third(n):
        ag_d(n, 3).wait_recv()
        ag_d(n, 2).start()

    def ag_last(n):
        ag_x(n, 3).wait_recv()
        ag_x(n, 2).wait_recv()
        ag_d(n, 1).wait_recv()
        ag_d(n, 2).wait_recv()
        sib(n).start()

    def partial(half, j):
        first = pl.multiple_of((half * NCH + j) * FC, FC)
        w_copy(half, j).wait()
        return dot_nt(g_buf[...], w_buf[pl.ds(first, FC), :])

    def p_copy(j):
        return remote(p_send.at[j], p_recv.at[j], p_ss.at[j], p_rs.at[j], sibling)

    def sib_half(j):
        p_send[j] = partial(other, j).astype(BF16)
        p_copy(j).start()

    def index(j):
        return j if j < 4 else j - 4

    def x_way(j):
        return 1 if index(j) % 2 == 0 else 3

    def x_block(j, d):
        there = lax.rem(x + d, 4)
        return r_buf.at[j, there] if j >= 4 else r_buf.at[j, there, y_lo]

    def x_copy(j, kind):
        way = x_way(j)
        d, to = ((2, way), (way, way), (4 - way, 4 - way))[kind]
        if j >= 4:
            n, ss, rs, mid, last = index(j), rx_ss, rx_rs, rx_mid, rx_recv
        else:
            n, ss, rs, mid, last = index(j), ryx_ss, ryx_rs, ry_mid, ry_last
        dst = mid.at[n] if kind == 0 else last.at[n, kind - 1]
        return remote(
            x_block(j, d), dst, ss.at[n, kind], rs.at[n, kind], (dp, x_chip(to) * 2 + core)
        )

    def x_first(j):
        x_copy(j, 0).start()
        x_copy(j, 2).start()

    def x_mid(j):
        x_copy(j, 0).wait_recv()
        there = lax.rem(x + x_way(j), 4)
        if j >= 4:
            for k in range(2):
                r_buf[j, there, k] = (
                    r_buf[j, there, k].astype(F32) + rx_mid[index(j), k].astype(F32)
                ).astype(BF16)
        else:
            r_buf[j, there, y_lo] = (
                r_buf[j, there, y_lo].astype(F32) + ry_mid[index(j)].astype(F32)
            ).astype(BF16)
        x_copy(j, 1).start()

    def rxy_copy(j):
        n = index(j)
        return remote(
            rx_send.at[n], rx_last.at[n], rxy_ss.at[n], rxy_rs.at[n], (dp, y_chip * 2 + core)
        )

    def ry_copy(j):
        return remote(
            r_buf.at[j, :, 1 - y_lo], ry_recv.at[index(j)], ry_ss.at[index(j)], ry_rs.at[index(j)],
            (dp, y_chip * 2 + core),
        )

    def own_half(j):
        cols = slice(FC * j, FC * j + FC)
        both = jnp.concatenate([wkv[core, :, cols], wkv_sib[:, cols]], axis=0)
        total = partial(core, j) + dot(kvg_buf[...], both)
        p_copy(j).wait_recv()
        total = (total + p_recv[j].astype(F32)).astype(BF16)
        r_buf[j] = total.reshape(4, 2, CHIP_TOK, FC)

    def own_send(j):
        if j < 4:
            ry_copy(j).start()
        else:
            x_first(j)

    def rs_second(j):
        if j < 4:
            ry_copy(j).wait_recv()
            for k in range(4):
                r_buf[j, k, y_lo] = (
                    r_buf[j, k, y_lo].astype(F32) + ry_recv[index(j), k].astype(F32)
                ).astype(BF16)
            x_first(j)
        else:
            x_mid(j)

    def rs_third(j):
        if j < 4:
            x_mid(j)
        else:
            n = index(j)
            x_copy(j, 1).wait_recv()
            x_copy(j, 2).wait_recv()
            out = r_buf[j, x, 1 - y_lo].astype(F32)
            for d in range(2):
                out = out + rx_recv[n, d, 1 - y_lo].astype(F32)
            rx_send[n] = out.astype(BF16)
            rxy_copy(j).start()

    def rs_last(j):
        total = r_buf[j, x, y_lo].astype(F32)
        if j < 4:
            x_copy(j, 1).wait_recv()
            x_copy(j, 2).wait_recv()
            for d in range(2):
                total = total + ry_last[index(j), d].astype(F32)
        else:
            n = index(j)
            for d in range(2):
                total = total + rx_recv[n, d, y_lo].astype(F32)
            rxy_copy(j).wait_recv()
            total = total + rx_last[n].astype(F32)
        low, high = total[0:24], total[24:48]
        pad = jnp.zeros((8, FC), F32)
        mine = jnp.where(core == 0, low, high)
        theirs = jnp.where(core == 0, high, low)
        f_buf[core, j] = jnp.concatenate([mine, pad], axis=0).astype(BF16)
        f_send[j] = jnp.concatenate([theirs, pad], axis=0).astype(BF16)
        f_copy(j).start()

    def f_copy(j):
        return remote(f_send.at[j], f_buf.at[core, j], f_ss.at[j], f_rs.at[j], sibling)

    def f_in(j):
        return remote(f_send.at[j], f_buf.at[other, j], f_ss.at[j], f_rs.at[j], sibling)

    def wgrad(za, zb, top_rows, with_kv):
        top = jnp.concatenate([gt_buf[za, top_rows, :], gt_buf[zb, top_rows, :]], axis=1)
        low = jnp.concatenate([kv_all[za], kv_all[zb]], axis=1)
        for c in range(3):
            cols = slice(TOK * c, TOK * c + TOK)
            rhs = jnp.concatenate([n_buf[za, :, cols], n_buf[zb, :, cols]], axis=0)
            acc[top_rows, cols] += dot(top, rhs)
            if with_kv:
                acc[QC:GC, cols] += dot(low, rhs)

    def wgrad_pair(n):
        wgrad(lax.rem(z + n, NZ), lax.rem(z + n + 4, NZ), slice(0, QC), True)

    def y_copy(r):
        cols = slice(256 * r, 256 * r + 256)
        return remote(y_send.at[:, cols], y_recv.at[:, cols], y_ss.at[r], y_rs.at[r], y_mate)

    def ykv_copy():
        return remote(ykv_send, ykv_recv, y_ss.at[2], y_rs.at[2], y_mate)

    def halves(rows):
        here = acc[rows, :]
        lower = here[:, 0:YW]
        upper = pltpu.roll(here, BLOCK, 1)[:, 0:YW]
        return jnp.where(y_hi == 0, lower, upper), jnp.where(y_hi == 0, upper, lower)

    acc[...] = jnp.zeros_like(acc)
    @pl.when(core == zhalf)
    def _():
        ag_send(0)

    sib_half(0)
    sib_half(1)
    kv_pair.wait_recv()
    kv_buf[core] = (kv_buf[core].astype(F32) + kv_sib[...].astype(F32)).astype(BF16)
    for i in range(1, CHIPS):
        kv_copy(i).start()
    sib_half(2)
    sib_half(3)
    sib_half(4)
    sib_half(5)
    for i in range(1, CHIPS):
        kv_copy(i).wait_recv()
    kv_sum = kv_buf[core, chip].astype(F32)
    for i in range(CHIPS - 1):
        kv_sum = kv_sum + kv_recv[i].astype(F32)
    kv_all[z] = kv_sum.astype(BF16)
    kvs_copy = remote(kv_all.at[z], kvs_recv, s_sems.at[4], s_sems.at[5], sibling)
    kvs_copy.start()
    kz_start(1)
    ag_first(0)
    ring_start(0, 1)
    wkv_copy.wait_recv()
    kvs_copy.wait_recv()
    kvg_buf[...] = jnp.transpose(
        jnp.concatenate([kv_sum, kvs_recv[...].astype(F32)], axis=0)
    ).astype(BF16)
    own_half(0)
    ag_first(1)
    own_half(1)
    ag_first(2)
    ring_start(1, 1)
    own_half(2)
    ag_first(3)
    ag_second(0)
    own_half(3)
    own_send(0)
    ag_second(1)
    ring_wait(0, 1)
    ring_start(0, 2)
    own_half(4)
    own_half(5)
    ag_second(2)
    own_send(1)
    ag_third(0)
    ag_second(3)
    ring_wait(1, 1)
    ring_start(1, 2)
    kz_wait(1)
    kz_start(2)
    ag_third(1)
    own_send(2)
    ag_third(2)
    ring_wait(0, 2)
    ring_start(0, 3)
    ag_third(3)
    own_send(3)
    ag_last(0)
    ring_wait(1, 2)
    ring_start(1, 3)
    kz_wait(2)
    kz_start(3)
    ag_last(1)
    rs_second(0)
    ring_wait(0, 3)
    ring_start(0, 4)
    sib_in(2).wait_recv()
    wgrad_pair(2)
    rs_second(1)
    ag_last(2)
    own_send(4)
    ring_wait(1, 3)
    ring_start(1, 4)
    kz_wait(3)
    kz_start(4)
    sib_in(1).wait_recv()
    wgrad_pair(1)
    own_send(5)
    rs_second(2)
    ag_last(3)
    sib_in(3).wait_recv()
    wgrad_pair(3)
    rs_second(3)
    sib_in(0).wait_recv()
    kz_wait(4)
    for r in range(2):
        rows = slice(256 * r, 256 * r + 256)
        ring_wait(r, 4)
        wgrad(z, lax.rem(z + 4, NZ), rows, r == 1)
        for q in range(2):
            quarter = slice(256 * r + 128 * q, 256 * r + 128 * q + 128)
            mine, theirs = halves(quarter)
            y_send[:, quarter] = jnp.transpose(theirs)[0:BLOCK].astype(BF16)
            own_buf[:, quarter] = jnp.transpose(mine)[0:BLOCK]
        y_copy(r).start()
    mine, theirs = halves(slice(QC, GC))
    own_kv[...] = mine
    ykv_send[...] = theirs.astype(BF16)
    ykv_copy().start()
    rs_third(0)
    rs_third(1)
    rs_second(4)
    rs_third(2)
    rs_second(5)
    rs_third(3)
    rs_third(4)
    rs_third(5)
    rs_last(0)
    rs_last(1)
    rs_last(2)
    rs_last(3)
    rs_last(4)
    rs_last(5)
    for j in range(NCH):
        f_in(j).wait_recv()
    for h in range(2):
        for j in range(NCH):
            out_in[:, HALF * h + FC * j : HALF * h + FC * j + FC] = f_buf[h, j].astype(F32)[
                0:24
            ].astype(BF16)
    for r in range(2):
        y_copy(r).wait_recv()
        cols = slice(256 * r, 256 * r + 256)
        out_wq[:, cols] = (own_buf[:, cols] + y_recv[:, cols].astype(F32)).astype(BF16)
    ykv_copy().wait_recv()
    total = (own_kv[...] + ykv_recv[...].astype(F32))[:, 0:BLOCK].astype(BF16)
    out_wk[...] = total[0:16]
    out_wv[...] = total[16:32]

    s_copy.wait_send()
    for j in range(4):
        @pl.when(4 * core + j != z)
        def _(j=j):
            a2a(j).wait_send()
    kv_pair.wait_send()
    wkv_copy.wait_send()
    kvs_copy.wait_send()
    for i in range(1, CHIPS):
        kv_copy(i).wait_send()
    for n in range(4):
        ag_y(n).wait_send()
        for d in range(1, 4):
            ag_x(n, d).wait_send()
            ag_d(n, d).wait_send()
    for n in range(4):
        sib(n).wait_send()
    for s in range(1, 5):
        for copy in (*ring(0, s), *ring(1, s), *kz(s)):
            copy.wait_send()
    for j in range(NCH):
        p_copy(j).wait_send()
        f_copy(j).wait_send()
        if j < 4:
            ry_copy(j).wait_send()
        else:
            rxy_copy(j).wait_send()
        for kind in range(3):
            x_copy(j, kind).wait_send()
    for r in range(2):
        y_copy(r).wait_send()
    ykv_copy().wait_send()


def place(*refs):
    for i in range(4):
        refs[4 + i][...] = refs[i][...]


def shards(normed, w_query, w_key, w_value, query, key, value, grad_context):
    vmem = pl.BlockSpec(memory_space=pltpu.VMEM)
    dma = pltpu.SemaphoreType.DMA
    anywhere = pl.BlockSpec(memory_space=pl.ANY)
    results = (
        jax.ShapeDtypeStruct((24, FEAT), BF16),
        jax.ShapeDtypeStruct((BLOCK, QC), BF16),
        jax.ShapeDtypeStruct((16, BLOCK), BF16),
        jax.ShapeDtypeStruct((16, BLOCK), BF16),
    )
    grads = pl.pallas_call(
        kernel,
        out_shape=results,
        in_specs=[anywhere] * 8,
        out_specs=(vmem, vmem, vmem, vmem),
        scratch_shapes=[
            pltpu.VMEM((24, FEAT), BF16),
            pltpu.VMEM((16, FEAT), BF16),
            pltpu.VMEM((16, FEAT), BF16),
            pltpu.VMEM((TOK, QC), BF16),
            pltpu.VMEM((TOK, HEAD_DIM), BF16),
            pltpu.VMEM((TOK, HEAD_DIM), BF16),
            pltpu.VMEM((TOK, QC), BF16),
            pltpu.VMEM((FEAT, QC), BF16),
            pltpu.VMEM((2, 32, HALF), BF16),
            pltpu.VMEM((32, HALF), BF16),
            pltpu.VMEM((2, 32, HALF), BF16),
            pltpu.VMEM((32, HALF), BF16),
            pltpu.VMEM((4, CHIP_TOK, ZF), BF16),
            pltpu.VMEM((NZ, TOK, ZF), BF16),
            pltpu.VMEM((NZ, QC, TOK), BF16),
            pltpu.VMEM((TOK, QC), BF16),
            pltpu.VMEM((2, CHIPS, 32, TOK), BF16),
            pltpu.VMEM((CHIPS, 32, TOK), BF16),
            pltpu.VMEM((CHIPS - 1, 32, TOK), BF16),
            pltpu.VMEM((NZ, 32, TOK), BF16),
            pltpu.VMEM((32, TOK), BF16),
            pltpu.VMEM((TOK, 64), BF16),
            pltpu.VMEM((NCH, TOK, FC), BF16),
            pltpu.VMEM((NCH, TOK, FC), BF16),
            pltpu.VMEM((NCH, 4, 2, CHIP_TOK, FC), BF16),
            pltpu.VMEM((2, 2, CHIP_TOK, FC), BF16),
            pltpu.VMEM((2, 2, 2, CHIP_TOK, FC), BF16),
            pltpu.VMEM((2, CHIP_TOK, FC), BF16),
            pltpu.VMEM((2, CHIP_TOK, FC), BF16),
            pltpu.VMEM((4, 4, CHIP_TOK, FC), BF16),
            pltpu.VMEM((4, CHIP_TOK, FC), BF16),
            pltpu.VMEM((4, 2, CHIP_TOK, FC), BF16),
            pltpu.VMEM((NCH, 32, FC), BF16),
            pltpu.VMEM((2, NCH, 32, FC), BF16),
            pltpu.VMEM((GC, ZF), F32),
            pltpu.VMEM((BLOCK, QC), F32),
            pltpu.VMEM((32, YW), F32),
            pltpu.VMEM((BLOCK, QC), BF16),
            pltpu.VMEM((BLOCK, QC), BF16),
            pltpu.VMEM((32, YW), BF16),
            pltpu.VMEM((32, YW), BF16),
            dma((7,)),
            dma((2 * NCH,)),
            dma((6,)),
            dma((4,)), dma((4,)),
            dma((4,)), dma((4,)),
            dma((4, 3)), dma((4, 3)),
            dma((4, 3)), dma((4, 3)),
            dma((4,)), dma((4,)),
            dma((8,)), dma((8,)),
            dma((2, 4)), dma((2, 4)),
            dma((2, 4)), dma((2, 4)), dma((2, 4)), dma((2, 4)),
            dma((NCH,)), dma((NCH,)),
            dma((2, 3)), dma((2, 3)), dma((2,)), dma((2,)),
            dma((4,)), dma((4,)), dma((4, 3)), dma((4, 3)),
            dma((NCH,)), dma((NCH,)),
            dma((3,)), dma((3,)),
        ],
        compiler_params=pltpu.CompilerParams(
            collective_id=0, has_side_effects=True, vmem_limit_bytes=60 * 1024 * 1024
        ),
    )(
        normed, w_query, jnp.transpose(w_key), jnp.transpose(w_value),
        query, key, value, grad_context,
    )
    grad_input, grad_wq, grad_wk, grad_wv = pl.pallas_call(
        place,
        out_shape=results,
        in_specs=[vmem] * 4,
        out_specs=(vmem,) * 4,
    )(*grads)
    return grad_input, grad_wq, jnp.transpose(grad_wk), jnp.transpose(grad_wv)


def solution(mesh):
    placed = (
        P(("dp", "mp"), None),
        P(None, "mp"),
        P(None, "mp"),
        P(None, "mp"),
        P("dp", "mp"),
        P("dp", None),
        P("dp", None),
        P("dp", "mp"),
    )
    return jax.shard_map(
        shards,
        mesh=mesh,
        in_specs=placed,
        out_specs=(P(("dp", "mp"), None), P("dp", "mp"), P("dp", "mp"), P("dp", "mp")),
        check_vma=False,
    )
```

```python
import jax
import jax.numpy as jnp
from jax import lax
from jax.experimental import pallas as pl
from jax.experimental.pallas import tpu as pltpu
from jax.sharding import PartitionSpec as P

HEAD_DIM = 256
TOK = 384
NZ = 8
CHIPS = 8
CHIP_TOK = 48
FEAT = 9216
HALF = FEAT // 2
BLOCK = 576
ZF = 2 * BLOCK
QC = 512
GC = 544
FC = 768
NCH = HALF // FC
YW = 640
MESH = pl.DeviceIdType.MESH
F32 = jnp.float32
BF16 = jnp.bfloat16
NT = (((1,), (1,)), ((), ()))


def dot(a, b):
    return jnp.dot(a, b, preferred_element_type=F32)


def dot_nt(a, b):
    return lax.dot_general(a, b, NT, preferred_element_type=F32)


def kernel(
    normed_hbm, wq_hbm, wk_hbm, wv_hbm, query_hbm, key_hbm, value_hbm, grad_hbm,
    in_hbm, wq_out_hbm, wk_out_hbm, wv_out_hbm,
    out_in, out_wq, out_wk, out_wv,
    normed, wk_t, wv_t, query, key, value, grad,
    w_buf, wkv, wkv_sib, s_buf, s_recv, t_buf, n_buf, gt_buf, g_buf, kv_buf, kv_sib, kv_recv, kv_all, kvs_recv, kvg_buf,
    p_send, p_recv, r_buf, rx_mid, rx_recv, rx_send, rx_last, ry_recv, ry_mid, ry_last, f_send, f_buf,
    acc, own_buf, own_kv, y_send, y_recv, ykv_send, ykv_recv,
    out_sems, in_sems, w_sems, s_sems, a2a_ss, a2a_rs, agy_ss, agy_rs, agx_ss, agx_rs, agd_ss, agd_rs,
    sib_ss, sib_rs, kv_ss, kv_rs, kz_ss, kz_rs,
    cw_ss, cw_rs, cc_ss, cc_rs, p_ss, p_rs,
    rx_ss, rx_rs, rxy_ss, rxy_rs, ry_ss, ry_rs, ryx_ss, ryx_rs, f_ss, f_rs, y_ss, y_rs,
):
    dp = lax.axis_index("dp")
    mp = lax.axis_index("mp")
    z = lax.rem(dp, NZ)
    y_hi = lax.div(dp, NZ)
    base = y_hi * NZ
    core = lax.rem(mp, 2)
    chip = lax.div(mp, 2)
    other = 1 - core
    sibling = (dp, chip * 2 + other)
    zhalf = lax.div(z, 4)
    x = lax.div(chip, 2)
    y_lo = lax.rem(chip, 2)
    y_chip = chip + 1 - 2 * y_lo
    y_mate = (lax.rem(dp + NZ, 2 * NZ), mp)

    def remote(src, dst, ss, rs, device):
        return pltpu.make_async_remote_copy(
            src_ref=src, dst_ref=dst, send_sem=ss, recv_sem=rs,
            device_id=device, device_id_type=MESH,
        )

    def w_copy(half, j):
        rows = pl.ds(pl.multiple_of((half * NCH + j) * FC, FC), FC)
        return pltpu.make_async_copy(
            wq_hbm.at[rows, :], w_buf.at[rows, :], w_sems.at[half * NCH + j]
        )


    inputs = (
        (normed_hbm, normed), (query_hbm, query), (key_hbm, key), (grad_hbm, grad),
        (value_hbm, value), (wk_hbm, wk_t), (wv_hbm, wv_t),
    )
    loads = [
        pltpu.make_async_copy(there, here, in_sems.at[i])
        for i, (there, here) in enumerate(inputs)
    ]
    for load in loads:
        load.start()

    barrier = pltpu.get_barrier_semaphore()
    for i in range(1, NZ):
        there = base + lax.rem(z + i, NZ)
        pl.semaphore_signal(barrier, inc=1, device_id=(there, mp), device_id_type=MESH)
        pl.semaphore_signal(
            barrier, inc=1, device_id=(there, chip * 2 + other), device_id_type=MESH
        )
    pl.semaphore_signal(barrier, inc=1, device_id=y_mate, device_id_type=MESH)
    for i in range(1, 2 * CHIPS):
        pl.semaphore_signal(
            barrier, inc=1, device_id=(dp, lax.rem(mp + i, 2 * CHIPS)), device_id_type=MESH
        )

    for j in range(NCH):
        w_copy(other, j).start()
    for j in range(NCH):
        w_copy(core, j).start()
    loads[0].wait()
    for h in range(2):
        for part in range(2):
            cols = normed[:, HALF * part + 2304 * h : HALF * part + 2304 * h + 2304].astype(F32)
            padded = jnp.concatenate([cols, jnp.zeros((8, 2304), F32)], axis=0)
            s_buf[h, :, 2304 * part : 2304 * part + 2304] = padded.astype(BF16)
    pl.semaphore_wait(barrier, 2 * (NZ - 1) + 1 + 2 * CHIPS - 1)
    s_copy = remote(s_buf.at[other], s_recv, s_sems.at[0], s_sems.at[1], sibling)
    s_copy.start()
    loads[5].wait()
    loads[6].wait()
    for h in range(2):
        wkv[h, 0:16, :] = wk_t[:, HALF * h : HALF * h + HALF]
        wkv[h, 16:32, :] = wv_t[:, HALF * h : HALF * h + HALF]
    wkv_copy = remote(wkv.at[other], wkv_sib, s_sems.at[2], s_sems.at[3], sibling)
    wkv_copy.start()

    right = (base + lax.rem(z + 1, NZ), mp)
    left = (base + lax.rem(z + NZ - 1, NZ), mp)

    def ring_pair(h, s, slot_r, slot_l):
        first = HEAD_DIM * h
        if s < 4:
            src_r = gt_buf.at[slot_r, first : first + 256, :]
            src_l = gt_buf.at[slot_l, first : first + 256, :]
        else:
            src_r = gt_buf.at[slot_r, first : first + 128, :]
            src_l = gt_buf.at[slot_l, first + 128 : first + 256, :]
        return (
            remote(src_r, src_r, cw_ss.at[h, s - 1], cw_rs.at[h, s - 1], right),
            remote(src_l, src_l, cc_ss.at[h, s - 1], cc_rs.at[h, s - 1], left),
        )

    def ring(h, s):
        return ring_pair(h, s, lax.rem(z - (s - 1) + NZ, NZ), lax.rem(z + (s - 1), NZ))

    def ring_start(h, s):
        for copy in ring(h, s):
            copy.start()

    def ring_wait(h, s):
        for copy in ring_pair(h, s, lax.rem(z - s + NZ, NZ), lax.rem(z + s, NZ)):
            copy.wait_recv()

    def kz_pair(s, slot_r, slot_l):
        src_r, src_l = kv_all.at[slot_r], kv_all.at[slot_l]
        copies = [remote(src_r, src_r, kz_ss.at[0, s - 1], kz_rs.at[0, s - 1], right)]
        if s < 4:
            copies.append(remote(src_l, src_l, kz_ss.at[1, s - 1], kz_rs.at[1, s - 1], left))
        return copies

    def kz(s):
        return kz_pair(s, lax.rem(z - (s - 1) + NZ, NZ), lax.rem(z + (s - 1), NZ))

    def kz_start(s):
        for copy in kz(s):
            copy.start()

    def kz_wait(s):
        for copy in kz_pair(s, lax.rem(z - s + NZ, NZ), lax.rem(z + s, NZ)):
            copy.wait_recv()

    def piece_n(o):
        return jnp.where(core == zhalf, (0, 2, 1, 3)[o], (2, 1, 3, 0)[o])

    def piece_z(o):
        return lax.rem(z + piece_n(o), 4)

    for i in range(1, 5):
        loads[i].wait()
    key_v = key[...]
    value_v = value[...]
    key_t = jnp.transpose(key_v.astype(F32)).astype(BF16)
    scale = HEAD_DIM ** (-0.5)
    causal = lax.broadcasted_iota(jnp.int32, (TOK, TOK), 0) <= lax.broadcasted_iota(
        jnp.int32, (TOK, TOK), 1
    )
    kp = None
    vp = None
    for h in range(2):
        q_h = query[:, HEAD_DIM * h : HEAD_DIM * h + HEAD_DIM]
        g_h = grad[:, HEAD_DIM * h : HEAD_DIM * h + HEAD_DIM]
        scores = jnp.where(causal, dot_nt(key_v, q_h) * scale, -jnp.inf)
        expo = jnp.exp(scores - jnp.max(scores, axis=0, keepdims=True))
        probs = expo * (1.0 / jnp.sum(expo, axis=0, keepdims=True))
        low = probs.astype(BF16)
        dprob = dot_nt(value_v, g_h)
        delta = jnp.sum(low.astype(F32) * dprob, axis=0, keepdims=True)
        dscore = (probs * (dprob - delta)).astype(BF16)
        kp_h = dot(dscore, q_h)
        vp_h = dot(low, g_h)
        kp = kp_h if kp is None else kp + kp_h
        vp = vp_h if vp is None else vp + vp_h
        gq = dot(key_t, dscore) * scale
        gt_buf[z, HEAD_DIM * h : HEAD_DIM * h + HEAD_DIM, :] = gq.astype(BF16)
        g_buf[:, HEAD_DIM * h : HEAD_DIM * h + HEAD_DIM] = jnp.transpose(gq).astype(BF16)
        if h == 0:
            s_copy.wait_recv()
            mine = s_buf[core].astype(F32)[:24]
            theirs = s_recv[...].astype(F32)[:24]
            first = jnp.where(core == 0, mine, theirs)
            second = jnp.where(core == 0, theirs, mine)
            both = jnp.concatenate([first, second], axis=0)
            for j in range(4):
                block = jnp.concatenate(
                    [
                        both[:, BLOCK * j : BLOCK * j + BLOCK],
                        both[:, 2304 + BLOCK * j : 2304 + BLOCK * j + BLOCK],
                    ],
                    axis=1,
                )
                t_buf[j] = block.astype(BF16)
            chip_rows = pl.ds(pl.multiple_of(chip * CHIP_TOK, 16), CHIP_TOK)

            def a2a(j):
                peer = 4 * core + j
                return remote(
                    t_buf.at[j], n_buf.at[z, chip_rows, :], a2a_ss.at[j], a2a_rs.at[lax.rem(z, 4)],
                    (base + peer, chip * 2 + zhalf),
                )

            def a2a_in(j):
                peer = 4 * core + j
                return remote(
                    t_buf.at[j], n_buf.at[peer, chip_rows, :], a2a_ss.at[j], a2a_rs.at[j],
                    (base + peer, chip * 2 + zhalf),
                )

            def a2a_send(o):
                j = lax.rem(z + 4 - piece_n(o), 4)

                @pl.when(4 * core + j != z)
                def _():
                    a2a(j).start()

                @pl.when(4 * core + j == z)
                def _():
                    n_buf[z, chip_rows, :] = t_buf[j]

            a2a_send(0)
            a2a_send(1)

    kp_t = jnp.transpose(kp * scale)
    vp_t = jnp.transpose(vp)
    for c in range(2):
        kv_buf[c, :, 0:16, :] = kp_t.reshape(CHIPS, 2, 16, TOK)[:, c].astype(BF16)
        kv_buf[c, :, 16:32, :] = vp_t.reshape(CHIPS, 2, 16, TOK)[:, c].astype(BF16)
    kv_pair = remote(kv_buf.at[other], kv_sib, kv_ss.at[7], kv_rs.at[7], sibling)
    kv_pair.start()

    def kv_copy(i):
        there = lax.rem(chip + i, CHIPS)
        return remote(
            kv_buf.at[core, there], kv_recv.at[i - 1], kv_ss.at[i - 1], kv_rs.at[i - 1],
            (dp, there * 2 + core),
        )

    def n_rows(k):
        return pl.ds(pl.multiple_of(k * CHIP_TOK, 16), CHIP_TOK)

    def piece(o, k):
        return n_buf.at[4 * core + piece_z(o), n_rows(k), :]

    def x_chip(d):
        return lax.rem(x + d, 4) * 2 + y_lo

    def x_from(d):
        return lax.rem(x + 4 - d, 4) * 2 + y_lo

    def ag_y(n):
        return remote(
            piece(n, chip), piece(n, chip), agy_ss.at[n], agy_rs.at[n], (dp, y_chip * 2 + core)
        )

    def ag_x(n, d):
        k, to = (x_from(1), 1) if d == 2 else (chip, d)
        return remote(
            piece(n, k), piece(n, k), agx_ss.at[n, d - 1], agx_rs.at[n, d - 1],
            (dp, x_chip(to) * 2 + core),
        )

    def ag_d(n, d):
        if d == 2:
            k, there = x_from(3) + 1 - 2 * y_lo, x_chip(3)
        else:
            k, there = y_chip, x_chip(d)
        return remote(
            piece(n, k), piece(n, k), agd_ss.at[n, d - 1], agd_rs.at[n, d - 1],
            (dp, there * 2 + core),
        )

    def sib(n):
        block = n_buf.at[4 * core + piece_z(n)]
        return remote(block, block, sib_ss.at[n], sib_rs.at[n], sibling)

    def sib_in(n):
        o = jnp.where(core == zhalf, (3, 1, 0, 2)[n], (0, 2, 1, 3)[n])
        block = n_buf.at[4 * other + lax.rem(z + n, 4)]
        return remote(block, block, sib_ss.at[o], sib_rs.at[o], sibling)

    def ag_send(n):
        ag_y(n).start()
        ag_x(n, 1).start()
        ag_x(n, 3).start()

    def ag_first(n):
        j = piece_z(n)
        if n == 0:
            @pl.when(core != zhalf)
            def _():
                a2a_in(j).wait_recv()
                ag_send(0)
        else:
            @pl.when(4 * core + j != z)
            def _():
                a2a_in(j).wait_recv()

            ag_send(n)

    def ag_second(n):
        ag_x(n, 1).wait_recv()
        ag_x(n, 2).start()
        ag_y(n).wait_recv()
        ag_d(n, 1).start()
        ag_d(n, 3).start()

    def ag_third(n):
        ag_d(n, 3).wait_recv()
        ag_d(n, 2).start()

    def ag_last(n):
        ag_x(n, 3).wait_recv()
        ag_x(n, 2).wait_recv()
        ag_d(n, 1).wait_recv()
        ag_d(n, 2).wait_recv()
        sib(n).start()

    def partial(half, j):
        first = pl.multiple_of((half * NCH + j) * FC, FC)
        w_copy(half, j).wait()
        return dot_nt(g_buf[...], w_buf[pl.ds(first, FC), :])

    def p_copy(j):
        return remote(p_send.at[j], p_recv.at[j], p_ss.at[j], p_rs.at[j], sibling)

    def sib_half(j):
        p_send[j] = partial(other, j).astype(BF16)
        p_copy(j).start()

    def index(j):
        return j if j < 4 else j - 4

    def x_way(j):
        return 1 if index(j) % 2 == 0 else 3

    def x_block(j, d):
        there = lax.rem(x + d, 4)
        return r_buf.at[j, there] if j >= 4 else r_buf.at[j, there, y_lo]

    def x_copy(j, kind):
        way = x_way(j)
        d, to = ((2, way), (way, way), (4 - way, 4 - way))[kind]
        if j >= 4:
            n, ss, rs, mid, last = index(j), rx_ss, rx_rs, rx_mid, rx_recv
        else:
            n, ss, rs, mid, last = index(j), ryx_ss, ryx_rs, ry_mid, ry_last
        dst = mid.at[n] if kind == 0 else last.at[n, kind - 1]
        return remote(
            x_block(j, d), dst, ss.at[n, kind], rs.at[n, kind], (dp, x_chip(to) * 2 + core)
        )

    def x_first(j):
        x_copy(j, 0).start()
        x_copy(j, 2).start()

    def x_mid(j):
        x_copy(j, 0).wait_recv()
        there = lax.rem(x + x_way(j), 4)
        if j >= 4:
            for k in range(2):
                r_buf[j, there, k] = (
                    r_buf[j, there, k].astype(F32) + rx_mid[index(j), k].astype(F32)
                ).astype(BF16)
        else:
            r_buf[j, there, y_lo] = (
                r_buf[j, there, y_lo].astype(F32) + ry_mid[index(j)].astype(F32)
            ).astype(BF16)
        x_copy(j, 1).start()

    def rxy_copy(j):
        n = index(j)
        return remote(
            rx_send.at[n], rx_last.at[n], rxy_ss.at[n], rxy_rs.at[n], (dp, y_chip * 2 + core)
        )

    def ry_copy(j):
        return remote(
            r_buf.at[j, :, 1 - y_lo], ry_recv.at[index(j)], ry_ss.at[index(j)], ry_rs.at[index(j)],
            (dp, y_chip * 2 + core),
        )

    def own_half(j):
        cols = slice(FC * j, FC * j + FC)
        both = jnp.concatenate([wkv[core, :, cols], wkv_sib[:, cols]], axis=0)
        total = partial(core, j) + dot(kvg_buf[...], both)
        p_copy(j).wait_recv()
        total = (total + p_recv[j].astype(F32)).astype(BF16)
        r_buf[j] = total.reshape(4, 2, CHIP_TOK, FC)

    def own_send(j):
        if j < 4:
            ry_copy(j).start()
        else:
            x_first(j)

    def rs_second(j):
        if j < 4:
            ry_copy(j).wait_recv()
            for k in range(4):
                r_buf[j, k, y_lo] = (
                    r_buf[j, k, y_lo].astype(F32) + ry_recv[index(j), k].astype(F32)
                ).astype(BF16)
            x_first(j)
        else:
            x_mid(j)

    def rs_third(j):
        if j < 4:
            x_mid(j)
        else:
            n = index(j)
            x_copy(j, 1).wait_recv()
            x_copy(j, 2).wait_recv()
            out = r_buf[j, x, 1 - y_lo].astype(F32)
            for d in range(2):
                out = out + rx_recv[n, d, 1 - y_lo].astype(F32)
            rx_send[n] = out.astype(BF16)
            rxy_copy(j).start()

    def rs_last(j):
        total = r_buf[j, x, y_lo].astype(F32)
        if j < 4:
            x_copy(j, 1).wait_recv()
            x_copy(j, 2).wait_recv()
            for d in range(2):
                total = total + ry_last[index(j), d].astype(F32)
        else:
            n = index(j)
            for d in range(2):
                total = total + rx_recv[n, d, y_lo].astype(F32)
            rxy_copy(j).wait_recv()
            total = total + rx_last[n].astype(F32)
        low, high = total[0:24], total[24:48]
        pad = jnp.zeros((8, FC), F32)
        mine = jnp.where(core == 0, low, high)
        theirs = jnp.where(core == 0, high, low)
        f_buf[core, j] = jnp.concatenate([mine, pad], axis=0).astype(BF16)
        f_send[j] = jnp.concatenate([theirs, pad], axis=0).astype(BF16)
        f_copy(j).start()

    def f_copy(j):
        return remote(f_send.at[j], f_buf.at[core, j], f_ss.at[j], f_rs.at[j], sibling)

    def f_in(j):
        return remote(f_send.at[j], f_buf.at[other, j], f_ss.at[j], f_rs.at[j], sibling)

    def wgrad(za, zb, first, with_kv):
        lhs = [jnp.concatenate([gt_buf[za, first, :], gt_buf[zb, first, :]], axis=1)]
        if with_kv:
            lhs.append(jnp.concatenate([kv_all[za], kv_all[zb]], axis=1))
        lhs = jnp.concatenate(lhs, axis=0)
        rows = slice(first.start, first.start + lhs.shape[0])
        for cols in (slice(0, 512), slice(512, 1024), slice(1024, ZF)):
            rhs = jnp.concatenate([n_buf[za, :, cols], n_buf[zb, :, cols]], axis=0)
            acc[rows, cols] += dot(lhs, rhs)

    def wgrad_pair(n):
        wgrad(lax.rem(z + n, NZ), lax.rem(z + n + 4, NZ), slice(0, QC), True)

    def y_copy(r):
        cols = slice(256 * r, 256 * r + 256)
        return remote(y_send.at[:, cols], y_recv.at[:, cols], y_ss.at[r], y_rs.at[r], y_mate)

    def ykv_copy():
        return remote(ykv_send, ykv_recv, y_ss.at[2], y_rs.at[2], y_mate)

    def halves(rows):
        here = acc[rows, :]
        lower = here[:, 0:YW]
        upper = pltpu.roll(here, BLOCK, 1)[:, 0:YW]
        return jnp.where(y_hi == 0, lower, upper), jnp.where(y_hi == 0, upper, lower)

    acc[...] = jnp.zeros_like(acc)
    @pl.when(core == zhalf)
    def _():
        ag_send(0)

    sib_half(0)
    sib_half(1)
    kv_pair.wait_recv()
    kv_buf[core] = (kv_buf[core].astype(F32) + kv_sib[...].astype(F32)).astype(BF16)
    for i in range(1, CHIPS):
        kv_copy(i).start()
    a2a_send(2)
    sib_half(2)
    sib_half(3)
    a2a_send(3)
    sib_half(4)
    sib_half(5)
    for i in range(1, CHIPS):
        kv_copy(i).wait_recv()
    kv_sum = kv_buf[core, chip].astype(F32)
    for i in range(CHIPS - 1):
        kv_sum = kv_sum + kv_recv[i].astype(F32)
    kv_all[z] = kv_sum.astype(BF16)
    kvs_copy = remote(kv_all.at[z], kvs_recv, s_sems.at[4], s_sems.at[5], sibling)
    kvs_copy.start()
    kz_start(1)
    ag_first(0)
    ring_start(0, 1)
    wkv_copy.wait_recv()
    kvs_copy.wait_recv()
    kvg_buf[...] = jnp.transpose(
        jnp.concatenate([kv_sum, kvs_recv[...].astype(F32)], axis=0)
    ).astype(BF16)
    own_half(0)
    ag_first(1)
    own_half(1)
    ag_first(2)
    ring_start(1, 1)
    own_half(2)
    ag_first(3)
    ag_second(0)
    own_half(3)
    own_send(0)
    ag_second(1)
    ring_wait(0, 1)
    ring_start(0, 2)
    own_half(4)
    own_half(5)
    ag_second(2)
    own_send(1)
    ag_third(0)
    ag_second(3)
    ring_wait(1, 1)
    ring_start(1, 2)
    kz_wait(1)
    kz_start(2)
    ag_third(1)
    own_send(2)
    ag_third(2)
    ring_wait(0, 2)
    ring_start(0, 3)
    ag_third(3)
    own_send(3)
    ag_last(0)
    ring_wait(1, 2)
    ring_start(1, 3)
    kz_wait(2)
    kz_start(3)
    ag_last(1)
    rs_second(0)
    ring_wait(0, 3)
    ring_start(0, 4)
    own_send(4)
    sib_in(2).wait_recv()
    wgrad_pair(2)
    rs_second(1)
    ag_last(2)
    ring_wait(1, 3)
    ring_start(1, 4)
    kz_wait(3)
    kz_start(4)
    sib_in(1).wait_recv()
    wgrad_pair(1)
    own_send(5)
    rs_second(2)
    ag_last(3)
    sib_in(3).wait_recv()
    wgrad_pair(3)
    rs_second(3)
    rs_second(4)
    sib_in(0).wait_recv()
    kz_wait(4)
    for r in range(2):
        rows = slice(256 * r, 256 * r + 256)
        ring_wait(r, 4)
        wgrad(z, lax.rem(z + 4, NZ), rows, r == 1)
        for q in range(2):
            quarter = slice(256 * r + 128 * q, 256 * r + 128 * q + 128)
            mine, theirs = halves(quarter)
            y_send[:, quarter] = jnp.transpose(theirs)[0:BLOCK].astype(BF16)
            own_buf[:, quarter] = jnp.transpose(mine)[0:BLOCK]
        y_copy(r).start()
    mine, theirs = halves(slice(QC, GC))
    own_kv[...] = mine
    ykv_send[...] = theirs.astype(BF16)
    ykv_copy().start()
    rs_third(0)
    rs_third(1)
    rs_third(2)
    rs_second(5)
    rs_third(3)
    rs_third(4)
    rs_third(5)
    rs_last(0)
    rs_last(1)
    rs_last(2)
    rs_last(3)
    s_copy.wait_send()
    for j in range(4):
        @pl.when(4 * core + j != z)
        def _(j=j):
            a2a(j).wait_send()
    kv_pair.wait_send()
    wkv_copy.wait_send()
    kvs_copy.wait_send()
    for i in range(1, CHIPS):
        kv_copy(i).wait_send()
    for n in range(4):
        ag_y(n).wait_send()
        for d in range(1, 4):
            ag_x(n, d).wait_send()
            ag_d(n, d).wait_send()
    for n in range(4):
        sib(n).wait_send()
    for s in range(1, 5):
        for copy in (*ring(0, s), *ring(1, s), *kz(s)):
            copy.wait_send()
    for j in range(NCH):
        p_copy(j).wait_send()
        if j < 4:
            ry_copy(j).wait_send()
        for kind in range(3):
            x_copy(j, kind).wait_send()
    rs_last(4)
    rs_last(5)
    outs = []
    for r in range(2):
        y_copy(r).wait_recv()
        cols = slice(256 * r, 256 * r + 256)
        out_wq[:, cols] = (own_buf[:, cols] + y_recv[:, cols].astype(F32)).astype(BF16)
        outs.append(
            pltpu.make_async_copy(out_wq.at[:, cols], wq_out_hbm.at[:, cols], out_sems.at[r])
        )
        outs[-1].start()
    ykv_copy().wait_recv()
    total = (own_kv[...] + ykv_recv[...].astype(F32))[:, 0:BLOCK].astype(BF16)
    out_wk[...] = total[0:16]
    out_wv[...] = total[16:32]
    outs.append(pltpu.make_async_copy(out_wk, wk_out_hbm, out_sems.at[2]))
    outs[-1].start()
    outs.append(pltpu.make_async_copy(out_wv, wv_out_hbm, out_sems.at[3]))
    outs[-1].start()
    for j in range(NCH):
        f_in(j).wait_recv()
    for h in range(2):
        for j in range(NCH):
            out_in[:, HALF * h + FC * j : HALF * h + FC * j + FC] = f_buf[h, j].astype(F32)[
                0:24
            ].astype(BF16)
    outs.append(pltpu.make_async_copy(out_in, in_hbm, out_sems.at[4]))
    outs[-1].start()
    for j in range(NCH):
        f_copy(j).wait_send()
        if j >= 4:
            rxy_copy(j).wait_send()
    for r in range(2):
        y_copy(r).wait_send()
    ykv_copy().wait_send()
    for out in outs:
        out.wait()


def place(*refs):
    ins, outs, held, sems = refs[0:4], refs[4:8], refs[8:12], refs[12]
    parts = [(0, slice(0, 24)), (1, slice(0, 288)), (1, slice(288, 576))]
    parts += [(2, slice(0, 16)), (3, slice(0, 16))]
    first = []
    for n, (i, rows) in enumerate(parts):
        first.append(pltpu.make_async_copy(ins[i].at[rows], held[i].at[rows], sems.at[n, 0]))
        first[-1].start()
    second = []
    for n, (i, rows) in enumerate(parts):
        first[n].wait()
        second.append(pltpu.make_async_copy(held[i].at[rows], outs[i].at[rows], sems.at[n, 1]))
        second[-1].start()
    for copy in second:
        copy.wait()


def shards(normed, w_query, w_key, w_value, query, key, value, grad_context):
    dma = pltpu.SemaphoreType.DMA
    anywhere = pl.BlockSpec(memory_space=pl.ANY)
    results = (
        jax.ShapeDtypeStruct((24, FEAT), BF16),
        jax.ShapeDtypeStruct((BLOCK, QC), BF16),
        jax.ShapeDtypeStruct((16, BLOCK), BF16),
        jax.ShapeDtypeStruct((16, BLOCK), BF16),
    )
    grads = pl.pallas_call(
        kernel,
        out_shape=results,
        in_specs=[anywhere] * 8,
        out_specs=(anywhere,) * 4,
        scratch_shapes=[
            pltpu.VMEM((24, FEAT), BF16),
            pltpu.VMEM((BLOCK, QC), BF16),
            pltpu.VMEM((16, BLOCK), BF16),
            pltpu.VMEM((16, BLOCK), BF16),
            pltpu.VMEM((24, FEAT), BF16),
            pltpu.VMEM((16, FEAT), BF16),
            pltpu.VMEM((16, FEAT), BF16),
            pltpu.VMEM((TOK, QC), BF16),
            pltpu.VMEM((TOK, HEAD_DIM), BF16),
            pltpu.VMEM((TOK, HEAD_DIM), BF16),
            pltpu.VMEM((TOK, QC), BF16),
            pltpu.VMEM((FEAT, QC), BF16),
            pltpu.VMEM((2, 32, HALF), BF16),
            pltpu.VMEM((32, HALF), BF16),
            pltpu.VMEM((2, 32, HALF), BF16),
            pltpu.VMEM((32, HALF), BF16),
            pltpu.VMEM((4, CHIP_TOK, ZF), BF16),
            pltpu.VMEM((NZ, TOK, ZF), BF16),
            pltpu.VMEM((NZ, QC, TOK), BF16),
            pltpu.VMEM((TOK, QC), BF16),
            pltpu.VMEM((2, CHIPS, 32, TOK), BF16),
            pltpu.VMEM((CHIPS, 32, TOK), BF16),
            pltpu.VMEM((CHIPS - 1, 32, TOK), BF16),
            pltpu.VMEM((NZ, 32, TOK), BF16),
            pltpu.VMEM((32, TOK), BF16),
            pltpu.VMEM((TOK, 64), BF16),
            pltpu.VMEM((NCH, TOK, FC), BF16),
            pltpu.VMEM((NCH, TOK, FC), BF16),
            pltpu.VMEM((NCH, 4, 2, CHIP_TOK, FC), BF16),
            pltpu.VMEM((2, 2, CHIP_TOK, FC), BF16),
            pltpu.VMEM((2, 2, 2, CHIP_TOK, FC), BF16),
            pltpu.VMEM((2, CHIP_TOK, FC), BF16),
            pltpu.VMEM((2, CHIP_TOK, FC), BF16),
            pltpu.VMEM((4, 4, CHIP_TOK, FC), BF16),
            pltpu.VMEM((4, CHIP_TOK, FC), BF16),
            pltpu.VMEM((4, 2, CHIP_TOK, FC), BF16),
            pltpu.VMEM((NCH, 32, FC), BF16),
            pltpu.VMEM((2, NCH, 32, FC), BF16),
            pltpu.VMEM((GC, ZF), F32),
            pltpu.VMEM((BLOCK, QC), F32),
            pltpu.VMEM((32, YW), F32),
            pltpu.VMEM((BLOCK, QC), BF16),
            pltpu.VMEM((BLOCK, QC), BF16),
            pltpu.VMEM((32, YW), BF16),
            pltpu.VMEM((32, YW), BF16),
            dma((5,)),
            dma((7,)),
            dma((2 * NCH,)),
            dma((6,)),
            dma((4,)), dma((4,)),
            dma((4,)), dma((4,)),
            dma((4, 3)), dma((4, 3)),
            dma((4, 3)), dma((4, 3)),
            dma((4,)), dma((4,)),
            dma((8,)), dma((8,)),
            dma((2, 4)), dma((2, 4)),
            dma((2, 4)), dma((2, 4)), dma((2, 4)), dma((2, 4)),
            dma((NCH,)), dma((NCH,)),
            dma((2, 3)), dma((2, 3)), dma((2,)), dma((2,)),
            dma((4,)), dma((4,)), dma((4, 3)), dma((4, 3)),
            dma((NCH,)), dma((NCH,)),
            dma((3,)), dma((3,)),
        ],
        compiler_params=pltpu.CompilerParams(
            collective_id=0, has_side_effects=True, vmem_limit_bytes=60 * 1024 * 1024
        ),
    )(
        normed, w_query, jnp.transpose(w_key), jnp.transpose(w_value),
        query, key, value, grad_context,
    )
    grad_input, grad_wq, grad_wk, grad_wv = pl.pallas_call(
        place,
        out_shape=results,
        in_specs=[anywhere] * 4,
        out_specs=(anywhere,) * 4,
        scratch_shapes=[pltpu.VMEM(result.shape, BF16) for result in results] + [dma((5, 2))],
        compiler_params=pltpu.CompilerParams(vmem_limit_bytes=60 * 1024 * 1024),
    )(*grads)
    return grad_input, grad_wq, jnp.transpose(grad_wk), jnp.transpose(grad_wv)


def solution(mesh):
    placed = (
        P(("dp", "mp"), None),
        P(None, "mp"),
        P(None, "mp"),
        P(None, "mp"),
        P("dp", "mp"),
        P("dp", None),
        P("dp", None),
        P("dp", "mp"),
    )
    return jax.shard_map(
        shards,
        mesh=mesh,
        in_specs=placed,
        out_specs=(P(("dp", "mp"), None), P("dp", "mp"), P("dp", "mp"), P("dp", "mp")),
        check_vma=False,
    )
```

```python
import jax
import jax.numpy as jnp
from jax import lax
from jax.experimental import pallas as pl
from jax.experimental.pallas import tpu as pltpu
from jax.sharding import PartitionSpec as P

HEAD_DIM = 256
TOK = 384
NZ = 8
CHIPS = 8
CHIP_TOK = 48
FEAT = 9216
HALF = FEAT // 2
BLOCK = 576
ZF = 2 * BLOCK
QC = 512
GC = 544
FC = 768
NCH = HALF // FC
YW = 640
MESH = pl.DeviceIdType.MESH
F32 = jnp.float32
BF16 = jnp.bfloat16
NT = (((1,), (1,)), ((), ()))


def dot(a, b):
    return jnp.dot(a, b, preferred_element_type=F32)


def dot_nt(a, b):
    return lax.dot_general(a, b, NT, preferred_element_type=F32)


def kernel(
    normed, wq_hbm, wk_hbm, wv_hbm, query_hbm, key_hbm, value_hbm, grad_hbm,
    out_in, wq_out_hbm, wk_out_hbm, wv_out_hbm,
    out_wq, out_wk, out_wv,
    wk_t, wv_t, query, key, value, grad,
    w_buf, wkv, wkv_sib, s_buf, s_recv, t_buf, n_buf, gt_buf, g_buf, kv_buf, kv_sib, kv_recv, kv_all, kvs_recv, kvg_buf,
    p_send, p_recv, r_buf, rx_mid, rx_recv, rx_send, rx_last, ry_recv, ry_mid, ry_last, f_send, f_buf,
    acc, own_buf, own_kv, y_send, y_recv, ykv_send, ykv_recv,
    out_sems, in_sems, w_sems, s_sems, a2a_ss, a2a_rs, agy_ss, agy_rs, agx_ss, agx_rs, agd_ss, agd_rs,
    sib_ss, sib_rs, kv_ss, kv_rs, kz_ss, kz_rs,
    cw_ss, cw_rs, cc_ss, cc_rs, p_ss, p_rs,
    rx_ss, rx_rs, rxy_ss, rxy_rs, ry_ss, ry_rs, ryx_ss, ryx_rs, f_ss, f_rs, y_ss, y_rs,
):
    dp = lax.axis_index("dp")
    mp = lax.axis_index("mp")
    z = lax.rem(dp, NZ)
    y_hi = lax.div(dp, NZ)
    base = y_hi * NZ
    core = lax.rem(mp, 2)
    chip = lax.div(mp, 2)
    other = 1 - core
    sibling = (dp, chip * 2 + other)
    zhalf = lax.div(z, 4)
    x = lax.div(chip, 2)
    y_lo = lax.rem(chip, 2)
    y_chip = chip + 1 - 2 * y_lo
    y_mate = (lax.rem(dp + NZ, 2 * NZ), mp)

    def remote(src, dst, ss, rs, device):
        return pltpu.make_async_remote_copy(
            src_ref=src, dst_ref=dst, send_sem=ss, recv_sem=rs,
            device_id=device, device_id_type=MESH,
        )

    def w_copy(half, j):
        rows = pl.ds(pl.multiple_of((half * NCH + j) * FC, FC), FC)
        return pltpu.make_async_copy(
            wq_hbm.at[rows, :], w_buf.at[rows, :], w_sems.at[half * NCH + j]
        )


    inputs = (
        (query_hbm, query), (key_hbm, key), (grad_hbm, grad),
        (value_hbm, value), (wk_hbm, wk_t), (wv_hbm, wv_t),
    )
    loads = [
        pltpu.make_async_copy(there, here, in_sems.at[i])
        for i, (there, here) in enumerate(inputs)
    ]
    for load in loads:
        load.start()

    barrier = pltpu.get_barrier_semaphore()
    for i in range(1, NZ):
        there = base + lax.rem(z + i, NZ)
        pl.semaphore_signal(barrier, inc=1, device_id=(there, mp), device_id_type=MESH)
        pl.semaphore_signal(
            barrier, inc=1, device_id=(there, chip * 2 + other), device_id_type=MESH
        )
    pl.semaphore_signal(barrier, inc=1, device_id=y_mate, device_id_type=MESH)
    for i in range(1, 2 * CHIPS):
        pl.semaphore_signal(
            barrier, inc=1, device_id=(dp, lax.rem(mp + i, 2 * CHIPS)), device_id_type=MESH
        )

    for j in range(NCH):
        w_copy(other, j).start()
    for j in range(NCH):
        w_copy(core, j).start()
    for h in range(2):
        for part in range(2):
            cols = normed[:, HALF * part + 2304 * h : HALF * part + 2304 * h + 2304].astype(F32)
            padded = jnp.concatenate([cols, jnp.zeros((8, 2304), F32)], axis=0)
            s_buf[h, :, 2304 * part : 2304 * part + 2304] = padded.astype(BF16)
    pl.semaphore_wait(barrier, 2 * (NZ - 1) + 1 + 2 * CHIPS - 1)
    s_copy = remote(s_buf.at[other], s_recv, s_sems.at[0], s_sems.at[1], sibling)
    s_copy.start()
    loads[4].wait()
    loads[5].wait()
    for h in range(2):
        wkv[h, 0:16, :] = wk_t[:, HALF * h : HALF * h + HALF]
        wkv[h, 16:32, :] = wv_t[:, HALF * h : HALF * h + HALF]
    wkv_copy = remote(wkv.at[other], wkv_sib, s_sems.at[2], s_sems.at[3], sibling)
    wkv_copy.start()

    right = (base + lax.rem(z + 1, NZ), mp)
    left = (base + lax.rem(z + NZ - 1, NZ), mp)

    def ring_pair(h, s, slot_r, slot_l):
        first = HEAD_DIM * h
        if s < 4:
            src_r = gt_buf.at[slot_r, first : first + 256, :]
            src_l = gt_buf.at[slot_l, first : first + 256, :]
        else:
            src_r = gt_buf.at[slot_r, first : first + 128, :]
            src_l = gt_buf.at[slot_l, first + 128 : first + 256, :]
        return (
            remote(src_r, src_r, cw_ss.at[h, s - 1], cw_rs.at[h, s - 1], right),
            remote(src_l, src_l, cc_ss.at[h, s - 1], cc_rs.at[h, s - 1], left),
        )

    def ring(h, s):
        return ring_pair(h, s, lax.rem(z - (s - 1) + NZ, NZ), lax.rem(z + (s - 1), NZ))

    def ring_start(h, s):
        for copy in ring(h, s):
            copy.start()

    def ring_wait(h, s):
        for copy in ring_pair(h, s, lax.rem(z - s + NZ, NZ), lax.rem(z + s, NZ)):
            copy.wait_recv()

    def kz_pair(s, slot_r, slot_l):
        src_r, src_l = kv_all.at[slot_r], kv_all.at[slot_l]
        copies = [remote(src_r, src_r, kz_ss.at[0, s - 1], kz_rs.at[0, s - 1], right)]
        if s < 4:
            copies.append(remote(src_l, src_l, kz_ss.at[1, s - 1], kz_rs.at[1, s - 1], left))
        return copies

    def kz(s):
        return kz_pair(s, lax.rem(z - (s - 1) + NZ, NZ), lax.rem(z + (s - 1), NZ))

    def kz_start(s):
        for copy in kz(s):
            copy.start()

    def kz_wait(s):
        for copy in kz_pair(s, lax.rem(z - s + NZ, NZ), lax.rem(z + s, NZ)):
            copy.wait_recv()

    def piece_n(o):
        return jnp.where(core == zhalf, (0, 2, 1, 3)[o], (2, 1, 3, 0)[o])

    def piece_z(o):
        return lax.rem(z + piece_n(o), 4)

    for i in range(4):
        loads[i].wait()
    key_v = key[...]
    value_v = value[...]
    key_t = jnp.transpose(key_v.astype(F32)).astype(BF16)
    scale = HEAD_DIM ** (-0.5)
    causal = lax.broadcasted_iota(jnp.int32, (TOK, TOK), 0) <= lax.broadcasted_iota(
        jnp.int32, (TOK, TOK), 1
    )
    kp = None
    vp = None
    for h in range(2):
        q_h = query[:, HEAD_DIM * h : HEAD_DIM * h + HEAD_DIM]
        g_h = grad[:, HEAD_DIM * h : HEAD_DIM * h + HEAD_DIM]
        scores = jnp.where(causal, dot_nt(key_v, q_h) * scale, -jnp.inf)
        expo = jnp.exp(scores - jnp.max(scores, axis=0, keepdims=True))
        probs = expo * (1.0 / jnp.sum(expo, axis=0, keepdims=True))
        low = probs.astype(BF16)
        dprob = dot_nt(value_v, g_h)
        delta = jnp.sum(low.astype(F32) * dprob, axis=0, keepdims=True)
        dscore = (probs * (dprob - delta)).astype(BF16)
        kp_h = dot(dscore, q_h)
        vp_h = dot(low, g_h)
        kp = kp_h if kp is None else kp + kp_h
        vp = vp_h if vp is None else vp + vp_h
        gq = dot(key_t, dscore) * scale
        gt_buf[z, HEAD_DIM * h : HEAD_DIM * h + HEAD_DIM, :] = gq.astype(BF16)
        g_buf[:, HEAD_DIM * h : HEAD_DIM * h + HEAD_DIM] = jnp.transpose(gq).astype(BF16)
        if h == 0:
            s_copy.wait_recv()
            mine = s_buf[core].astype(F32)[:24]
            theirs = s_recv[...].astype(F32)[:24]
            first = jnp.where(core == 0, mine, theirs)
            second = jnp.where(core == 0, theirs, mine)
            both = jnp.concatenate([first, second], axis=0)
            for j in range(4):
                block = jnp.concatenate(
                    [
                        both[:, BLOCK * j : BLOCK * j + BLOCK],
                        both[:, 2304 + BLOCK * j : 2304 + BLOCK * j + BLOCK],
                    ],
                    axis=1,
                )
                t_buf[j] = block.astype(BF16)
            chip_rows = pl.ds(pl.multiple_of(chip * CHIP_TOK, 16), CHIP_TOK)

            def a2a(j):
                peer = 4 * core + j
                return remote(
                    t_buf.at[j], n_buf.at[z, chip_rows, :], a2a_ss.at[j], a2a_rs.at[lax.rem(z, 4)],
                    (base + peer, chip * 2 + zhalf),
                )

            def a2a_in(j):
                peer = 4 * core + j
                return remote(
                    t_buf.at[j], n_buf.at[peer, chip_rows, :], a2a_ss.at[j], a2a_rs.at[j],
                    (base + peer, chip * 2 + zhalf),
                )

            def a2a_send(o):
                j = lax.rem(z + 4 - piece_n(o), 4)

                @pl.when(4 * core + j != z)
                def _():
                    a2a(j).start()

                @pl.when(4 * core + j == z)
                def _():
                    n_buf[z, chip_rows, :] = t_buf[j]

            a2a_send(0)
            a2a_send(1)

    kp_t = jnp.transpose(kp * scale)
    vp_t = jnp.transpose(vp)
    for c in range(2):
        kv_buf[c, :, 0:16, :] = kp_t.reshape(CHIPS, 2, 16, TOK)[:, c].astype(BF16)
        kv_buf[c, :, 16:32, :] = vp_t.reshape(CHIPS, 2, 16, TOK)[:, c].astype(BF16)
    kv_pair = remote(kv_buf.at[other], kv_sib, kv_ss.at[7], kv_rs.at[7], sibling)
    kv_pair.start()

    def kv_copy(i):
        there = lax.rem(chip + i, CHIPS)
        return remote(
            kv_buf.at[core, there], kv_recv.at[i - 1], kv_ss.at[i - 1], kv_rs.at[i - 1],
            (dp, there * 2 + core),
        )

    def n_rows(k):
        return pl.ds(pl.multiple_of(k * CHIP_TOK, 16), CHIP_TOK)

    def piece(o, k):
        return n_buf.at[4 * core + piece_z(o), n_rows(k), :]

    def x_chip(d):
        return lax.rem(x + d, 4) * 2 + y_lo

    def x_from(d):
        return lax.rem(x + 4 - d, 4) * 2 + y_lo

    def ag_y(n):
        return remote(
            piece(n, chip), piece(n, chip), agy_ss.at[n], agy_rs.at[n], (dp, y_chip * 2 + core)
        )

    def ag_x(n, d):
        k, to = (x_from(1), 1) if d == 2 else (chip, d)
        return remote(
            piece(n, k), piece(n, k), agx_ss.at[n, d - 1], agx_rs.at[n, d - 1],
            (dp, x_chip(to) * 2 + core),
        )

    def ag_d(n, d):
        if d == 2:
            k, there = x_from(3) + 1 - 2 * y_lo, x_chip(3)
        else:
            k, there = y_chip, x_chip(d)
        return remote(
            piece(n, k), piece(n, k), agd_ss.at[n, d - 1], agd_rs.at[n, d - 1],
            (dp, there * 2 + core),
        )

    def sib(n):
        block = n_buf.at[4 * core + piece_z(n)]
        return remote(block, block, sib_ss.at[n], sib_rs.at[n], sibling)

    def sib_in(n):
        o = jnp.where(core == zhalf, (3, 1, 0, 2)[n], (0, 2, 1, 3)[n])
        block = n_buf.at[4 * other + lax.rem(z + n, 4)]
        return remote(block, block, sib_ss.at[o], sib_rs.at[o], sibling)

    def ag_send(n):
        ag_y(n).start()
        ag_x(n, 1).start()
        ag_x(n, 3).start()

    def ag_first(n):
        j = piece_z(n)
        if n == 0:
            @pl.when(core != zhalf)
            def _():
                a2a_in(j).wait_recv()
                ag_send(0)
        else:
            @pl.when(4 * core + j != z)
            def _():
                a2a_in(j).wait_recv()

            ag_send(n)

    def ag_second(n):
        ag_x(n, 1).wait_recv()
        ag_x(n, 2).start()
        ag_y(n).wait_recv()
        ag_d(n, 1).start()
        ag_d(n, 3).start()

    def ag_third(n):
        ag_d(n, 3).wait_recv()
        ag_d(n, 2).start()

    def ag_last(n):
        ag_x(n, 3).wait_recv()
        ag_x(n, 2).wait_recv()
        ag_d(n, 1).wait_recv()
        ag_d(n, 2).wait_recv()
        sib(n).start()

    def partial(half, j):
        first = pl.multiple_of((half * NCH + j) * FC, FC)
        w_copy(half, j).wait()
        return dot_nt(g_buf[...], w_buf[pl.ds(first, FC), :])

    def p_copy(j):
        return remote(p_send.at[j], p_recv.at[j], p_ss.at[j], p_rs.at[j], sibling)

    def sib_half(j):
        p_send[j] = partial(other, j).astype(BF16)
        p_copy(j).start()

    def index(j):
        return j if j < 4 else j - 4

    def x_way(j):
        return 1 if index(j) % 2 == 0 else 3

    def x_block(j, d):
        there = lax.rem(x + d, 4)
        return r_buf.at[j, there] if j >= 4 else r_buf.at[j, there, y_lo]

    def x_copy(j, kind):
        way = x_way(j)
        d, to = ((2, way), (way, way), (4 - way, 4 - way))[kind]
        if j >= 4:
            n, ss, rs, mid, last = index(j), rx_ss, rx_rs, rx_mid, rx_recv
        else:
            n, ss, rs, mid, last = index(j), ryx_ss, ryx_rs, ry_mid, ry_last
        dst = mid.at[n] if kind == 0 else last.at[n, kind - 1]
        return remote(
            x_block(j, d), dst, ss.at[n, kind], rs.at[n, kind], (dp, x_chip(to) * 2 + core)
        )

    def x_first(j):
        x_copy(j, 0).start()
        x_copy(j, 2).start()

    def x_mid(j):
        x_copy(j, 0).wait_recv()
        there = lax.rem(x + x_way(j), 4)
        if j >= 4:
            for k in range(2):
                r_buf[j, there, k] = (
                    r_buf[j, there, k].astype(F32) + rx_mid[index(j), k].astype(F32)
                ).astype(BF16)
        else:
            r_buf[j, there, y_lo] = (
                r_buf[j, there, y_lo].astype(F32) + ry_mid[index(j)].astype(F32)
            ).astype(BF16)
        x_copy(j, 1).start()

    def rxy_copy(j):
        n = index(j)
        return remote(
            rx_send.at[n], rx_last.at[n], rxy_ss.at[n], rxy_rs.at[n], (dp, y_chip * 2 + core)
        )

    def ry_copy(j):
        return remote(
            r_buf.at[j, :, 1 - y_lo], ry_recv.at[index(j)], ry_ss.at[index(j)], ry_rs.at[index(j)],
            (dp, y_chip * 2 + core),
        )

    def own_half(j):
        cols = slice(FC * j, FC * j + FC)
        both = jnp.concatenate([wkv[core, :, cols], wkv_sib[:, cols]], axis=0)
        total = partial(core, j) + dot(kvg_buf[...], both)
        p_copy(j).wait_recv()
        total = (total + p_recv[j].astype(F32)).astype(BF16)
        r_buf[j] = total.reshape(4, 2, CHIP_TOK, FC)

    def own_send(j):
        if j < 4:
            ry_copy(j).start()
        else:
            x_first(j)

    def rs_second(j):
        if j < 4:
            ry_copy(j).wait_recv()
            for k in range(4):
                r_buf[j, k, y_lo] = (
                    r_buf[j, k, y_lo].astype(F32) + ry_recv[index(j), k].astype(F32)
                ).astype(BF16)
            x_first(j)
        else:
            x_mid(j)

    def rs_third(j):
        if j < 4:
            x_mid(j)
        else:
            n = index(j)
            x_copy(j, 1).wait_recv()
            x_copy(j, 2).wait_recv()
            out = r_buf[j, x, 1 - y_lo].astype(F32)
            for d in range(2):
                out = out + rx_recv[n, d, 1 - y_lo].astype(F32)
            rx_send[n] = out.astype(BF16)
            rxy_copy(j).start()

    def rs_last(j):
        total = r_buf[j, x, y_lo].astype(F32)
        if j < 4:
            x_copy(j, 1).wait_recv()
            x_copy(j, 2).wait_recv()
            for d in range(2):
                total = total + ry_last[index(j), d].astype(F32)
        else:
            n = index(j)
            for d in range(2):
                total = total + rx_recv[n, d, y_lo].astype(F32)
            rxy_copy(j).wait_recv()
            total = total + rx_last[n].astype(F32)
        low, high = total[0:24], total[24:48]
        pad = jnp.zeros((8, FC), F32)
        mine = jnp.where(core == 0, low, high)
        theirs = jnp.where(core == 0, high, low)
        f_buf[core, j] = jnp.concatenate([mine, pad], axis=0).astype(BF16)
        f_send[j] = jnp.concatenate([theirs, pad], axis=0).astype(BF16)
        f_copy(j).start()

    def f_copy(j):
        return remote(f_send.at[j], f_buf.at[core, j], f_ss.at[j], f_rs.at[j], sibling)

    def f_in(j):
        return remote(f_send.at[j], f_buf.at[other, j], f_ss.at[j], f_rs.at[j], sibling)

    def wgrad(za, zb, first, with_kv):
        lhs = [jnp.concatenate([gt_buf[za, first, :], gt_buf[zb, first, :]], axis=1)]
        if with_kv:
            lhs.append(jnp.concatenate([kv_all[za], kv_all[zb]], axis=1))
        lhs = jnp.concatenate(lhs, axis=0)
        rows = slice(first.start, first.start + lhs.shape[0])
        for cols in (slice(0, 512), slice(512, 1024), slice(1024, ZF)):
            rhs = jnp.concatenate([n_buf[za, :, cols], n_buf[zb, :, cols]], axis=0)
            acc[rows, cols] += dot(lhs, rhs)

    def wgrad_pair(n):
        wgrad(lax.rem(z + n, NZ), lax.rem(z + n + 4, NZ), slice(0, QC), True)

    def y_copy(r):
        cols = slice(256 * r, 256 * r + 256)
        return remote(y_send.at[:, cols], y_recv.at[:, cols], y_ss.at[r], y_rs.at[r], y_mate)

    def ykv_copy():
        return remote(ykv_send, ykv_recv, y_ss.at[2], y_rs.at[2], y_mate)

    def halves(rows):
        here = acc[rows, :]
        lower = here[:, 0:YW]
        upper = pltpu.roll(here, BLOCK, 1)[:, 0:YW]
        return jnp.where(y_hi == 0, lower, upper), jnp.where(y_hi == 0, upper, lower)

    acc[...] = jnp.zeros_like(acc)
    @pl.when(core == zhalf)
    def _():
        ag_send(0)

    sib_half(0)
    sib_half(1)
    kv_pair.wait_recv()
    kv_buf[core] = (kv_buf[core].astype(F32) + kv_sib[...].astype(F32)).astype(BF16)
    for i in range(1, CHIPS):
        kv_copy(i).start()
    a2a_send(2)
    sib_half(2)
    sib_half(3)
    a2a_send(3)
    sib_half(4)
    sib_half(5)
    for i in range(1, CHIPS):
        kv_copy(i).wait_recv()
    kv_sum = kv_buf[core, chip].astype(F32)
    for i in range(CHIPS - 1):
        kv_sum = kv_sum + kv_recv[i].astype(F32)
    kv_all[z] = kv_sum.astype(BF16)
    kvs_copy = remote(kv_all.at[z], kvs_recv, s_sems.at[4], s_sems.at[5], sibling)
    kvs_copy.start()
    kz_start(1)
    ag_first(0)
    ring_start(0, 1)
    wkv_copy.wait_recv()
    kvs_copy.wait_recv()
    kvg_buf[...] = jnp.transpose(
        jnp.concatenate([kv_sum, kvs_recv[...].astype(F32)], axis=0)
    ).astype(BF16)
    own_half(0)
    ag_first(1)
    own_half(1)
    ag_first(2)
    ring_start(1, 1)
    own_half(2)
    ag_first(3)
    ag_second(0)
    own_half(3)
    own_send(0)
    ag_second(1)
    ring_wait(0, 1)
    ring_start(0, 2)
    own_half(4)
    own_half(5)
    ag_second(2)
    own_send(1)
    ag_third(0)
    ag_second(3)
    ring_wait(1, 1)
    ring_start(1, 2)
    kz_wait(1)
    kz_start(2)
    ag_third(1)
    own_send(2)
    ag_third(2)
    ring_wait(0, 2)
    ring_start(0, 3)
    ag_third(3)
    own_send(3)
    ag_last(0)
    ring_wait(1, 2)
    ring_start(1, 3)
    kz_wait(2)
    kz_start(3)
    ag_last(1)
    rs_second(0)
    ring_wait(0, 3)
    ring_start(0, 4)
    own_send(4)
    sib_in(2).wait_recv()
    wgrad_pair(2)
    rs_second(1)
    ag_last(2)
    ring_wait(1, 3)
    ring_start(1, 4)
    kz_wait(3)
    kz_start(4)
    sib_in(1).wait_recv()
    wgrad_pair(1)
    own_send(5)
    rs_second(2)
    ag_last(3)
    sib_in(3).wait_recv()
    wgrad_pair(3)
    rs_second(3)
    rs_second(4)
    sib_in(0).wait_recv()
    kz_wait(4)
    for r in range(2):
        rows = slice(256 * r, 256 * r + 256)
        ring_wait(r, 4)
        wgrad(z, lax.rem(z + 4, NZ), rows, r == 1)
        for q in range(2):
            quarter = slice(256 * r + 128 * q, 256 * r + 128 * q + 128)
            mine, theirs = halves(quarter)
            y_send[:, quarter] = jnp.transpose(theirs)[0:BLOCK].astype(BF16)
            own_buf[:, quarter] = jnp.transpose(mine)[0:BLOCK]
        y_copy(r).start()
    mine, theirs = halves(slice(QC, GC))
    own_kv[...] = mine
    ykv_send[...] = theirs.astype(BF16)
    ykv_copy().start()
    rs_third(0)
    rs_third(1)
    rs_third(2)
    rs_second(5)
    rs_third(3)
    rs_third(4)
    rs_third(5)
    rs_last(0)
    rs_last(1)
    rs_last(2)
    rs_last(3)
    s_copy.wait_send()
    for j in range(4):
        @pl.when(4 * core + j != z)
        def _(j=j):
            a2a(j).wait_send()
    kv_pair.wait_send()
    wkv_copy.wait_send()
    kvs_copy.wait_send()
    for i in range(1, CHIPS):
        kv_copy(i).wait_send()
    for n in range(4):
        ag_y(n).wait_send()
        for d in range(1, 4):
            ag_x(n, d).wait_send()
            ag_d(n, d).wait_send()
    for n in range(4):
        sib(n).wait_send()
    for s in range(1, 5):
        for copy in (*ring(0, s), *ring(1, s), *kz(s)):
            copy.wait_send()
    for j in range(NCH):
        p_copy(j).wait_send()
        if j < 4:
            ry_copy(j).wait_send()
        for kind in range(3):
            x_copy(j, kind).wait_send()
    rs_last(4)
    rs_last(5)
    outs = []
    for r in range(2):
        y_copy(r).wait_recv()
        cols = slice(256 * r, 256 * r + 256)
        out_wq[:, cols] = (own_buf[:, cols] + y_recv[:, cols].astype(F32)).astype(BF16)
        outs.append(
            pltpu.make_async_copy(out_wq.at[:, cols], wq_out_hbm.at[:, cols], out_sems.at[r])
        )
        outs[-1].start()
    ykv_copy().wait_recv()
    total = (own_kv[...] + ykv_recv[...].astype(F32))[:, 0:BLOCK].astype(BF16)
    out_wk[...] = total[0:16]
    out_wv[...] = total[16:32]
    outs.append(pltpu.make_async_copy(out_wk, wk_out_hbm, out_sems.at[2]))
    outs[-1].start()
    outs.append(pltpu.make_async_copy(out_wv, wv_out_hbm, out_sems.at[3]))
    outs[-1].start()
    for j in range(NCH):
        f_in(j).wait_recv()
    for h in range(2):
        for j in range(NCH):
            out_in[:, HALF * h + FC * j : HALF * h + FC * j + FC] = f_buf[h, j].astype(F32)[
                0:24
            ].astype(BF16)
    for j in range(NCH):
        f_copy(j).wait_send()
        if j >= 4:
            rxy_copy(j).wait_send()
    for r in range(2):
        y_copy(r).wait_send()
    ykv_copy().wait_send()
    for out in outs:
        out.wait()


def place(*refs):
    ins, outs, held, sems = refs[0:4], refs[4:8], (None, *refs[8:11]), refs[11]
    parts = [(1, slice(0, 288)), (1, slice(288, 576))]
    parts += [(2, slice(0, 16)), (3, slice(0, 16))]
    first = []
    for n, (i, rows) in enumerate(parts):
        first.append(pltpu.make_async_copy(ins[i].at[rows], held[i].at[rows], sems.at[n, 0]))
        first[-1].start()
    second = []
    outs[0][...] = ins[0][...]
    for n, (i, rows) in enumerate(parts):
        first[n].wait()
        second.append(pltpu.make_async_copy(held[i].at[rows], outs[i].at[rows], sems.at[n, 1]))
        second[-1].start()
    for copy in second:
        copy.wait()


def shards(normed, w_query, w_key, w_value, query, key, value, grad_context):
    dma = pltpu.SemaphoreType.DMA
    vmem = pl.BlockSpec(memory_space=pltpu.VMEM)
    anywhere = pl.BlockSpec(memory_space=pl.ANY)
    results = (
        jax.ShapeDtypeStruct((24, FEAT), BF16),
        jax.ShapeDtypeStruct((BLOCK, QC), BF16),
        jax.ShapeDtypeStruct((16, BLOCK), BF16),
        jax.ShapeDtypeStruct((16, BLOCK), BF16),
    )
    grads = pl.pallas_call(
        kernel,
        out_shape=results,
        in_specs=[vmem] + [anywhere] * 7,
        out_specs=(vmem,) + (anywhere,) * 3,
        scratch_shapes=[
            pltpu.VMEM((BLOCK, QC), BF16),
            pltpu.VMEM((16, BLOCK), BF16),
            pltpu.VMEM((16, BLOCK), BF16),
            pltpu.VMEM((16, FEAT), BF16),
            pltpu.VMEM((16, FEAT), BF16),
            pltpu.VMEM((TOK, QC), BF16),
            pltpu.VMEM((TOK, HEAD_DIM), BF16),
            pltpu.VMEM((TOK, HEAD_DIM), BF16),
            pltpu.VMEM((TOK, QC), BF16),
            pltpu.VMEM((FEAT, QC), BF16),
            pltpu.VMEM((2, 32, HALF), BF16),
            pltpu.VMEM((32, HALF), BF16),
            pltpu.VMEM((2, 32, HALF), BF16),
            pltpu.VMEM((32, HALF), BF16),
            pltpu.VMEM((4, CHIP_TOK, ZF), BF16),
            pltpu.VMEM((NZ, TOK, ZF), BF16),
            pltpu.VMEM((NZ, QC, TOK), BF16),
            pltpu.VMEM((TOK, QC), BF16),
            pltpu.VMEM((2, CHIPS, 32, TOK), BF16),
            pltpu.VMEM((CHIPS, 32, TOK), BF16),
            pltpu.VMEM((CHIPS - 1, 32, TOK), BF16),
            pltpu.VMEM((NZ, 32, TOK), BF16),
            pltpu.VMEM((32, TOK), BF16),
            pltpu.VMEM((TOK, 64), BF16),
            pltpu.VMEM((NCH, TOK, FC), BF16),
            pltpu.VMEM((NCH, TOK, FC), BF16),
            pltpu.VMEM((NCH, 4, 2, CHIP_TOK, FC), BF16),
            pltpu.VMEM((2, 2, CHIP_TOK, FC), BF16),
            pltpu.VMEM((2, 2, 2, CHIP_TOK, FC), BF16),
            pltpu.VMEM((2, CHIP_TOK, FC), BF16),
            pltpu.VMEM((2, CHIP_TOK, FC), BF16),
            pltpu.VMEM((4, 4, CHIP_TOK, FC), BF16),
            pltpu.VMEM((4, CHIP_TOK, FC), BF16),
            pltpu.VMEM((4, 2, CHIP_TOK, FC), BF16),
            pltpu.VMEM((NCH, 32, FC), BF16),
            pltpu.VMEM((2, NCH, 32, FC), BF16),
            pltpu.VMEM((GC, ZF), F32),
            pltpu.VMEM((BLOCK, QC), F32),
            pltpu.VMEM((32, YW), F32),
            pltpu.VMEM((BLOCK, QC), BF16),
            pltpu.VMEM((BLOCK, QC), BF16),
            pltpu.VMEM((32, YW), BF16),
            pltpu.VMEM((32, YW), BF16),
            dma((4,)),
            dma((6,)),
            dma((2 * NCH,)),
            dma((6,)),
            dma((4,)), dma((4,)),
            dma((4,)), dma((4,)),
            dma((4, 3)), dma((4, 3)),
            dma((4, 3)), dma((4, 3)),
            dma((4,)), dma((4,)),
            dma((8,)), dma((8,)),
            dma((2, 4)), dma((2, 4)),
            dma((2, 4)), dma((2, 4)), dma((2, 4)), dma((2, 4)),
            dma((NCH,)), dma((NCH,)),
            dma((2, 3)), dma((2, 3)), dma((2,)), dma((2,)),
            dma((4,)), dma((4,)), dma((4, 3)), dma((4, 3)),
            dma((NCH,)), dma((NCH,)),
            dma((3,)), dma((3,)),
        ],
        compiler_params=pltpu.CompilerParams(
            collective_id=0, has_side_effects=True, vmem_limit_bytes=60 * 1024 * 1024
        ),
    )(
        normed, w_query, jnp.transpose(w_key), jnp.transpose(w_value),
        query, key, value, grad_context,
    )
    grad_input, grad_wq, grad_wk, grad_wv = pl.pallas_call(
        place,
        out_shape=results,
        in_specs=[vmem] + [anywhere] * 3,
        out_specs=(vmem,) + (anywhere,) * 3,
        scratch_shapes=[pltpu.VMEM(result.shape, BF16) for result in results[1:]] + [dma((4, 2))],
        compiler_params=pltpu.CompilerParams(vmem_limit_bytes=60 * 1024 * 1024),
    )(*grads)
    return grad_input, grad_wq, jnp.transpose(grad_wk), jnp.transpose(grad_wv)


def solution(mesh):
    placed = (
        P(("dp", "mp"), None),
        P(None, "mp"),
        P(None, "mp"),
        P(None, "mp"),
        P("dp", "mp"),
        P("dp", None),
        P("dp", None),
        P("dp", "mp"),
    )
    return jax.shard_map(
        shards,
        mesh=mesh,
        in_specs=placed,
        out_specs=(P(("dp", "mp"), None), P("dp", "mp"), P("dp", "mp"), P("dp", "mp")),
        check_vma=False,
    )
```
